512 devices in a mesh: dp: 16 (over y, core), tensor: 32 (over x, z).
Axes of the slice: x: 4, y: 8, z: 8, core: 2. Of those that a mesh axis runs over, the one named last changes fastest.
Arguments:
- residual: bfloat16 [4096, 4608], P('tensor', 'dp'), may hold values from -6 to 6
- picked: int32 [512], P('tensor'), may hold values from 0 to 4095, as said below
- enc_weight: bfloat16 [4608, 32768], P('dp', 'tensor'), may hold values from -0.09375 to 0.09375
- enc_bias: float32 [32768], P('tensor'), may hold values from -3 to 3
- dec_weight: bfloat16 [32768, 4608], P('tensor', 'dp'), may hold values from -0.0234375 to 0.0234375
- dec_bias: float32 [4608], P('dp'), may hold values from -3 to 3
Outputs:
- enc_grad: float32 [4608, 32768], P('dp', 'tensor')
- bias_grad: float32 [32768], P('tensor')
- dec_grad: float32 [32768, 4608], P('tensor', 'dp')
The draws below stay inside these ranges and needn't reach their ends.
Inputs may be any that keep to these rules, and one draw needn't show every extreme that they name: The entries of the aligned block k of 16 rows of picked are distinct tokens of k * 128 to (k + 1) * 128 - 1.
All inputs are finite; a program needn't handle non-finite values.
Results may differ from the reference program's by a relative error of at most 0.0039.
Values may be sent and summed in bfloat16 or wider, within the bound.
No kernel may reach another device: no remote copies, remote signals or barrier semaphores. Data moves between devices by JAX's collectives and lax.ppermute only.
A program may use at most 64 MiB of HBM per device.

```python
import jax
import jax.numpy as jnp
from jax import lax

D = 4608
LATENTS = 32768
ROWS = 512
TOK_DEV = 128
TOKENS = 4096
N_TENSOR = 32


def draw_picked(key, part):
    key = jax.random.fold_in(key, 7)
    per_device = ROWS // N_TENSOR
    block_keys = jax.random.split(key, N_TENSOR)

    def one_block(block_key):
        return jax.random.permutation(block_key, TOK_DEV)[:per_device].astype(jnp.int32)
    orders = jax.vmap(one_block)(block_keys)
    offsets = jnp.arange(N_TENSOR, dtype=jnp.int32)[:, None] * TOK_DEV
    return (orders + offsets).reshape(ROWS).astype(jnp.int32)


def block_scale(own_key, extent, shards, low, high):
    level = 1.0
    for dim, blocks in shards:
        steps = jax.random.uniform(jax.random.fold_in(jax.random.fold_in(own_key, 6), dim), (blocks,), jnp.float32, low / len(shards), high / len(shards))
        level = level * jnp.repeat(jnp.exp(steps), extent[dim] // blocks).reshape((-1,) + (1,) * (len(extent) - 1 - dim))
    return level


def gaussian(rng, shape, scale, bound, shards=(), kind=jnp.bfloat16):
    entries = scale * jax.random.normal(rng, shape, jnp.float32)
    if shards:
        entries = entries * block_scale(rng, shape, shards, -0.22, 0.18)
    return jnp.clip(entries, -bound, bound).astype(kind)


def setup_inputs(seed: int = 0) -> dict:
    seeds = jax.random.split(jax.random.key(seed), 7)
    return {
        "residual": gaussian(seeds[0], (TOKENS, D), 1.0, 6.0, ((0, 32), (1, 16))),
        "picked": draw_picked(jax.random.fold_in(seeds[6], 71), 0),
        "enc_weight": gaussian(seeds[2], (D, LATENTS), D ** -0.5, 0.09375, ((0, 16), (1, 32))),
        "enc_bias": gaussian(seeds[3], (LATENTS,), 0.5, 3.0, ((0, 32),), jnp.float32),
        "dec_weight": gaussian(seeds[4], (LATENTS, D), (16 * D) ** -0.5, 0.0234375, ((0, 32), (1, 16))),
        "dec_bias": gaussian(seeds[5], (D,), 0.5, 3.0, ((0, 16),), jnp.float32),
    }


def reference(residual, picked, enc_weight, enc_bias, dec_weight, dec_bias):
    sharpness = 8.0
    sparsity_weight = 1.0
    sampled = jnp.take(residual, picked, axis=0)
    centered = (sampled.astype(jnp.float32) - dec_bias).astype(jnp.bfloat16)
    pre_acts = jnp.dot(centered, enc_weight, preferred_element_type=jnp.float32) + enc_bias
    active = (jax.nn.softplus(sharpness * pre_acts) / sharpness).astype(jnp.bfloat16)
    dec_float = dec_weight.astype(jnp.float32)
    row_norms = jnp.sqrt(lax.optimization_barrier(jnp.sum(dec_float * dec_float, axis=1)) + 1e-06)
    unit_rows = (dec_float / row_norms[:, None]).astype(jnp.bfloat16)
    rebuilt = jnp.dot(active, unit_rows, preferred_element_type=jnp.float32) + dec_bias
    err_grad = (2.0 / ROWS * (rebuilt - sampled.astype(jnp.float32))).astype(jnp.bfloat16)
    latent_grad = jnp.dot(err_grad, unit_rows.T, preferred_element_type=jnp.float32) + sparsity_weight / ROWS
    pre_grad = (latent_grad * jax.nn.sigmoid(sharpness * pre_acts)).astype(jnp.bfloat16)
    enc_grad = jnp.dot(centered.T, pre_grad, preferred_element_type=jnp.float32)
    bias_grad = lax.optimization_barrier(jnp.sum(pre_grad.astype(jnp.float32), axis=0))
    unit_grad = jnp.dot(active.T, err_grad, preferred_element_type=jnp.float32)
    dot_sums = lax.optimization_barrier(jnp.sum(unit_grad * unit_rows.astype(jnp.float32), axis=1))
    dec_grad = (unit_grad - unit_rows.astype(jnp.float32) * dot_sums[:, None]) / row_norms[:, None]
    return (enc_grad, bias_grad, dec_grad)
```

```python
import jax
import jax.numpy as jnp
from jax import lax
from jax.sharding import Mesh
from jax.sharding import PartitionSpec as P

ROWS = 512
TENSOR = ("x", "z")
F32 = jnp.float32
BF16 = jnp.bfloat16


def exchange(blocks, axis):
    return lax.all_to_all(blocks, axis, 0, 0, tiled=False)


def gather(block, axis):
    count = lax.axis_size(axis)
    return exchange(jnp.broadcast_to(block[None], (count,) + block.shape), axis)


def swap(block):
    return lax.ppermute(block, "core", [(0, 1), (1, 0)])


def split(value):
    high = lax.reduce_precision(value, 8, 7)
    return jnp.stack([high, value - high]).astype(BF16)


def rows_of(value):
    return jnp.pad(split(value), ((0, 6), (0, 0)))


def merge(rows):
    return rows[..., 0, :].astype(F32) + rows[..., 1, :].astype(F32)


def body(residual, picked, enc_weight, enc_bias, dec_weight, dec_bias):
    sharpness = 8.0
    first = lax.axis_index("core") == 0
    half = enc_weight.shape[1] // 2
    count_y = lax.axis_size("y")
    share = ROWS // count_y

    def mine(value):
        return jnp.where(first, value[..., :half], value[..., half:])

    def other(value):
        return jnp.where(first, value[..., half:], value[..., :half])

    def join(own, its):
        low = jnp.where(first, own, its)
        high = jnp.where(first, its, own)
        return jnp.concatenate([low, high], axis=-1)

    first_token = lax.axis_index(TENSOR) * residual.shape[0]
    local_rows = jnp.take(residual, picked - first_token, axis=0)
    sampled = gather(local_rows, TENSOR).reshape(ROWS, -1)
    centered = (sampled.astype(F32) - dec_bias).astype(BF16)
    dec_float = dec_weight.astype(F32)
    squares = jnp.sum(dec_float * dec_float, axis=1)

    def reduce_rows(partial, extra):
        sent = other(partial).astype(BF16)
        if extra is not None:
            sent = jnp.concatenate([sent, rows_of(other(extra))])
        got = swap(sent)
        total = (mine(partial) + got[:ROWS].astype(F32)).astype(BF16)
        total = total.reshape(count_y, share, half)
        if extra is not None:
            extra = mine(extra) + merge(got[ROWS:])
            rows = jnp.broadcast_to(rows_of(extra)[None], (count_y, 8, half))
            total = jnp.concatenate([total, rows], axis=1)
        blocks = exchange(total, "y")
        result = jnp.sum(blocks[:, :share].astype(F32), axis=0)
        if extra is None:
            return result, None
        return result, jnp.sum(merge(blocks[:, share:]), axis=0)

    partial_pre = jnp.dot(centered, enc_weight, preferred_element_type=F32)
    pre_share, squares = reduce_rows(partial_pre, squares)
    pre_share = pre_share + mine(enc_bias)
    norms_half = jnp.sqrt(squares + 1e-06)
    active_share = (jax.nn.softplus(sharpness * pre_share) / sharpness).astype(BF16)
    active_half = gather(active_share, "y").reshape(ROWS, half)
    got = swap(jnp.concatenate([active_half, rows_of(norms_half)]))
    active = join(active_half, got[:ROWS])
    row_norms = join(norms_half, merge(got[ROWS:]))
    unit_rows = (dec_float / row_norms[:, None]).astype(BF16)
    partial_rebuilt = jnp.dot(active, unit_rows, preferred_element_type=F32)
    count_t = lax.axis_size(TENSOR)
    blocks = exchange(
        partial_rebuilt.astype(BF16).reshape(count_t, ROWS // count_t, -1), TENSOR
    )
    rebuilt_share = jnp.sum(blocks.astype(F32), axis=0) + dec_bias
    err_share = (2.0 / ROWS * (rebuilt_share - local_rows.astype(F32))).astype(BF16)
    err_grad = gather(err_share, TENSOR).reshape(ROWS, -1)
    partial_raw = lax.dot_general(
        err_grad, unit_rows, (((1,), (1,)), ((), ())), preferred_element_type=F32
    )
    raw_share, _ = reduce_rows(partial_raw, None)
    grad_share = ((raw_share + 1.0 / ROWS) * jax.nn.sigmoid(sharpness * pre_share)).astype(BF16)
    dots_share = jnp.sum(active_share.astype(F32) * raw_share, axis=0)
    blocks = gather(jnp.concatenate([grad_share, rows_of(dots_share)]), "y")
    grad_half = blocks[:, :share].reshape(ROWS, half)
    dots_half = jnp.sum(merge(blocks[:, share:]), axis=0)
    got = swap(jnp.concatenate([grad_half, rows_of(dots_half)]))
    pre_grad = join(grad_half, got[:ROWS])
    dot_sums = join(dots_half, merge(got[ROWS:]))
    enc_grad = lax.dot_general(
        centered, pre_grad, (((0,), (0,)), ((), ())), preferred_element_type=F32
    )
    bias_grad = jnp.sum(pre_grad.astype(F32), axis=0)
    unit_grad = lax.dot_general(
        active, err_grad, (((0,), (0,)), ((), ())), preferred_element_type=F32
    )
    dec_grad = (unit_grad - unit_rows.astype(F32) * dot_sums[:, None]) / row_norms[:, None]
    return (enc_grad, bias_grad, dec_grad)


def solution(mesh):
    grid = Mesh(mesh.devices.reshape(8, 2, 4, 8), ("y", "core", "x", "z"))
    dp = ("y", "core")
    return jax.shard_map(
        body,
        mesh=grid,
        in_specs=(
            P(TENSOR, dp),
            P(TENSOR),
            P(dp, TENSOR),
            P(TENSOR),
            P(TENSOR, dp),
            P(dp),
        ),
        out_specs=(P(dp, TENSOR), P(TENSOR), P(TENSOR, dp)),
        check_vma=False,
    )
```

```python
import jax
import jax.numpy as jnp
from jax import lax
from jax.sharding import Mesh
from jax.sharding import PartitionSpec as P

ROWS = 512
TENSOR = ("x", "z")
F32 = jnp.float32
BF16 = jnp.bfloat16


def exchange(blocks, axis):
    return lax.all_to_all(blocks, axis, 0, 0, tiled=False)


def gather(block, axis):
    count = lax.axis_size(axis)
    return exchange(jnp.broadcast_to(block[None], (count,) + block.shape), axis)


def swap(block):
    return lax.ppermute(block, "core", [(0, 1), (1, 0)])


def rows_of(value):
    high = lax.reduce_precision(value, 8, 7)
    return jnp.pad(jnp.stack([high, value - high]).astype(BF16), ((0, 6), (0, 0)))


def merge(rows):
    return rows[..., 0, :].astype(F32) + rows[..., 1, :].astype(F32)


def dot(a, b, dims):
    return lax.dot_general(a, b, (dims, ((), ())), preferred_element_type=F32)


def body(residual, picked, enc_weight, enc_bias, dec_weight, dec_bias):
    sharpness = 8.0
    core = lax.axis_index("core")
    count_y = lax.axis_size("y")
    count_t = lax.axis_size(TENSOR)
    rows = ROWS // 2
    share = rows // count_y
    piece = rows // count_t
    latents = enc_weight.shape[1]
    width = enc_weight.shape[0]

    local_picked = picked - lax.axis_index(TENSOR) * residual.shape[0]
    both = jnp.take(residual, local_picked, axis=0).reshape(2, piece, width)
    own_rows = jnp.where(core == 0, both[0], both[1])
    other_rows = jnp.where(core == 0, both[1], both[0])
    local_rows = jnp.concatenate([own_rows, swap(other_rows)], axis=1)
    dec_t = dec_weight.T
    enc_all = jnp.concatenate([enc_weight, swap(enc_weight)], axis=0)
    dec_all = jnp.concatenate([dec_t, swap(dec_t)], axis=0)
    bias_all = jnp.concatenate([dec_bias, swap(dec_bias)], axis=0)
    dec_float = dec_all.astype(F32)
    squares = jnp.sum(dec_float * dec_float, axis=0)

    sampled = gather(local_rows, TENSOR).reshape(rows, 2 * width)
    centered = (sampled.astype(F32) - bias_all).astype(BF16)
    partial = dot(centered, enc_all, ((1,), (0,))).astype(BF16)
    extra = jnp.broadcast_to(rows_of(squares)[None], (count_y, 8, latents))
    blocks = jnp.concatenate([partial.reshape(count_y, share, latents), extra], axis=1)
    blocks = exchange(blocks, "y")
    pre_share = jnp.sum(blocks[:, :share].astype(F32), axis=0) + enc_bias
    row_norms = jnp.sqrt(jnp.sum(merge(blocks[:, share:]), axis=0) + 1e-06)
    active_share = (jax.nn.softplus(sharpness * pre_share) / sharpness).astype(BF16)
    active = gather(active_share, "y").reshape(rows, latents)
    unit_t = (dec_float / row_norms).astype(BF16)
    partial = dot(active, unit_t, ((1,), (1,))).astype(BF16)
    blocks = exchange(partial.reshape(count_t, piece, 2 * width), TENSOR)
    rebuilt_share = jnp.sum(blocks.astype(F32), axis=0) + bias_all
    err_share = (2.0 / ROWS * (rebuilt_share - local_rows.astype(F32))).astype(BF16)
    err_grad = gather(err_share, TENSOR).reshape(rows, 2 * width)
    partial = dot(err_grad, unit_t, ((1,), (0,))).astype(BF16)
    blocks = exchange(partial.reshape(count_y, share, latents), "y")
    raw_share = jnp.sum(blocks.astype(F32), axis=0)
    grad_share = ((raw_share + 1.0 / ROWS) * jax.nn.sigmoid(sharpness * pre_share)).astype(BF16)
    dots_share = jnp.sum(active_share.astype(F32) * raw_share, axis=0)
    own = gather(jnp.concatenate([grad_share, rows_of(dots_share)]), "y")
    its = swap(own)
    dot_sums = jnp.sum(merge(own[:, share:]), axis=0) + jnp.sum(merge(its[:, share:]), axis=0)
    own_grad = own[:, :share].reshape(rows, latents)
    its_grad = its[:, :share].reshape(rows, latents)
    its_centered = swap(centered[:, width:])
    its_err = swap(err_grad[:, width:])
    its_active = swap(active)
    enc_grad = dot(centered[:, :width], own_grad, ((0,), (0,))) + dot(
        its_centered, its_grad, ((0,), (0,))
    )
    bias_grad = jnp.sum(own_grad.astype(F32), axis=0) + jnp.sum(its_grad.astype(F32), axis=0)
    unit_grad = dot(err_grad[:, :width], active, ((0,), (0,))) + dot(
        its_err, its_active, ((0,), (0,))
    )
    dec_grad = (unit_grad - unit_t[:width].astype(F32) * dot_sums) / row_norms
    return (enc_grad, bias_grad, dec_grad.T)


def solution(mesh):
    grid = Mesh(mesh.devices.reshape(8, 2, 4, 8), ("y", "core", "x", "z"))
    dp = ("y", "core")
    return jax.shard_map(
        body,
        mesh=grid,
        in_specs=(
            P(TENSOR, dp),
            P(TENSOR),
            P(dp, TENSOR),
            P(TENSOR),
            P(TENSOR, dp),
            P(dp),
        ),
        out_specs=(P(dp, TENSOR), P(TENSOR), P(TENSOR, dp)),
        check_vma=False,
    )
```

```python
import jax
import jax.numpy as jnp
from jax import lax
from jax.experimental import pallas as pl
from jax.experimental.pallas import tpu as pltpu
from jax.sharding import Mesh
from jax.sharding import PartitionSpec as P

ROWS = 512
LANES = 128
TENSOR = ("x", "z")
F32 = jnp.float32
BF16 = jnp.bfloat16
SHARPNESS = 8.0
VMEM = pl.BlockSpec(memory_space=pltpu.VMEM)
SMEM = pl.BlockSpec(memory_space=pltpu.SMEM)
ANY = pl.BlockSpec(memory_space=pl.ANY)


def exchange(blocks, axis):
    return lax.all_to_all(blocks, axis, 0, 0, tiled=False)


def swap(block):
    return lax.ppermute(block, "core", [(0, 1), (1, 0)])


def dot(a, b, dims):
    return lax.dot_general(a, b, (dims, ((), ())), preferred_element_type=F32)


def call(kernel, outs, specs, cost, scratch=(), out_specs=None):
    flops, moved = cost
    return pl.pallas_call(
        kernel,
        out_shape=outs,
        in_specs=specs,
        out_specs=jax.tree.map(lambda _: VMEM, outs) if out_specs is None else out_specs,
        scratch_shapes=list(scratch),
        compiler_params=pltpu.CompilerParams(vmem_limit_bytes=24 * 1024 * 1024),
        cost_estimate=pl.CostEstimate(flops=flops, bytes_accessed=moved, transcendentals=0),
    )


def shape(dims, kind):
    return jax.ShapeDtypeStruct(dims, kind)


def store_parts(value, store):
    high = value.astype(BF16)
    store(0, high)
    store(1, (value - high.astype(F32)).astype(BF16))


def pick_kernel(picked_ref, residual_ref, own_ref, other_ref):
    width, tokens = residual_ref.shape
    piece = own_ref.shape[0]
    core = lax.axis_index("core")
    place = lax.axis_index("x") * lax.axis_size("z") + lax.axis_index("z")
    row = lax.broadcasted_iota(jnp.int32, (piece, tokens), 0)
    token = lax.broadcasted_iota(jnp.int32, (piece, tokens), 1) + place * tokens
    table = residual_ref[...]
    zeros = jnp.zeros_like(table)

    def pick(start, columns):
        wanted = jnp.zeros((piece, tokens), jnp.int32)
        for i in range(piece):
            wanted = jnp.where(row == i, picked_ref[start + i], wanted)
        hot = jnp.where(wanted == token, 1.0, 0.0).astype(BF16)
        return dot(hot, columns, ((1,), (1,))).astype(BF16)

    own_ref[...] = pick(core * piece, jnp.concatenate([table, zeros], axis=0))
    other_ref[...] = pick((1 - core) * piece, jnp.concatenate([zeros, table], axis=0))


def join_kernel(own_ref, got_ref, rows_ref, copies_ref):
    rows = own_ref[...] + got_ref[...]
    rows_ref[...] = rows
    for i in range(copies_ref.shape[0]):
        copies_ref[i] = rows


def pack_kernel(enc_own, enc_other, dec_own, dec_other, enc_ref, dec_ref, squares_ref):
    width, latents = enc_own.shape
    enc_ref[:width] = enc_own[...]
    enc_ref[width:] = enc_other[...]
    dec_ref[:width] = dec_own[...]
    dec_ref[width:] = dec_other[...]
    count = latents // LANES
    row = lax.broadcasted_iota(jnp.int32, (count, LANES), 0)
    total = jnp.zeros((count, LANES), F32)
    for k in range(count):
        lanes = pl.ds(k * LANES, LANES)
        a = dec_own[:, lanes].astype(F32)
        b = dec_other[:, lanes].astype(F32)
        part = jnp.sum(a * a + b * b, axis=0, keepdims=True)
        total = jnp.where(row == k, part, total)
    high = total.astype(BF16).astype(F32)
    squares_ref[...] = jnp.concatenate([high, total - high], axis=0).astype(BF16)


def spread(value, out_ref, first):
    share = value.shape[0] // out_ref.shape[0]
    for y in range(out_ref.shape[0]):
        for k in range(value.shape[1] // LANES):
            out_ref[y, pl.ds((first + k) * share, share), :] = value[
                y * share : (y + 1) * share, k * LANES : (k + 1) * LANES
            ]


def pre_kernel(rows_ref, bias_ref, enc_ref, squares_ref, out_ref, centered_ref):
    count = rows_ref.shape[0] * rows_ref.shape[1]
    rows = rows_ref[...].astype(F32).reshape(count, rows_ref.shape[2])
    centered_ref[...] = (rows - bias_ref[...]).astype(BF16)
    step = 2 * LANES
    for n in range(enc_ref.shape[1] // step):
        part = dot(centered_ref[...], enc_ref[:, n * step : (n + 1) * step], ((1,), (0,)))
        spread(part.astype(BF16), out_ref, 2 * n)
    extra = squares_ref.shape[0]
    for y in range(out_ref.shape[0]):
        out_ref[y, pl.ds(out_ref.shape[1] - extra, extra), :] = squares_ref[...]


def sum_blocks(blocks_ref, size):
    total = blocks_ref[0, :size, :].astype(F32)
    for y in range(1, blocks_ref.shape[0]):
        total = total + blocks_ref[y, :size, :].astype(F32)
    return total


def sum_parts(blocks_ref, size):
    total = blocks_ref[0, size:, :].astype(F32)
    for y in range(1, blocks_ref.shape[0]):
        total = total + blocks_ref[y, size:, :].astype(F32)
    half = total.shape[0] // 2
    return total[:half] + total[half:]


def act_kernel(blocks_ref, bias_ref, copies_ref, active_ref, gate_ref, norms_ref):
    size = copies_ref.shape[1]
    count = bias_ref.shape[0]
    share = size // count
    total = sum_blocks(blocks_ref, size)
    for k in range(count):
        lines = slice(k * share, (k + 1) * share)
        value = SHARPNESS * (total[lines] + bias_ref[k : k + 1, :])
        small = jnp.exp(-jnp.abs(value))
        soft = jnp.maximum(value, 0.0) + jnp.log1p(small)
        active = (soft / SHARPNESS).astype(BF16)
        active_ref[lines, :] = active
        gate_ref[lines, :] = jnp.where(value >= 0.0, 1.0, small) / (1.0 + small)
        for y in range(copies_ref.shape[0]):
            copies_ref[y, lines, :] = active
    norms_ref[...] = jnp.sqrt(sum_parts(blocks_ref, size) + 1e-06)


def unit_kernel(dec_ref, norms_ref, unit_ref):
    for k in range(norms_ref.shape[0]):
        lanes = pl.ds(k * LANES, LANES)
        unit_ref[:, lanes] = (dec_ref[:, lanes].astype(F32) / norms_ref[k : k + 1, :]).astype(BF16)


def rebuild_kernel(copies_ref, unit_ref, out_ref, active_ref):
    latents = unit_ref.shape[1]
    count = latents // LANES
    share = copies_ref.shape[1] // count
    for y in range(copies_ref.shape[0]):
        for k in range(count):
            active_ref[y * share : (y + 1) * share, k * LANES : (k + 1) * LANES] = copies_ref[
                y, k * share : (k + 1) * share, :
            ]
    part = dot(active_ref[...], unit_ref[...], ((1,), (1,)))
    out_ref[...] = part.astype(BF16).reshape(out_ref.shape)


def error_kernel(blocks_ref, bias_ref, rows_ref, copies_ref):
    total = blocks_ref[0].astype(F32)
    for i in range(1, blocks_ref.shape[0]):
        total = total + blocks_ref[i].astype(F32)
    rebuilt = total + bias_ref[...]
    error = (2.0 / ROWS * (rebuilt - rows_ref[...].astype(F32))).astype(BF16)
    for i in range(copies_ref.shape[0]):
        copies_ref[i] = error


def raw_kernel(error_ref, unit_ref, out_ref):
    count = error_ref.shape[0] * error_ref.shape[1]
    error = error_ref[...].reshape(count, error_ref.shape[2])
    step = 2 * LANES
    for n in range(unit_ref.shape[1] // step):
        part = dot(error, unit_ref[:, n * step : (n + 1) * step], ((1,), (0,)))
        spread(part.astype(BF16), out_ref, 2 * n)


def grad_kernel(blocks_ref, active_ref, gate_ref, copies_ref):
    size = blocks_ref.shape[1]
    extra = copies_ref.shape[1] - size
    count = extra // 2
    share = size // count
    raw = sum_blocks(blocks_ref, size)
    grad = ((raw + 1.0 / ROWS) * gate_ref[...]).astype(BF16)
    product = active_ref[...].astype(F32) * raw
    row = lax.broadcasted_iota(jnp.int32, (count, LANES), 0)
    dots = jnp.zeros((count, LANES), F32)
    for k in range(count):
        part = jnp.sum(product[k * share : (k + 1) * share], axis=0, keepdims=True)
        dots = jnp.where(row == k, part, dots)
    high = dots.astype(BF16).astype(F32)
    parts = jnp.concatenate([high, dots - high], axis=0).astype(BF16)
    for y in range(copies_ref.shape[0]):
        copies_ref[y, :size, :] = grad
        copies_ref[y, size:, :] = parts


def last_kernel(
    own_ref, its_ref, centered_own, centered_its, product_ref, unit_ref, norms_ref,
    enc_out, bias_ref, dec_out,
    own_grad, its_grad, enc_ref, dec_ref, sems,
):
    count = norms_ref.shape[0]
    size = own_ref.shape[1] - 2 * count
    share = size // count
    dots = sum_parts(own_ref, size) + sum_parts(its_ref, size)
    step = 2 * LANES
    copies = []
    for n in range(count // 2):
        lanes = pl.ds(n * step, step)
        for k in (2 * n, 2 * n + 1):
            cut = pl.ds(k * LANES, LANES)
            lines = pl.ds(k * share, share)
            ratio = 1.0 / norms_ref[k : k + 1, :]
            dec_ref[:, cut] = (
                product_ref[:, cut] - unit_ref[:, cut].astype(F32) * dots[k : k + 1]
            ) * ratio
            total = jnp.zeros((share, LANES), F32)
            for y in range(own_ref.shape[0]):
                a, b = own_ref[y, lines, :], its_ref[y, lines, :]
                own_grad[pl.ds(y * share, share), cut] = a
                its_grad[pl.ds(y * share, share), cut] = b
                total = total + a.astype(F32) + b.astype(F32)
            bias_ref[k : k + 1, :] = jnp.sum(total, axis=0, keepdims=True)
        copies.append(pltpu.make_async_copy(dec_ref.at[:, lanes], dec_out.at[:, lanes], sems.at[2 * n]))
        copies[-1].start()
        enc_ref[:, lanes] = dot(centered_own[...], own_grad[:, lanes], ((1,), (0,))) + dot(
            centered_its[...], its_grad[:, lanes], ((1,), (0,))
        )
        copies.append(
            pltpu.make_async_copy(enc_ref.at[:, lanes], enc_out.at[:, lanes], sems.at[2 * n + 1])
        )
        copies[-1].start()
    for copy in copies:
        copy.wait()


def body(residual, picked, enc_weight, enc_bias, dec_weight, dec_bias):
    count_y = lax.axis_size("y")
    count_t = lax.axis_size(TENSOR)
    rows = ROWS // 2
    share = rows // count_y
    piece = rows // count_t
    width, latents = enc_weight.shape
    blocks_n = latents // LANES
    size = share * blocks_n
    extra = 2 * blocks_n
    wide = 2 * width
    matmul = 2 * rows * wide * latents
    moved = 3 << 20

    small = shape((piece, wide), BF16)
    own_rows, other_rows = call(pick_kernel, (small, small), [SMEM, VMEM], (1 << 20, 1 << 17))(
        picked, residual.T
    )
    tensor_blocks = shape((count_t, piece, wide), BF16)
    local_rows, copies = call(join_kernel, (small, tensor_blocks), [VMEM] * 2, (1 << 12, 1 << 19))(
        own_rows, swap(other_rows)
    )
    sampled = exchange(copies, TENSOR)
    dec_t = dec_weight.T
    weights = shape((wide, latents), BF16)
    enc_all, dec_all, squares = call(
        pack_kernel, (weights, weights, shape((extra, LANES), BF16)), [VMEM] * 4, (1 << 21, moved)
    )(enc_weight, swap(enc_weight), dec_t, swap(dec_t))
    bias_all = jnp.concatenate([dec_bias, swap(dec_bias)], axis=0)[None]

    pre_blocks, centered = call(
        pre_kernel,
        (shape((count_y, size + extra, LANES), BF16), shape((rows, wide), BF16)),
        [VMEM] * 4,
        (matmul, moved),
    )(sampled, bias_all, enc_all, squares)
    copies, active_share, gate, norms = call(
        act_kernel,
        (
            shape((count_y, size, LANES), BF16),
            shape((size, LANES), BF16),
            shape((size, LANES), F32),
            shape((blocks_n, LANES), F32),
        ),
        [VMEM] * 2,
        (1 << 20, 1 << 20),
    )(exchange(pre_blocks, "y"), enc_bias.reshape(blocks_n, LANES))
    copies = exchange(copies, "y")
    unit = call(unit_kernel, weights, [VMEM] * 2, (1 << 20, moved))(dec_all, norms)
    partial, active = call(
        rebuild_kernel,
        (tensor_blocks, shape((rows, latents), BF16)),
        [VMEM] * 2,
        (matmul, moved),
    )(copies, unit)
    copies = call(error_kernel, tensor_blocks, [VMEM] * 3, (1 << 20, 1 << 20))(
        exchange(partial, TENSOR), bias_all, local_rows
    )
    its_active = swap(active)
    its_centered = swap(centered[:, width:])
    error = exchange(copies, TENSOR)
    raw_blocks = call(
        raw_kernel, shape((count_y, size, LANES), BF16), [VMEM] * 2, (matmul, moved)
    )(error, unit)
    err_grad = error.reshape(rows, wide)
    its_err = swap(err_grad[:, width:])
    product = dot(err_grad[:, :width], active, ((0,), (0,))) + dot(
        its_err, its_active, ((0,), (0,))
    )
    own = exchange(
        call(
            grad_kernel,
            shape((count_y, size + extra, LANES), BF16),
            [VMEM] * 3,
            (1 << 20, 1 << 20),
        )(exchange(raw_blocks, "y"), active_share, gate),
        "y",
    )
    its = swap(own)
    out = shape((width, latents), F32)
    enc_grad, bias_grad, dec_grad = call(
        last_kernel,
        (out, shape((blocks_n, LANES), F32), out),
        [VMEM] * 7,
        (matmul, 2 * moved),
        [
            pltpu.VMEM((rows, latents), BF16),
            pltpu.VMEM((rows, latents), BF16),
            pltpu.VMEM((width, latents), F32),
            pltpu.VMEM((width, latents), F32),
            pltpu.SemaphoreType.DMA((blocks_n,)),
        ],
        (ANY, VMEM, ANY),
    )(own, its, centered[:, :width].T, its_centered.T, product, unit[:width], norms)
    return (enc_grad, bias_grad.reshape(latents), dec_grad.T)


def solution(mesh):
    grid = Mesh(mesh.devices.reshape(8, 2, 4, 8), ("y", "core", "x", "z"))
    dp = ("y", "core")
    return jax.shard_map(
        body,
        mesh=grid,
        in_specs=(
            P(TENSOR, dp),
            P(TENSOR),
            P(dp, TENSOR),
            P(TENSOR),
            P(TENSOR, dp),
            P(dp),
        ),
        out_specs=(P(dp, TENSOR), P(TENSOR), P(TENSOR, dp)),
        check_vma=False,
    )
```

```python
import jax
import jax.numpy as jnp
from jax import lax
from jax.experimental import pallas as pl
from jax.experimental.pallas import tpu as pltpu
from jax.sharding import Mesh
from jax.sharding import PartitionSpec as P

ROWS = 512
LANES = 128
TENSOR = ("x", "z")
F32 = jnp.float32
BF16 = jnp.bfloat16
SHARPNESS = 8.0
VMEM = pl.BlockSpec(memory_space=pltpu.VMEM)
ANY = pl.BlockSpec(memory_space=pl.ANY)
HBM = pl.BlockSpec(memory_space=pltpu.HBM)


def exchange(blocks, axis):
    return lax.all_to_all(blocks, axis, 0, 0, tiled=False)


def swap(block):
    return lax.ppermute(block, "core", [(0, 1), (1, 0)])


def dot(a, b, dims):
    return lax.dot_general(a, b, (dims, ((), ())), preferred_element_type=F32)


def call(kernel, outs, specs, cost, scratch=(), out_specs=None):
    flops, moved = cost
    return pl.pallas_call(
        kernel,
        out_shape=outs,
        in_specs=specs,
        out_specs=jax.tree.map(lambda _: VMEM, outs) if out_specs is None else out_specs,
        scratch_shapes=list(scratch),
        compiler_params=pltpu.CompilerParams(vmem_limit_bytes=24 * 1024 * 1024),
        cost_estimate=pl.CostEstimate(flops=flops, bytes_accessed=moved, transcendentals=0),
    )


def shape(dims, kind):
    return jax.ShapeDtypeStruct(dims, kind)


def pick_kernel(picked_hbm, residual_hbm, bias_hbm, own_ref, other_ref, bias, picked, table, sems):
    width, tokens = table.shape
    piece = own_ref.shape[0]
    pairs = ((residual_hbm, table), (picked_hbm, picked), (bias_hbm, bias))
    copies = [pltpu.make_async_copy(a, b, sems.at[i]) for i, (a, b) in enumerate(pairs)]
    for copy in copies:
        copy.start()
    for copy in copies:
        copy.wait()
    core = lax.axis_index("core")
    place = lax.axis_index("x") * lax.axis_size("z") + lax.axis_index("z")
    row = lax.broadcasted_iota(jnp.int32, (piece, tokens), 0)
    token = lax.broadcasted_iota(jnp.int32, (piece, tokens), 1) + place * tokens
    columns = table[...]
    zeros = jnp.zeros_like(columns)

    def pick(start, columns):
        wanted = jnp.zeros((piece, tokens), jnp.int32)
        for i in range(piece):
            wanted = jnp.where(row == i, picked[start + i], wanted)
        hot = jnp.where(wanted == token, 1.0, 0.0).astype(BF16)
        return dot(hot, columns, ((1,), (1,))).astype(BF16)

    own_ref[...] = pick(core * piece, jnp.concatenate([columns, zeros], axis=0))
    other_ref[:piece] = pick((1 - core) * piece, jnp.concatenate([zeros, columns], axis=0))
    high = bias[...].astype(BF16).astype(F32)
    middle = (bias[...] - high).astype(BF16).astype(F32)
    low = bias[...] - high - middle
    row = lax.broadcasted_iota(jnp.int32, (piece, width), 0)
    parts = jnp.where(row == 0, high, jnp.where(row == 1, middle, jnp.where(row == 2, low, 0.0)))
    line = lax.broadcasted_iota(jnp.int32, (width, 2 * width), 0)
    lane = lax.broadcasted_iota(jnp.int32, (width, 2 * width), 1)
    move = jnp.where(lane == line + width, 1.0, 0.0).astype(BF16)
    other_ref[piece:] = dot(parts.astype(BF16), move, ((1,), (0,))).astype(BF16)


def join_kernel(own_ref, got_ref, bias_ref, rows_ref, copies_ref, biases_ref):
    piece = own_ref.shape[0]
    width = bias_ref.shape[1]
    rows = own_ref[...] + got_ref[:piece]
    rows_ref[...] = rows
    for i in range(copies_ref.shape[0]):
        copies_ref[i] = rows
    parts = got_ref[piece:].astype(F32)
    biases_ref[...] = parts[0:1] + parts[1:2] + parts[2:3]
    biases_ref[:, :width] = bias_ref[...]


def stage_kernel(enc_hbm, dec_hbm, after_hbm, both_ref, sems):
    width = enc_hbm.shape[0]
    copies = [
        pltpu.make_async_copy(enc_hbm, both_ref.at[pl.ds(0, width)], sems.at[0]),
        pltpu.make_async_copy(dec_hbm, both_ref.at[pl.ds(width, width)], sems.at[1]),
    ]
    for copy in copies:
        copy.start()
    for copy in copies:
        copy.wait()


def pack_kernel(own_ref, other_ref, enc_ref, dec_ref, squares_ref):
    width = own_ref.shape[0] // 2
    latents = own_ref.shape[1]
    enc_ref[:width] = own_ref[:width]
    enc_ref[width:] = other_ref[:width]
    dec_ref[:width] = own_ref[width:]
    dec_ref[width:] = other_ref[width:]
    count = latents // LANES
    row = lax.broadcasted_iota(jnp.int32, (count, LANES), 0)
    total = jnp.zeros((count, LANES), F32)
    for k in range(count):
        lanes = pl.ds(k * LANES, LANES)
        a = own_ref[width:, lanes].astype(F32)
        b = other_ref[width:, lanes].astype(F32)
        part = jnp.sum(a * a + b * b, axis=0, keepdims=True)
        total = jnp.where(row == k, part, total)
    high = total.astype(BF16).astype(F32)
    squares_ref[...] = jnp.concatenate([high, total - high], axis=0).astype(BF16)


def turn_kernel(value_ref, own_ref, other_ref):
    turned = value_ref[...].astype(F32).T
    width = own_ref.shape[0]
    own_ref[...] = turned[:width].astype(BF16)
    other_ref[...] = turned[width:].astype(BF16)


def spread(value, out_ref, first):
    share = value.shape[0] // out_ref.shape[0]
    for y in range(out_ref.shape[0]):
        for k in range(value.shape[1] // LANES):
            out_ref[y, pl.ds((first + k) * share, share), :] = value[
                y * share : (y + 1) * share, k * LANES : (k + 1) * LANES
            ]


def pre_kernel(rows_ref, bias_ref, enc_ref, squares_ref, out_ref, centered_ref):
    count = rows_ref.shape[0] * rows_ref.shape[1]
    rows = rows_ref[...].astype(F32).reshape(count, rows_ref.shape[2])
    centered_ref[...] = (rows - bias_ref[...]).astype(BF16)
    step = 2 * LANES
    for n in range(enc_ref.shape[1] // step):
        part = dot(centered_ref[...], enc_ref[:, n * step : (n + 1) * step], ((1,), (0,)))
        spread(part.astype(BF16), out_ref, 2 * n)
    extra = squares_ref.shape[0]
    for y in range(out_ref.shape[0]):
        out_ref[y, pl.ds(out_ref.shape[1] - extra, extra), :] = squares_ref[...]


def sum_blocks(blocks_ref, size):
    total = blocks_ref[0, :size, :].astype(F32)
    for y in range(1, blocks_ref.shape[0]):
        total = total + blocks_ref[y, :size, :].astype(F32)
    return total


def sum_parts(blocks_ref, size):
    total = blocks_ref[0, size:, :].astype(F32)
    for y in range(1, blocks_ref.shape[0]):
        total = total + blocks_ref[y, size:, :].astype(F32)
    half = total.shape[0] // 2
    return total[:half] + total[half:]


def act_kernel(blocks_ref, bias_ref, copies_ref, active_ref, gate_ref, norms_ref):
    size = copies_ref.shape[1]
    count = bias_ref.shape[0]
    share = size // count
    total = sum_blocks(blocks_ref, size)
    for k in range(count):
        lines = slice(k * share, (k + 1) * share)
        value = SHARPNESS * (total[lines] + bias_ref[k : k + 1, :])
        small = jnp.exp(-jnp.abs(value))
        soft = jnp.maximum(value, 0.0) + jnp.log1p(small)
        active = (soft / SHARPNESS).astype(BF16)
        active_ref[lines, :] = active
        gate_ref[lines, :] = jnp.where(value >= 0.0, 1.0, small) / (1.0 + small)
        for y in range(copies_ref.shape[0]):
            copies_ref[y, lines, :] = active
    norms_ref[...] = jnp.sqrt(sum_parts(blocks_ref, size) + 1e-06)


def unit_kernel(dec_ref, norms_ref, unit_ref):
    for k in range(norms_ref.shape[0]):
        lanes = pl.ds(k * LANES, LANES)
        unit_ref[:, lanes] = (dec_ref[:, lanes].astype(F32) / norms_ref[k : k + 1, :]).astype(BF16)


def rebuild_kernel(copies_ref, unit_ref, out_ref, active_ref):
    latents = unit_ref.shape[1]
    count = latents // LANES
    share = copies_ref.shape[1] // count
    for y in range(copies_ref.shape[0]):
        for k in range(count):
            active_ref[y * share : (y + 1) * share, k * LANES : (k + 1) * LANES] = copies_ref[
                y, k * share : (k + 1) * share, :
            ]
    part = dot(active_ref[...], unit_ref[...], ((1,), (1,)))
    out_ref[...] = part.astype(BF16).reshape(out_ref.shape)


def error_kernel(blocks_ref, bias_ref, rows_ref, copies_ref):
    total = blocks_ref[0].astype(F32)
    for i in range(1, blocks_ref.shape[0]):
        total = total + blocks_ref[i].astype(F32)
    rebuilt = total + bias_ref[...]
    error = (2.0 / ROWS * (rebuilt - rows_ref[...].astype(F32))).astype(BF16)
    for i in range(copies_ref.shape[0]):
        copies_ref[i] = error


def raw_kernel(error_ref, unit_ref, out_ref):
    count = error_ref.shape[0] * error_ref.shape[1]
    error = error_ref[...].reshape(count, error_ref.shape[2])
    step = 2 * LANES
    for n in range(unit_ref.shape[1] // step):
        part = dot(error, unit_ref[:, n * step : (n + 1) * step], ((1,), (0,)))
        spread(part.astype(BF16), out_ref, 2 * n)


def grad_kernel(blocks_ref, active_ref, gate_ref, copies_ref):
    size = blocks_ref.shape[1]
    extra = copies_ref.shape[1] - size
    count = extra // 2
    share = size // count
    raw = sum_blocks(blocks_ref, size)
    grad = ((raw + 1.0 / ROWS) * gate_ref[...]).astype(BF16)
    product = active_ref[...].astype(F32) * raw
    row = lax.broadcasted_iota(jnp.int32, (count, LANES), 0)
    dots = jnp.zeros((count, LANES), F32)
    for k in range(count):
        part = jnp.sum(product[k * share : (k + 1) * share], axis=0, keepdims=True)
        dots = jnp.where(row == k, part, dots)
    high = dots.astype(BF16).astype(F32)
    parts = jnp.concatenate([high, dots - high], axis=0).astype(BF16)
    for y in range(copies_ref.shape[0]):
        copies_ref[y, :size, :] = grad
        copies_ref[y, size:, :] = parts


def last_kernel(
    own_ref, its_ref, centered_own, centered_its, product_ref, unit_ref, norms_ref,
    enc_out, bias_ref, dec_out,
    own_grad, its_grad, enc_ref, dec_ref, sems,
):
    count = norms_ref.shape[0]
    size = own_ref.shape[1] - 2 * count
    share = size // count
    dots = sum_parts(own_ref, size) + sum_parts(its_ref, size)
    step = 2 * LANES
    copies = []
    for n in range(count // 2):
        lanes = pl.ds(n * step, step)
        for k in (2 * n, 2 * n + 1):
            cut = pl.ds(k * LANES, LANES)
            lines = pl.ds(k * share, share)
            ratio = 1.0 / norms_ref[k : k + 1, :]
            dec_ref[:, cut] = (
                product_ref[:, cut] - unit_ref[:, cut].astype(F32) * dots[k : k + 1]
            ) * ratio
            total = jnp.zeros((share, LANES), F32)
            for y in range(own_ref.shape[0]):
                a, b = own_ref[y, lines, :], its_ref[y, lines, :]
                own_grad[pl.ds(y * share, share), cut] = a
                its_grad[pl.ds(y * share, share), cut] = b
                total = total + a.astype(F32) + b.astype(F32)
            bias_ref[k : k + 1, :] = jnp.sum(total, axis=0, keepdims=True)
        copies.append(pltpu.make_async_copy(dec_ref.at[:, lanes], dec_out.at[:, lanes], sems.at[2 * n]))
        copies[-1].start()
        enc_ref[:, lanes] = dot(centered_own[...], own_grad[:, lanes], ((1,), (0,))) + dot(
            centered_its[...], its_grad[:, lanes], ((1,), (0,))
        )
        copies.append(
            pltpu.make_async_copy(enc_ref.at[:, lanes], enc_out.at[:, lanes], sems.at[2 * n + 1])
        )
        copies[-1].start()
    for copy in copies:
        copy.wait()


def body(residual, picked, enc_weight, enc_bias, dec_weight, dec_bias):
    count_y = lax.axis_size("y")
    count_t = lax.axis_size(TENSOR)
    rows = ROWS // 2
    share = rows // count_y
    piece = rows // count_t
    width, latents = enc_weight.shape
    blocks_n = latents // LANES
    size = share * blocks_n
    extra = 2 * blocks_n
    wide = 2 * width
    matmul = 2 * rows * wide * latents
    moved = 3 << 20

    small = shape((piece, wide), BF16)
    own_rows, other_rows, own_bias = call(
        pick_kernel,
        (small, shape((2 * piece, wide), BF16), shape((1, width), F32)),
        [HBM] * 3,
        (1 << 20, 1 << 17),
        [
            pltpu.SMEM(picked.shape, jnp.int32),
            pltpu.VMEM(residual.shape[::-1], BF16),
            pltpu.SemaphoreType.DMA((3,)),
        ],
    )(picked, residual.T, dec_bias[None])
    tensor_blocks = shape((count_t, piece, wide), BF16)
    local_rows, copies, bias_all = call(
        join_kernel, (small, tensor_blocks, shape((1, wide), F32)), [VMEM] * 3, (1 << 12, 1 << 19)
    )(own_rows, swap(other_rows), own_bias)
    sampled = exchange(copies, TENSOR)
    weights = shape((wide, latents), BF16)
    both = call(
        stage_kernel, weights, [HBM] * 2 + [ANY], (1, moved), [pltpu.SemaphoreType.DMA((2,))]
    )(enc_weight, dec_weight.T, local_rows)
    enc_all, dec_all, squares = call(
        pack_kernel, (weights, weights, shape((extra, LANES), BF16)), [VMEM] * 2, (1 << 21, moved)
    )(both, swap(both))

    pre_blocks, centered = call(
        pre_kernel,
        (shape((count_y, size + extra, LANES), BF16), shape((rows, wide), BF16)),
        [VMEM] * 4,
        (matmul, moved),
    )(sampled, bias_all, enc_all, squares)
    copies, active_share, gate, norms = call(
        act_kernel,
        (
            shape((count_y, size, LANES), BF16),
            shape((size, LANES), BF16),
            shape((size, LANES), F32),
            shape((blocks_n, LANES), F32),
        ),
        [VMEM] * 2,
        (1 << 20, 1 << 20),
    )(exchange(pre_blocks, "y"), enc_bias.reshape(blocks_n, LANES))
    copies = exchange(copies, "y")
    unit = call(unit_kernel, weights, [VMEM] * 2, (1 << 20, moved))(dec_all, norms)
    partial, active = call(
        rebuild_kernel,
        (tensor_blocks, shape((rows, latents), BF16)),
        [VMEM] * 2,
        (matmul, moved),
    )(copies, unit)
    its_active = swap(active)
    turned = shape((width, rows), BF16)
    centered_own, centered_other = call(turn_kernel, (turned, turned), [VMEM], (1 << 20, 1 << 20))(
        centered
    )
    centered_its = swap(centered_other)
    copies = call(error_kernel, tensor_blocks, [VMEM] * 3, (1 << 20, 1 << 20))(
        exchange(partial, TENSOR), bias_all, local_rows
    )
    error = exchange(copies, TENSOR)
    raw_blocks = call(
        raw_kernel, shape((count_y, size, LANES), BF16), [VMEM] * 2, (matmul, moved)
    )(error, unit)
    err_grad = error.reshape(rows, wide)
    its_err = swap(err_grad[:, width:])
    product = dot(err_grad[:, :width], active, ((0,), (0,))) + dot(
        its_err, its_active, ((0,), (0,))
    )
    own = exchange(
        call(
            grad_kernel,
            shape((count_y, size + extra, LANES), BF16),
            [VMEM] * 3,
            (1 << 20, 1 << 20),
        )(exchange(raw_blocks, "y"), active_share, gate),
        "y",
    )
    its = swap(own)
    out = shape((width, latents), F32)
    enc_grad, bias_grad, dec_grad = call(
        last_kernel,
        (out, shape((blocks_n, LANES), F32), out),
        [VMEM] * 7,
        (matmul, 2 * moved),
        [
            pltpu.VMEM((rows, latents), BF16),
            pltpu.VMEM((rows, latents), BF16),
            pltpu.VMEM((width, latents), F32),
            pltpu.VMEM((width, latents), F32),
            pltpu.SemaphoreType.DMA((blocks_n,)),
        ],
        (ANY, VMEM, ANY),
    )(own, its, centered_own, centered_its, product, unit[:width], norms)
    return (enc_grad, bias_grad.reshape(latents), dec_grad.T)


def solution(mesh):
    grid = Mesh(mesh.devices.reshape(8, 2, 4, 8), ("y", "core", "x", "z"))
    dp = ("y", "core")
    return jax.shard_map(
        body,
        mesh=grid,
        in_specs=(
            P(TENSOR, dp),
            P(TENSOR),
            P(dp, TENSOR),
            P(TENSOR),
            P(TENSOR, dp),
            P(dp),
        ),
        out_specs=(P(dp, TENSOR), P(TENSOR), P(TENSOR, dp)),
        check_vma=False,
    )
```

```python
import jax
import jax.numpy as jnp
from jax import lax
from jax.experimental import pallas as pl
from jax.experimental.pallas import tpu as pltpu
from jax.sharding import Mesh
from jax.sharding import PartitionSpec as P

ROWS = 512
LANES = 128
TENSOR = ("x", "z")
F32 = jnp.float32
BF16 = jnp.bfloat16
SHARPNESS = 8.0
VMEM = pl.BlockSpec(memory_space=pltpu.VMEM)
ANY = pl.BlockSpec(memory_space=pl.ANY)
HBM = pl.BlockSpec(memory_space=pltpu.HBM)


def exchange(blocks, axis):
    return lax.all_to_all(blocks, axis, 0, 0, tiled=False)


def swap(block):
    return lax.ppermute(block, "core", [(0, 1), (1, 0)])


def dot(a, b, dims):
    return lax.dot_general(a, b, (dims, ((), ())), preferred_element_type=F32)


def call(kernel, outs, specs, cost, scratch=(), out_specs=None, limit=12):
    flops, moved = cost
    return pl.pallas_call(
        kernel,
        out_shape=outs,
        in_specs=specs,
        out_specs=jax.tree.map(lambda _: VMEM, outs) if out_specs is None else out_specs,
        scratch_shapes=list(scratch),
        compiler_params=pltpu.CompilerParams(vmem_limit_bytes=limit * 1024 * 1024),
        cost_estimate=pl.CostEstimate(flops=flops, bytes_accessed=moved, transcendentals=0),
    )


def shape(dims, kind):
    return jax.ShapeDtypeStruct(dims, kind)


def pick_kernel(picked_hbm, residual_hbm, own_ref, other_ref, picked, table, sems):
    width, tokens = table.shape
    piece = own_ref.shape[0]
    pairs = ((residual_hbm, table), (picked_hbm, picked))
    copies = [pltpu.make_async_copy(a, b, sems.at[i]) for i, (a, b) in enumerate(pairs)]
    for copy in copies:
        copy.start()
    for copy in copies:
        copy.wait()
    core = lax.axis_index("core")
    place = lax.axis_index("x") * lax.axis_size("z") + lax.axis_index("z")
    row = lax.broadcasted_iota(jnp.int32, (piece, tokens), 0)
    token = lax.broadcasted_iota(jnp.int32, (piece, tokens), 1) + place * tokens
    columns = table[...]
    zeros = jnp.zeros_like(columns)

    def pick(start, columns):
        wanted = jnp.zeros((piece, tokens), jnp.int32)
        for i in range(piece):
            wanted = jnp.where(row == i, picked[start + i], wanted)
        hot = jnp.where(wanted == token, 1.0, 0.0).astype(BF16)
        return dot(hot, columns, ((1,), (1,))).astype(BF16)

    own_ref[...] = pick(core * piece, jnp.concatenate([columns, zeros], axis=0))
    other_ref[...] = pick((1 - core) * piece, jnp.concatenate([zeros, columns], axis=0))


def join_kernel(own_ref, got_ref, rows_ref, copies_ref):
    rows = own_ref[...] + got_ref[...]
    rows_ref[...] = rows
    for i in range(copies_ref.shape[0]):
        copies_ref[i] = rows


def turn_kernel(value_ref, own_ref, other_ref):
    turned = value_ref[...].astype(F32).T
    width = own_ref.shape[0]
    own_ref[...] = turned[:width].astype(BF16)
    other_ref[...] = turned[width:].astype(BF16)


def spread(value, out_ref, first):
    share = value.shape[0] // out_ref.shape[0]
    for y in range(out_ref.shape[0]):
        for k in range(value.shape[1] // LANES):
            out_ref[y, pl.ds((first + k) * share, share), :] = value[
                y * share : (y + 1) * share, k * LANES : (k + 1) * LANES
            ]


def pre_kernel(centered_ref, enc_own, enc_other, out_ref, enc_ref):
    width, latents = enc_own.shape
    step = 2 * LANES
    for n in range(latents // step):
        lanes = pl.ds(n * step, step)
        enc_ref[:width, lanes] = enc_own[:, lanes]
        enc_ref[width:, lanes] = enc_other[:, lanes]
        part = dot(centered_ref[...], enc_ref[:, lanes], ((1,), (0,)))
        spread(part.astype(BF16), out_ref, 2 * n)


def sum_blocks(blocks_ref, size):
    total = blocks_ref[0, :size, :].astype(F32)
    for y in range(1, blocks_ref.shape[0]):
        total = total + blocks_ref[y, :size, :].astype(F32)
    return total


def sum_parts(blocks_ref, size):
    total = blocks_ref[0, size:, :].astype(F32)
    for y in range(1, blocks_ref.shape[0]):
        total = total + blocks_ref[y, size:, :].astype(F32)
    half = total.shape[0] // 2
    return total[:half] + total[half:]


def soft_parts(total, bias):
    value = SHARPNESS * (total + bias)
    small = jnp.exp(-jnp.abs(value))
    soft = jnp.maximum(value, 0.0) + jnp.log1p(small)
    return value, small, (soft / SHARPNESS).astype(BF16)


def act_kernel(blocks_ref, bias_ref, squares_ref, copies_ref):
    size = blocks_ref.shape[1]
    share = size // bias_ref.shape[0]
    total = sum_blocks(blocks_ref, size)
    squares = squares_ref[...]
    high = squares.astype(BF16).astype(F32)
    parts = jnp.concatenate([high, squares - high], axis=0).astype(BF16)
    for k in range(bias_ref.shape[0]):
        lines = slice(k * share, (k + 1) * share)
        _, _, active = soft_parts(total[lines], bias_ref[k : k + 1, :])
        for y in range(copies_ref.shape[0]):
            copies_ref[y, lines, :] = active
    for y in range(copies_ref.shape[0]):
        copies_ref[y, size:, :] = parts


def join_lanes(copies_ref, active_ref, share, k):
    for y in range(copies_ref.shape[0]):
        active_ref[y * share : (y + 1) * share, k * LANES : (k + 1) * LANES] = copies_ref[
            y, k * share : (k + 1) * share, :
        ]


def rebuild_kernel(copies_ref, dec_own, dec_other, out_ref, unit_ref, active_ref):
    width, latents = dec_own.shape
    count = latents // LANES
    size = copies_ref.shape[1] - 2 * count
    norms = jnp.sqrt(sum_parts(copies_ref, size) + 1e-06)
    for k in range(count):
        lanes = pl.ds(k * LANES, LANES)
        norm = norms[k : k + 1]
        unit_ref[:width, lanes] = (dec_own[:, lanes].astype(F32) / norm).astype(BF16)
        unit_ref[width:, lanes] = (dec_other[:, lanes].astype(F32) / norm).astype(BF16)
        join_lanes(copies_ref, active_ref, size // count, k)
    part = dot(active_ref[...], unit_ref[...], ((1,), (1,)))
    out_ref[...] = part.astype(BF16).reshape(out_ref.shape)


def keep_kernel(copies_ref, active_ref, norms_ref):
    count = norms_ref.shape[0]
    size = copies_ref.shape[1] - 2 * count
    norms_ref[...] = jnp.sqrt(sum_parts(copies_ref, size) + 1e-06)
    for k in range(count):
        join_lanes(copies_ref, active_ref, size // count, k)


def error_kernel(blocks_ref, bias_ref, rows_ref, copies_ref):
    total = blocks_ref[0].astype(F32)
    for i in range(1, blocks_ref.shape[0]):
        total = total + blocks_ref[i].astype(F32)
    rebuilt = total + bias_ref[...]
    error = (2.0 / ROWS * (rebuilt - rows_ref[...].astype(F32))).astype(BF16)
    for i in range(copies_ref.shape[0]):
        copies_ref[i] = error


def raw_kernel(error_ref, unit_ref, out_ref):
    count = error_ref.shape[0] * error_ref.shape[1]
    error = error_ref[...].reshape(count, error_ref.shape[2])
    step = 2 * LANES
    for n in range(unit_ref.shape[1] // step):
        part = dot(error, unit_ref[:, n * step : (n + 1) * step], ((1,), (0,)))
        spread(part.astype(BF16), out_ref, 2 * n)


def grad_kernel(blocks_ref, pre_ref, bias_ref, copies_ref):
    size = blocks_ref.shape[1]
    count = bias_ref.shape[0]
    share = size // count
    raw = sum_blocks(blocks_ref, size)
    pre = sum_blocks(pre_ref, size)
    row = lax.broadcasted_iota(jnp.int32, (count, LANES), 0)
    dots = jnp.zeros((count, LANES), F32)
    for k in range(count):
        lines = slice(k * share, (k + 1) * share)
        value, small, active = soft_parts(pre[lines], bias_ref[k : k + 1, :])
        gate = jnp.where(value >= 0.0, 1.0, small) / (1.0 + small)
        grad = ((raw[lines] + 1.0 / ROWS) * gate).astype(BF16)
        for y in range(copies_ref.shape[0]):
            copies_ref[y, lines, :] = grad
        part = jnp.sum(active.astype(F32) * raw[lines], axis=0, keepdims=True)
        dots = jnp.where(row == k, part, dots)
    high = dots.astype(BF16).astype(F32)
    parts = jnp.concatenate([high, dots - high], axis=0).astype(BF16)
    for y in range(copies_ref.shape[0]):
        copies_ref[y, size:, :] = parts


def last_kernel(
    own_ref, its_ref, centered_own, centered_its, product_ref, unit_ref, norms_ref,
    enc_out, bias_ref, dec_out,
    own_grad, its_grad, enc_ref, dec_ref, sems,
):
    count = norms_ref.shape[0]
    size = own_ref.shape[1] - 2 * count
    share = size // count
    dots = sum_parts(own_ref, size) + sum_parts(its_ref, size)
    step = 2 * LANES
    copies = []
    for n in range(count // 2):
        lanes = pl.ds(n * step, step)
        for k in (2 * n, 2 * n + 1):
            cut = pl.ds(k * LANES, LANES)
            lines = pl.ds(k * share, share)
            ratio = 1.0 / norms_ref[k : k + 1, :]
            dec_ref[:, cut] = (
                product_ref[:, cut] - unit_ref[:, cut].astype(F32) * dots[k : k + 1]
            ) * ratio
            total = jnp.zeros((share, LANES), F32)
            for y in range(own_ref.shape[0]):
                a, b = own_ref[y, lines, :], its_ref[y, lines, :]
                own_grad[pl.ds(y * share, share), cut] = a
                its_grad[pl.ds(y * share, share), cut] = b
                total = total + a.astype(F32) + b.astype(F32)
            bias_ref[k : k + 1, :] = jnp.sum(total, axis=0, keepdims=True)
        copies.append(pltpu.make_async_copy(dec_ref.at[:, lanes], dec_out.at[:, lanes], sems.at[2 * n]))
        copies[-1].start()
        enc_ref[:, lanes] = dot(centered_own[...], own_grad[:, lanes], ((1,), (0,))) + dot(
            centered_its[...], its_grad[:, lanes], ((1,), (0,))
        )
        copies.append(
            pltpu.make_async_copy(enc_ref.at[:, lanes], enc_out.at[:, lanes], sems.at[2 * n + 1])
        )
        copies[-1].start()
    for copy in copies:
        copy.wait()


def body(residual, picked, enc_weight, enc_bias, dec_weight, dec_bias):
    count_y = lax.axis_size("y")
    count_t = lax.axis_size(TENSOR)
    rows = ROWS // 2
    share = rows // count_y
    piece = rows // count_t
    width, latents = enc_weight.shape
    blocks_n = latents // LANES
    size = share * blocks_n
    extra = 2 * blocks_n
    wide = 2 * width
    matmul = 2 * rows * wide * latents
    moved = 3 << 20

    small = shape((piece, wide), BF16)
    own_rows, other_rows = call(
        pick_kernel,
        (small, small),
        [HBM] * 2,
        (1 << 20, 1 << 17),
        [
            pltpu.SMEM(picked.shape, jnp.int32),
            pltpu.VMEM(residual.shape[::-1], BF16),
            pltpu.SemaphoreType.DMA((2,)),
        ],
    )(picked, residual.T)
    tensor_blocks = shape((count_t, piece, wide), BF16)
    local_rows, copies = call(join_kernel, (small, tensor_blocks), [VMEM] * 2, (1 << 12, 1 << 19))(
        own_rows, swap(other_rows)
    )
    sampled = exchange(copies, TENSOR)
    bias_all = jnp.concatenate([dec_bias, swap(dec_bias)])[None]
    enc_other = swap(enc_weight)
    centered = (sampled.reshape(rows, wide).astype(F32) - bias_all).astype(BF16)
    pre_blocks = call(
        pre_kernel,
        shape((count_y, size, LANES), BF16),
        [VMEM] * 3,
        (matmul, moved),
        [pltpu.VMEM((wide, latents), BF16)],
    )(centered, enc_weight, enc_other)
    dec_own = dec_weight.T
    dec_other = swap(dec_own)
    squares = jnp.sum(jnp.square(dec_own.astype(F32)) + jnp.square(dec_other.astype(F32)), axis=0)
    blocks = exchange(pre_blocks, "y")
    enc_bias = enc_bias.reshape(blocks_n, LANES)
    copies = call(
        act_kernel, shape((count_y, size + extra, LANES), BF16), [VMEM] * 3, (1 << 20, 1 << 20)
    )(blocks, enc_bias, squares.reshape(blocks_n, LANES))
    copies = exchange(copies, "y")
    partial, unit = call(
        rebuild_kernel,
        (tensor_blocks, shape((wide, latents), BF16)),
        [VMEM] * 3,
        (matmul, moved),
        [pltpu.VMEM((rows, latents), BF16)],
    )(copies, dec_own, dec_other)
    active, norms = call(
        keep_kernel,
        (shape((rows, latents), BF16), shape((blocks_n, LANES), F32)),
        [VMEM],
        (1 << 20, 1 << 20),
    )(copies)
    its_active = swap(active)
    turned = shape((width, rows), BF16)
    centered_own, centered_other = call(turn_kernel, (turned, turned), [VMEM], (1 << 20, 1 << 20))(
        centered
    )
    centered_its = swap(centered_other)
    errors = call(error_kernel, tensor_blocks, [VMEM] * 3, (1 << 20, 1 << 20))(
        exchange(partial, TENSOR), bias_all, local_rows
    )
    error = exchange(errors, TENSOR)
    raw_blocks = call(
        raw_kernel, shape((count_y, size, LANES), BF16), [VMEM] * 2, (matmul, moved)
    )(error, unit)
    err_grad = error.reshape(rows, wide)
    its_err = swap(err_grad[:, width:])
    product = dot(err_grad[:, :width], active, ((0,), (0,))) + dot(
        its_err, its_active, ((0,), (0,))
    )
    own = exchange(
        call(
            grad_kernel,
            shape((count_y, size + extra, LANES), BF16),
            [VMEM] * 3,
            (1 << 20, 1 << 20),
        )(exchange(raw_blocks, "y"), blocks, enc_bias),
        "y",
    )
    its = swap(own)
    out = shape((width, latents), F32)
    enc_grad, bias_grad, dec_grad = call(
        last_kernel,
        (out, shape((blocks_n, LANES), F32), out),
        [VMEM] * 7,
        (matmul, 2 * moved),
        [
            pltpu.VMEM((rows, latents), BF16),
            pltpu.VMEM((rows, latents), BF16),
            pltpu.VMEM((width, latents), F32),
            pltpu.VMEM((width, latents), F32),
            pltpu.SemaphoreType.DMA((blocks_n,)),
        ],
        (ANY, VMEM, ANY),
    )(own, its, centered_own, centered_its, product, unit[:width], norms)
    return (enc_grad, bias_grad.reshape(latents), dec_grad.T)


def solution(mesh):
    grid = Mesh(mesh.devices.reshape(8, 2, 4, 8), ("y", "core", "x", "z"))
    dp = ("y", "core")
    return jax.shard_map(
        body,
        mesh=grid,
        in_specs=(
            P(TENSOR, dp),
            P(TENSOR),
            P(dp, TENSOR),
            P(TENSOR),
            P(TENSOR, dp),
            P(dp),
        ),
        out_specs=(P(dp, TENSOR), P(TENSOR), P(TENSOR, dp)),
        check_vma=False,
    )
```

```python
import jax
import jax.numpy as jnp
from jax import lax
from jax.experimental import pallas as pl
from jax.experimental.pallas import tpu as pltpu
from jax.sharding import Mesh
from jax.sharding import PartitionSpec as P

ROWS = 512
LANES = 128
TENSOR = ("x", "z")
F32 = jnp.float32
BF16 = jnp.bfloat16
SHARPNESS = 8.0
VMEM = pl.BlockSpec(memory_space=pltpu.VMEM)
ANY = pl.BlockSpec(memory_space=pl.ANY)
HBM = pl.BlockSpec(memory_space=pltpu.HBM)


def exchange(blocks, axis):
    return lax.all_to_all(blocks, axis, 0, 0, tiled=False)


def swap(block):
    return lax.ppermute(block, "core", [(0, 1), (1, 0)])


def dot(a, b, dims):
    return lax.dot_general(a, b, (dims, ((), ())), preferred_element_type=F32)


def call(kernel, outs, specs, cost, scratch=(), out_specs=None, limit=12):
    flops, moved = cost
    return pl.pallas_call(
        kernel,
        out_shape=outs,
        in_specs=specs,
        out_specs=jax.tree.map(lambda _: VMEM, outs) if out_specs is None else out_specs,
        scratch_shapes=list(scratch),
        compiler_params=pltpu.CompilerParams(vmem_limit_bytes=limit * 1024 * 1024),
        cost_estimate=pl.CostEstimate(flops=flops, bytes_accessed=moved, transcendentals=0),
    )


def shape(dims, kind):
    return jax.ShapeDtypeStruct(dims, kind)


def pick_kernel(picked_hbm, residual_hbm, own_ref, other_ref, picked, table, sems):
    width, tokens = table.shape
    piece = own_ref.shape[0]
    pairs = ((residual_hbm, table), (picked_hbm, picked))
    copies = [pltpu.make_async_copy(a, b, sems.at[i]) for i, (a, b) in enumerate(pairs)]
    for copy in copies:
        copy.start()
    for copy in copies:
        copy.wait()
    core = lax.axis_index("core")
    place = lax.axis_index("x") * lax.axis_size("z") + lax.axis_index("z")
    row = lax.broadcasted_iota(jnp.int32, (piece, tokens), 0)
    token = lax.broadcasted_iota(jnp.int32, (piece, tokens), 1) + place * tokens
    columns = table[...]
    zeros = jnp.zeros_like(columns)

    def pick(start, columns):
        wanted = jnp.zeros((piece, tokens), jnp.int32)
        for i in range(piece):
            wanted = jnp.where(row == i, picked[start + i], wanted)
        hot = jnp.where(wanted == token, 1.0, 0.0).astype(BF16)
        return dot(hot, columns, ((1,), (1,))).astype(BF16)

    own_ref[...] = pick(core * piece, jnp.concatenate([columns, zeros], axis=0))
    other_ref[...] = pick((1 - core) * piece, jnp.concatenate([zeros, columns], axis=0))


def join_kernel(own_ref, got_ref, rows_ref, copies_ref):
    rows = own_ref[...] + got_ref[...]
    rows_ref[...] = rows
    for i in range(copies_ref.shape[0]):
        copies_ref[i] = rows


def turn_kernel(value_ref, own_ref, other_ref):
    turned = value_ref[...].astype(F32).T
    width = own_ref.shape[0]
    own_ref[...] = turned[:width].astype(BF16)
    other_ref[...] = turned[width:].astype(BF16)


def spread(value, out_ref, first):
    share = value.shape[0] // out_ref.shape[0]
    for y in range(out_ref.shape[0]):
        for k in range(value.shape[1] // LANES):
            out_ref[y, pl.ds((first + k) * share, share), :] = value[
                y * share : (y + 1) * share, k * LANES : (k + 1) * LANES
            ]


def pre_kernel(centered_ref, enc_own, enc_other, squares_ref, out_ref, enc_ref):
    width, latents = enc_own.shape
    step = 2 * LANES
    squares = squares_ref[...]
    high = squares.astype(BF16).astype(F32)
    parts = jnp.concatenate([high, squares - high], axis=0).astype(BF16)
    for y in range(out_ref.shape[0]):
        out_ref[y, pl.ds(out_ref.shape[1] - parts.shape[0], parts.shape[0]), :] = parts
    for n in range(latents // step):
        lanes = pl.ds(n * step, step)
        enc_ref[:width, lanes] = enc_own[:, lanes]
        enc_ref[width:, lanes] = enc_other[:, lanes]
        part = dot(centered_ref[...], enc_ref[:, lanes], ((1,), (0,)))
        spread(part.astype(BF16), out_ref, 2 * n)


def sum_blocks(blocks_ref, size):
    total = blocks_ref[0, :size, :].astype(F32)
    for y in range(1, blocks_ref.shape[0]):
        total = total + blocks_ref[y, :size, :].astype(F32)
    return total


def sum_parts(blocks_ref, size):
    total = blocks_ref[0, size:, :].astype(F32)
    for y in range(1, blocks_ref.shape[0]):
        total = total + blocks_ref[y, size:, :].astype(F32)
    half = total.shape[0] // 2
    return total[:half] + total[half:]


def soft_parts(total, bias):
    value = SHARPNESS * (total + bias)
    small = jnp.exp(-jnp.abs(value))
    soft = jnp.maximum(value, 0.0) + jnp.log1p(small)
    return value, small, (soft / SHARPNESS).astype(BF16)


def act_kernel(blocks_ref, bias_ref, copies_ref):
    size = copies_ref.shape[1]
    share = size // bias_ref.shape[0]
    total = sum_blocks(blocks_ref, size)
    for k in range(bias_ref.shape[0]):
        lines = slice(k * share, (k + 1) * share)
        _, _, active = soft_parts(total[lines], bias_ref[k : k + 1, :])
        for y in range(copies_ref.shape[0]):
            copies_ref[y, lines, :] = active


def norms_of(blocks_ref, count):
    return jnp.sqrt(sum_parts(blocks_ref, blocks_ref.shape[1] - 2 * count) + 1e-06)


def unit_kernel(blocks_ref, dec_own, dec_other, unit_ref):
    width, latents = dec_own.shape
    norms = norms_of(blocks_ref, latents // LANES)
    for k in range(latents // LANES):
        lanes = pl.ds(k * LANES, LANES)
        norm = norms[k : k + 1]
        unit_ref[:width, lanes] = (dec_own[:, lanes].astype(F32) / norm).astype(BF16)
        unit_ref[width:, lanes] = (dec_other[:, lanes].astype(F32) / norm).astype(BF16)


def join_lanes(copies_ref, active_ref, share, k):
    for y in range(copies_ref.shape[0]):
        active_ref[y * share : (y + 1) * share, k * LANES : (k + 1) * LANES] = copies_ref[
            y, k * share : (k + 1) * share, :
        ]


def rebuild_kernel(copies_ref, unit_ref, out_ref, active_ref):
    count = unit_ref.shape[1] // LANES
    for k in range(count):
        join_lanes(copies_ref, active_ref, copies_ref.shape[1] // count, k)
    part = dot(active_ref[...], unit_ref[...], ((1,), (1,)))
    out_ref[...] = part.astype(BF16).reshape(out_ref.shape)


def keep_kernel(copies_ref, active_ref):
    count = active_ref.shape[1] // LANES
    for k in range(count):
        join_lanes(copies_ref, active_ref, copies_ref.shape[1] // count, k)


def error_kernel(blocks_ref, bias_ref, rows_ref, copies_ref):
    total = blocks_ref[0].astype(F32)
    for i in range(1, blocks_ref.shape[0]):
        total = total + blocks_ref[i].astype(F32)
    rebuilt = total + bias_ref[...]
    error = (2.0 / ROWS * (rebuilt - rows_ref[...].astype(F32))).astype(BF16)
    for i in range(copies_ref.shape[0]):
        copies_ref[i] = error


def raw_kernel(error_ref, unit_ref, out_ref):
    count = error_ref.shape[0] * error_ref.shape[1]
    error = error_ref[...].reshape(count, error_ref.shape[2])
    step = 2 * LANES
    for n in range(unit_ref.shape[1] // step):
        part = dot(error, unit_ref[:, n * step : (n + 1) * step], ((1,), (0,)))
        spread(part.astype(BF16), out_ref, 2 * n)


def grad_kernel(blocks_ref, pre_ref, bias_ref, copies_ref):
    size = blocks_ref.shape[1]
    count = bias_ref.shape[0]
    share = size // count
    raw = sum_blocks(blocks_ref, size)
    pre = sum_blocks(pre_ref, size)
    row = lax.broadcasted_iota(jnp.int32, (count, LANES), 0)
    dots = jnp.zeros((count, LANES), F32)
    for k in range(count):
        lines = slice(k * share, (k + 1) * share)
        value, small, active = soft_parts(pre[lines], bias_ref[k : k + 1, :])
        gate = jnp.where(value >= 0.0, 1.0, small) / (1.0 + small)
        grad = ((raw[lines] + 1.0 / ROWS) * gate).astype(BF16)
        for y in range(copies_ref.shape[0]):
            copies_ref[y, lines, :] = grad
        part = jnp.sum(active.astype(F32) * raw[lines], axis=0, keepdims=True)
        dots = jnp.where(row == k, part, dots)
    high = dots.astype(BF16).astype(F32)
    parts = jnp.concatenate([high, dots - high], axis=0).astype(BF16)
    for y in range(copies_ref.shape[0]):
        copies_ref[y, size:, :] = parts


def last_kernel(
    own_ref, its_ref, centered_own, centered_its, product_ref, unit_ref, blocks_ref,
    enc_out, bias_ref, dec_out,
    own_grad, its_grad, enc_ref, dec_ref, sems,
):
    count = enc_ref.shape[1] // LANES
    norms = norms_of(blocks_ref, count)
    size = own_ref.shape[1] - 2 * count
    share = size // count
    dots = sum_parts(own_ref, size) + sum_parts(its_ref, size)
    step = 2 * LANES
    copies = []
    for n in range(count // 2):
        lanes = pl.ds(n * step, step)
        for k in (2 * n, 2 * n + 1):
            cut = pl.ds(k * LANES, LANES)
            lines = pl.ds(k * share, share)
            ratio = 1.0 / norms[k : k + 1]
            dec_ref[:, cut] = (
                product_ref[:, cut] - unit_ref[:, cut].astype(F32) * dots[k : k + 1]
            ) * ratio
            total = jnp.zeros((share, LANES), F32)
            for y in range(own_ref.shape[0]):
                a, b = own_ref[y, lines, :], its_ref[y, lines, :]
                own_grad[pl.ds(y * share, share), cut] = a
                its_grad[pl.ds(y * share, share), cut] = b
                total = total + a.astype(F32) + b.astype(F32)
            bias_ref[k : k + 1, :] = jnp.sum(total, axis=0, keepdims=True)
        copies.append(pltpu.make_async_copy(dec_ref.at[:, lanes], dec_out.at[:, lanes], sems.at[2 * n]))
        copies[-1].start()
        enc_ref[:, lanes] = dot(centered_own[...], own_grad[:, lanes], ((1,), (0,))) + dot(
            centered_its[...], its_grad[:, lanes], ((1,), (0,))
        )
        copies.append(
            pltpu.make_async_copy(enc_ref.at[:, lanes], enc_out.at[:, lanes], sems.at[2 * n + 1])
        )
        copies[-1].start()
    for copy in copies:
        copy.wait()


def body(residual, picked, enc_weight, enc_bias, dec_weight, dec_bias):
    count_y = lax.axis_size("y")
    count_t = lax.axis_size(TENSOR)
    rows = ROWS // 2
    share = rows // count_y
    piece = rows // count_t
    width, latents = enc_weight.shape
    blocks_n = latents // LANES
    size = share * blocks_n
    extra = 2 * blocks_n
    wide = 2 * width
    matmul = 2 * rows * wide * latents
    moved = 3 << 20

    small = shape((piece, wide), BF16)
    own_rows, other_rows = call(
        pick_kernel,
        (small, small),
        [HBM] * 2,
        (1 << 20, 1 << 17),
        [
            pltpu.SMEM(picked.shape, jnp.int32),
            pltpu.VMEM(residual.shape[::-1], BF16),
            pltpu.SemaphoreType.DMA((2,)),
        ],
    )(picked, residual.T)
    tensor_blocks = shape((count_t, piece, wide), BF16)
    local_rows, copies = call(join_kernel, (small, tensor_blocks), [VMEM] * 2, (1 << 12, 1 << 19))(
        own_rows, swap(other_rows)
    )
    sampled = exchange(copies, TENSOR)
    bias_all = jnp.concatenate([dec_bias, swap(dec_bias)])[None]
    enc_other = swap(enc_weight)
    dec_own = dec_weight.T
    dec_other = swap(dec_own)
    squares = jnp.sum(jnp.square(dec_own.astype(F32)) + jnp.square(dec_other.astype(F32)), axis=0)
    centered = (sampled.reshape(rows, wide).astype(F32) - bias_all).astype(BF16)
    pre_blocks = call(
        pre_kernel,
        shape((count_y, size + extra, LANES), BF16),
        [VMEM] * 4,
        (matmul, moved),
        [pltpu.VMEM((wide, latents), BF16)],
    )(centered, enc_weight, enc_other, squares.reshape(blocks_n, LANES))
    blocks = exchange(pre_blocks, "y")
    enc_bias = enc_bias.reshape(blocks_n, LANES)
    copies = call(
        act_kernel, shape((count_y, size, LANES), BF16), [VMEM] * 2, (1 << 20, 1 << 20)
    )(blocks, enc_bias)
    unit = call(unit_kernel, shape((wide, latents), BF16), [VMEM] * 3, (1 << 20, moved))(
        blocks, dec_own, dec_other
    )
    copies = exchange(copies, "y")
    partial = call(
        rebuild_kernel,
        tensor_blocks,
        [VMEM] * 2,
        (matmul, moved),
        [pltpu.VMEM((rows, latents), BF16)],
    )(copies, unit)
    active = call(keep_kernel, shape((rows, latents), BF16), [VMEM], (1 << 20, 1 << 20))(copies)
    its_active = swap(active)
    turned = shape((width, rows), BF16)
    centered_own, centered_other = call(turn_kernel, (turned, turned), [VMEM], (1 << 20, 1 << 20))(
        centered
    )
    centered_its = swap(centered_other)
    errors = call(error_kernel, tensor_blocks, [VMEM] * 3, (1 << 20, 1 << 20))(
        exchange(partial, TENSOR), bias_all, local_rows
    )
    error = exchange(errors, TENSOR)
    raw_blocks = call(
        raw_kernel, shape((count_y, size, LANES), BF16), [VMEM] * 2, (matmul, moved)
    )(error, unit)
    err_grad = error.reshape(rows, wide)
    its_err = swap(err_grad[:, width:])
    product = dot(err_grad[:, :width], active, ((0,), (0,))) + dot(
        its_err, its_active, ((0,), (0,))
    )
    own = exchange(
        call(
            grad_kernel,
            shape((count_y, size + extra, LANES), BF16),
            [VMEM] * 3,
            (1 << 20, 1 << 20),
        )(exchange(raw_blocks, "y"), blocks, enc_bias),
        "y",
    )
    its = swap(own)
    out = shape((width, latents), F32)
    enc_grad, bias_grad, dec_grad = call(
        last_kernel,
        (out, shape((blocks_n, LANES), F32), out),
        [VMEM] * 7,
        (matmul, 2 * moved),
        [
            pltpu.VMEM((rows, latents), BF16),
            pltpu.VMEM((rows, latents), BF16),
            pltpu.VMEM((width, latents), F32),
            pltpu.VMEM((width, latents), F32),
            pltpu.SemaphoreType.DMA((blocks_n,)),
        ],
        (ANY, VMEM, ANY),
    )(own, its, centered_own, centered_its, product, unit[:width], blocks)
    return (enc_grad, bias_grad.reshape(latents), dec_grad.T)


def solution(mesh):
    grid = Mesh(mesh.devices.reshape(8, 2, 4, 8), ("y", "core", "x", "z"))
    dp = ("y", "core")
    return jax.shard_map(
        body,
        mesh=grid,
        in_specs=(
            P(TENSOR, dp),
            P(TENSOR),
            P(dp, TENSOR),
            P(TENSOR),
            P(TENSOR, dp),
            P(dp),
        ),
        out_specs=(P(dp, TENSOR), P(TENSOR), P(TENSOR, dp)),
        check_vma=False,
    )
```

```python
import jax
import jax.numpy as jnp
from jax import lax
from jax.experimental import pallas as pl
from jax.experimental.pallas import tpu as pltpu
from jax.sharding import Mesh
from jax.sharding import PartitionSpec as P

ROWS = 512
LANES = 128
TENSOR = ("x", "z")
F32 = jnp.float32
BF16 = jnp.bfloat16
SHARPNESS = 8.0
VMEM = pl.BlockSpec(memory_space=pltpu.VMEM)
ANY = pl.BlockSpec(memory_space=pl.ANY)
HBM = pl.BlockSpec(memory_space=pltpu.HBM)


def exchange(blocks, axis):
    return lax.all_to_all(blocks, axis, 0, 0, tiled=False)


def swap(block):
    return lax.ppermute(block, "core", [(0, 1), (1, 0)])


def dot(a, b, dims):
    return lax.dot_general(a, b, (dims, ((), ())), preferred_element_type=F32)


def call(kernel, outs, specs, cost, scratch=(), out_specs=None, limit=12):
    flops, moved = cost
    return pl.pallas_call(
        kernel,
        out_shape=outs,
        in_specs=specs,
        out_specs=jax.tree.map(lambda _: VMEM, outs) if out_specs is None else out_specs,
        scratch_shapes=list(scratch),
        compiler_params=pltpu.CompilerParams(vmem_limit_bytes=limit * 1024 * 1024),
        cost_estimate=pl.CostEstimate(flops=flops, bytes_accessed=moved, transcendentals=0),
    )


def shape(dims, kind):
    return jax.ShapeDtypeStruct(dims, kind)


def pick_kernel(picked_hbm, residual_hbm, own_ref, other_ref, picked, table, sems):
    width, tokens = table.shape
    piece = own_ref.shape[0]
    pairs = ((residual_hbm, table), (picked_hbm, picked))
    copies = [pltpu.make_async_copy(a, b, sems.at[i]) for i, (a, b) in enumerate(pairs)]
    for copy in copies:
        copy.start()
    for copy in copies:
        copy.wait()
    core = lax.axis_index("core")
    place = lax.axis_index("x") * lax.axis_size("z") + lax.axis_index("z")
    row = lax.broadcasted_iota(jnp.int32, (piece, tokens), 0)
    token = lax.broadcasted_iota(jnp.int32, (piece, tokens), 1) + place * tokens
    columns = table[...]
    zeros = jnp.zeros_like(columns)

    def pick(start, columns):
        wanted = jnp.zeros((piece, tokens), jnp.int32)
        for i in range(piece):
            wanted = jnp.where(row == i, picked[start + i], wanted)
        hot = jnp.where(wanted == token, 1.0, 0.0).astype(BF16)
        return dot(hot, columns, ((1,), (1,))).astype(BF16)

    own_ref[...] = pick(core * piece, jnp.concatenate([columns, zeros], axis=0))
    other_ref[...] = pick((1 - core) * piece, jnp.concatenate([zeros, columns], axis=0))


def join_kernel(own_ref, got_ref, rows_ref, copies_ref):
    rows = own_ref[...] + got_ref[...]
    rows_ref[...] = rows
    for i in range(copies_ref.shape[0]):
        copies_ref[i] = rows


def turn_kernel(value_ref, own_ref, other_ref):
    turned = value_ref[...].astype(F32).T
    width = own_ref.shape[0]
    own_ref[...] = turned[:width].astype(BF16)
    other_ref[...] = turned[width:].astype(BF16)


def spread(value, out_ref, first):
    share = value.shape[0] // out_ref.shape[0]
    for y in range(out_ref.shape[0]):
        for k in range(value.shape[1] // LANES):
            out_ref[y, pl.ds((first + k) * share, share), :] = value[
                y * share : (y + 1) * share, k * LANES : (k + 1) * LANES
            ]


def pre_kernel(centered_ref, enc_own, enc_other, squares_ref, out_ref, enc_ref):
    width, latents = enc_own.shape
    step = 2 * LANES
    squares = squares_ref[...]
    high = squares.astype(BF16).astype(F32)
    parts = jnp.concatenate([high, squares - high], axis=0).astype(BF16)
    for y in range(out_ref.shape[0]):
        out_ref[y, pl.ds(out_ref.shape[1] - parts.shape[0], parts.shape[0]), :] = parts
    for n in range(latents // step):
        lanes = pl.ds(n * step, step)
        enc_ref[:width, lanes] = enc_own[:, lanes]
        enc_ref[width:, lanes] = enc_other[:, lanes]
        part = dot(centered_ref[...], enc_ref[:, lanes], ((1,), (0,)))
        spread(part.astype(BF16), out_ref, 2 * n)


def sum_blocks(blocks_ref, size):
    total = blocks_ref[0, :size, :].astype(F32)
    for y in range(1, blocks_ref.shape[0]):
        total = total + blocks_ref[y, :size, :].astype(F32)
    return total


def sum_parts(blocks_ref, size):
    total = blocks_ref[0, size:, :].astype(F32)
    for y in range(1, blocks_ref.shape[0]):
        total = total + blocks_ref[y, size:, :].astype(F32)
    half = total.shape[0] // 2
    return total[:half] + total[half:]


def soft_parts(total, bias):
    value = SHARPNESS * (total + bias)
    small = jnp.exp(-jnp.abs(value))
    soft = jnp.maximum(value, 0.0) + jnp.log1p(small)
    return value, small, (soft / SHARPNESS).astype(BF16)


def act_kernel(blocks_ref, bias_ref, copies_ref):
    size = copies_ref.shape[1]
    share = size // bias_ref.shape[0]
    total = sum_blocks(blocks_ref, size)
    for k in range(bias_ref.shape[0]):
        lines = slice(k * share, (k + 1) * share)
        _, _, active = soft_parts(total[lines], bias_ref[k : k + 1, :])
        for y in range(copies_ref.shape[0]):
            copies_ref[y, lines, :] = active


def norms_of(blocks_ref, count):
    return jnp.sqrt(sum_parts(blocks_ref, blocks_ref.shape[1] - 2 * count) + 1e-06)


def unit_kernel(blocks_ref, dec_own, dec_other, unit_ref):
    width, latents = dec_own.shape
    norms = norms_of(blocks_ref, latents // LANES)
    for k in range(latents // LANES):
        lanes = pl.ds(k * LANES, LANES)
        norm = norms[k : k + 1]
        unit_ref[:width, lanes] = (dec_own[:, lanes].astype(F32) / norm).astype(BF16)
        unit_ref[width:, lanes] = (dec_other[:, lanes].astype(F32) / norm).astype(BF16)


def join_lanes(copies_ref, active_ref, share, k):
    for y in range(copies_ref.shape[0]):
        active_ref[y * share : (y + 1) * share, k * LANES : (k + 1) * LANES] = copies_ref[
            y, k * share : (k + 1) * share, :
        ]


def rebuild_kernel(copies_ref, unit_ref, out_ref, active_ref):
    count = unit_ref.shape[1] // LANES
    for k in range(count):
        join_lanes(copies_ref, active_ref, copies_ref.shape[1] // count, k)
    part = dot(active_ref[...], unit_ref[...], ((1,), (1,)))
    out_ref[...] = part.astype(BF16).reshape(out_ref.shape)


def keep_kernel(copies_ref, active_ref):
    count = active_ref.shape[1] // LANES
    for k in range(count):
        join_lanes(copies_ref, active_ref, copies_ref.shape[1] // count, k)


def error_kernel(blocks_ref, bias_ref, rows_ref, copies_ref):
    total = blocks_ref[0].astype(F32)
    for i in range(1, blocks_ref.shape[0]):
        total = total + blocks_ref[i].astype(F32)
    rebuilt = total + bias_ref[...]
    error = (2.0 / ROWS * (rebuilt - rows_ref[...].astype(F32))).astype(BF16)
    for i in range(copies_ref.shape[0]):
        copies_ref[i] = error


def raw_kernel(error_ref, unit_ref, out_ref):
    count = error_ref.shape[0] * error_ref.shape[1]
    error = error_ref[...].reshape(count, error_ref.shape[2])
    step = 2 * LANES
    for n in range(unit_ref.shape[1] // step):
        part = dot(error, unit_ref[:, n * step : (n + 1) * step], ((1,), (0,)))
        spread(part.astype(BF16), out_ref, 2 * n)


def grad_kernel(blocks_ref, pre_ref, bias_ref, copies_ref):
    size = blocks_ref.shape[1]
    count = bias_ref.shape[0]
    share = size // count
    raw = sum_blocks(blocks_ref, size)
    pre = sum_blocks(pre_ref, size)
    row = lax.broadcasted_iota(jnp.int32, (count, LANES), 0)
    dots = jnp.zeros((count, LANES), F32)
    for k in range(count):
        lines = slice(k * share, (k + 1) * share)
        value, small, active = soft_parts(pre[lines], bias_ref[k : k + 1, :])
        gate = jnp.where(value >= 0.0, 1.0, small) / (1.0 + small)
        grad = ((raw[lines] + 1.0 / ROWS) * gate).astype(BF16)
        for y in range(copies_ref.shape[0]):
            copies_ref[y, lines, :] = grad
        part = jnp.sum(active.astype(F32) * raw[lines], axis=0, keepdims=True)
        dots = jnp.where(row == k, part, dots)
    high = dots.astype(BF16).astype(F32)
    parts = jnp.concatenate([high, dots - high], axis=0).astype(BF16)
    for y in range(copies_ref.shape[0]):
        copies_ref[y, size:, :] = parts


def own_kernel(own_ref, centered_ref, blocks_ref, enc_ref, sums_ref, grad_ref):
    count = enc_ref.shape[1] // LANES
    size = own_ref.shape[1] - 2 * count
    share = size // count
    for k in range(count):
        cut = pl.ds(k * LANES, LANES)
        lines = pl.ds(k * share, share)
        total = jnp.zeros((share, LANES), F32)
        for y in range(own_ref.shape[0]):
            value = own_ref[y, lines, :]
            grad_ref[pl.ds(y * share, share), cut] = value
            total = total + value.astype(F32)
        sums_ref[k : k + 1, :] = jnp.sum(total, axis=0, keepdims=True)
    sums_ref[count : 2 * count] = sum_parts(own_ref, size)
    sums_ref[2 * count :] = 1.0 / norms_of(blocks_ref, count)
    enc_ref[...] = dot(centered_ref[...], grad_ref[...], ((1,), (0,)))


def last_kernel(
    its_ref, part_ref, sums_ref, centered_ref, product_ref, unit_ref,
    enc_out, bias_ref, dec_out,
    grad_ref, enc_ref, dec_ref, sems,
):
    count = enc_ref.shape[1] // LANES
    size = its_ref.shape[1] - 2 * count
    share = size // count
    dots = sums_ref[count : 2 * count] + sum_parts(its_ref, size)
    step = 2 * LANES
    copies = []
    for n in range(count // 2):
        lanes = pl.ds(n * step, step)
        for k in (2 * n, 2 * n + 1):
            cut = pl.ds(k * LANES, LANES)
            lines = pl.ds(k * share, share)
            ratio = sums_ref[2 * count + k : 2 * count + k + 1]
            dec_ref[:, cut] = (
                product_ref[:, cut] - unit_ref[:, cut].astype(F32) * dots[k : k + 1]
            ) * ratio
            total = jnp.zeros((share, LANES), F32)
            for y in range(its_ref.shape[0]):
                value = its_ref[y, lines, :]
                grad_ref[pl.ds(y * share, share), cut] = value
                total = total + value.astype(F32)
            bias_ref[k : k + 1, :] = sums_ref[k : k + 1, :] + jnp.sum(total, axis=0, keepdims=True)
        copies.append(pltpu.make_async_copy(dec_ref.at[:, lanes], dec_out.at[:, lanes], sems.at[2 * n]))
        copies[-1].start()
        enc_ref[:, lanes] = part_ref[:, lanes] + dot(
            centered_ref[...], grad_ref[:, lanes], ((1,), (0,))
        )
        copies.append(
            pltpu.make_async_copy(enc_ref.at[:, lanes], enc_out.at[:, lanes], sems.at[2 * n + 1])
        )
        copies[-1].start()
    for copy in copies:
        copy.wait()


def body(residual, picked, enc_weight, enc_bias, dec_weight, dec_bias):
    count_y = lax.axis_size("y")
    count_t = lax.axis_size(TENSOR)
    rows = ROWS // 2
    share = rows // count_y
    piece = rows // count_t
    width, latents = enc_weight.shape
    blocks_n = latents // LANES
    size = share * blocks_n
    extra = 2 * blocks_n
    wide = 2 * width
    matmul = 2 * rows * wide * latents
    moved = 3 << 20

    small = shape((piece, wide), BF16)
    own_rows, other_rows = call(
        pick_kernel,
        (small, small),
        [HBM] * 2,
        (1 << 20, 1 << 17),
        [
            pltpu.SMEM(picked.shape, jnp.int32),
            pltpu.VMEM(residual.shape[::-1], BF16),
            pltpu.SemaphoreType.DMA((2,)),
        ],
    )(picked, residual.T)
    tensor_blocks = shape((count_t, piece, wide), BF16)
    local_rows, copies = call(join_kernel, (small, tensor_blocks), [VMEM] * 2, (1 << 12, 1 << 19))(
        own_rows, swap(other_rows)
    )
    sampled = exchange(copies, TENSOR)
    bias_all = jnp.concatenate([dec_bias[None], swap(dec_bias)[None]], axis=1)
    enc_other = swap(enc_weight)
    dec_own = dec_weight.T
    dec_other = swap(dec_own)
    squares = jnp.sum(jnp.square(dec_own.astype(F32)) + jnp.square(dec_other.astype(F32)), axis=0)
    centered = (sampled.reshape(rows, wide).astype(F32) - bias_all).astype(BF16)
    pre_blocks = call(
        pre_kernel,
        shape((count_y, size + extra, LANES), BF16),
        [VMEM] * 4,
        (matmul, moved),
        [pltpu.VMEM((wide, latents), BF16)],
    )(centered, enc_weight, enc_other, squares.reshape(blocks_n, LANES))
    blocks = exchange(pre_blocks, "y")
    enc_bias = enc_bias.reshape(blocks_n, LANES)
    copies = call(
        act_kernel, shape((count_y, size, LANES), BF16), [VMEM] * 2, (1 << 20, 1 << 20)
    )(blocks, enc_bias)
    unit = call(unit_kernel, shape((wide, latents), BF16), [VMEM] * 3, (1 << 20, moved))(
        blocks, dec_own, dec_other
    )
    copies = exchange(copies, "y")
    partial = call(
        rebuild_kernel,
        tensor_blocks,
        [VMEM] * 2,
        (matmul, moved),
        [pltpu.VMEM((rows, latents), BF16)],
    )(copies, unit)
    active = call(keep_kernel, shape((rows, latents), BF16), [VMEM], (1 << 20, 1 << 20))(copies)
    its_active = swap(active)
    turned = shape((width, rows), BF16)
    centered_own, centered_other = call(turn_kernel, (turned, turned), [VMEM], (1 << 20, 1 << 20))(
        centered
    )
    centered_its = swap(centered_other)
    errors = call(error_kernel, tensor_blocks, [VMEM] * 3, (1 << 20, 1 << 20))(
        exchange(partial, TENSOR), bias_all, local_rows
    )
    error = exchange(errors, TENSOR)
    raw_blocks = call(
        raw_kernel, shape((count_y, size, LANES), BF16), [VMEM] * 2, (matmul, moved)
    )(error, unit)
    err_grad = error.reshape(rows, wide)
    its_err = swap(err_grad[:, width:])
    product = dot(err_grad[:, :width], active, ((0,), (0,))) + dot(
        its_err, its_active, ((0,), (0,))
    )
    own = exchange(
        call(
            grad_kernel,
            shape((count_y, size + extra, LANES), BF16),
            [VMEM] * 3,
            (1 << 20, 1 << 20),
        )(exchange(raw_blocks, "y"), blocks, enc_bias),
        "y",
    )
    its = swap(own)
    out = shape((width, latents), F32)
    enc_part, sums = call(
        own_kernel,
        (out, shape((3 * blocks_n, LANES), F32)),
        [VMEM] * 3,
        (40 * matmul, 20 * moved),
        [pltpu.VMEM((rows, latents), BF16)],
    )(own, centered_own, blocks)
    enc_grad, bias_grad, dec_grad = call(
        last_kernel,
        (out, shape((blocks_n, LANES), F32), out),
        [VMEM] * 6,
        (matmul, 2 * moved),
        [
            pltpu.VMEM((rows, latents), BF16),
            pltpu.VMEM((width, latents), F32),
            pltpu.VMEM((width, latents), F32),
            pltpu.SemaphoreType.DMA((blocks_n,)),
        ],
        (ANY, VMEM, ANY),
    )(its, enc_part, sums, centered_its, product, unit[:width])
    return (enc_grad, bias_grad.reshape(latents), dec_grad.T)


def solution(mesh):
    grid = Mesh(mesh.devices.reshape(8, 2, 4, 8), ("y", "core", "x", "z"))
    dp = ("y", "core")
    return jax.shard_map(
        body,
        mesh=grid,
        in_specs=(
            P(TENSOR, dp),
            P(TENSOR),
            P(dp, TENSOR),
            P(TENSOR),
            P(TENSOR, dp),
            P(dp),
        ),
        out_specs=(P(dp, TENSOR), P(TENSOR), P(TENSOR, dp)),
        check_vma=False,
    )
```

```python
import jax
import jax.numpy as jnp
from jax import lax
from jax.experimental import pallas as pl
from jax.experimental.pallas import tpu as pltpu
from jax.sharding import Mesh
from jax.sharding import PartitionSpec as P

ROWS = 512
LANES = 128
TENSOR = ("x", "z")
F32 = jnp.float32
BF16 = jnp.bfloat16
SHARPNESS = 8.0
PICK = 56
VMEM = pl.BlockSpec(memory_space=pltpu.VMEM)
ANY = pl.BlockSpec(memory_space=pl.ANY)
HBM = pl.BlockSpec(memory_space=pltpu.HBM)


def exchange(blocks, axis):
    return lax.all_to_all(blocks, axis, 0, 0, tiled=False)


def swap(block):
    return lax.ppermute(block, "core", [(0, 1), (1, 0)])


def dot(a, b, dims):
    return lax.dot_general(a, b, (dims, ((), ())), preferred_element_type=F32)


def call(kernel, outs, specs, cost, scratch=(), out_specs=None, limit=12):
    flops, moved = cost
    return pl.pallas_call(
        kernel,
        out_shape=outs,
        in_specs=specs,
        out_specs=jax.tree.map(lambda _: VMEM, outs) if out_specs is None else out_specs,
        scratch_shapes=list(scratch),
        compiler_params=pltpu.CompilerParams(vmem_limit_bytes=limit * 1024 * 1024),
        cost_estimate=pl.CostEstimate(flops=flops, bytes_accessed=moved, transcendentals=0),
    )


def shape(dims, kind):
    return jax.ShapeDtypeStruct(dims, kind)


def pick_kernel(picked_hbm, residual_hbm, own_ref, other_ref, picked, table, sems):
    width, tokens = table.shape
    piece = own_ref.shape[0]
    pairs = ((residual_hbm, table), (picked_hbm, picked))
    copies = [pltpu.make_async_copy(a, b, sems.at[i]) for i, (a, b) in enumerate(pairs)]
    for copy in copies:
        copy.start()
    for copy in copies:
        copy.wait()
    core = lax.axis_index("core")
    place = lax.axis_index("x") * lax.axis_size("z") + lax.axis_index("z")
    row = lax.broadcasted_iota(jnp.int32, (piece, tokens), 0)
    token = lax.broadcasted_iota(jnp.int32, (piece, tokens), 1) + place * tokens
    columns = table[...]
    zeros = jnp.zeros_like(columns)

    def pick(start, columns):
        wanted = jnp.zeros((piece, tokens), jnp.int32)
        for i in range(piece):
            wanted = jnp.where(row == i, picked[start + i], wanted)
        hot = jnp.where(wanted == token, 1.0, 0.0).astype(BF16)
        return dot(hot, columns, ((1,), (1,))).astype(BF16)

    own_ref[...] = pick(core * piece, jnp.concatenate([columns, zeros], axis=0))
    other_ref[...] = pick((1 - core) * piece, jnp.concatenate([zeros, columns], axis=0))


def give(one_ref, copies_hbm, sems):
    copies = [
        pltpu.make_async_copy(one_ref, copies_hbm.at[i], sems.at[i])
        for i in range(copies_hbm.shape[0])
    ]
    for copy in copies:
        copy.start()
    for copy in copies:
        copy.wait()


def join_kernel(own_ref, got_ref, rows_ref, copies_hbm, sems):
    rows_ref[...] = own_ref[...] + got_ref[...]
    give(rows_ref, copies_hbm, sems)


def turn_kernel(value_ref, own_ref, other_ref):
    turned = value_ref[...].astype(F32).T
    width = own_ref.shape[0]
    own_ref[...] = turned[:width].astype(BF16)
    other_ref[...] = turned[width:].astype(BF16)


def spread(value, out_ref, first):
    share = value.shape[0] // out_ref.shape[0]
    for y in range(out_ref.shape[0]):
        for k in range(value.shape[1] // LANES):
            out_ref[y, pl.ds((first + k) * share, share), :] = value[
                y * share : (y + 1) * share, k * LANES : (k + 1) * LANES
            ]


def pre_kernel(centered_ref, enc_own, enc_other, squares_ref, out_ref, enc_ref):
    width, latents = enc_own.shape
    step = 2 * LANES
    squares = squares_ref[...]
    high = squares.astype(BF16).astype(F32)
    parts = jnp.concatenate([high, squares - high], axis=0).astype(BF16)
    for y in range(out_ref.shape[0]):
        out_ref[y, pl.ds(out_ref.shape[1] - parts.shape[0], parts.shape[0]), :] = parts
    for n in range(latents // step):
        lanes = pl.ds(n * step, step)
        enc_ref[:width, lanes] = enc_own[:, lanes]
        enc_ref[width:, lanes] = enc_other[:, lanes]
        part = dot(centered_ref[...], enc_ref[:, lanes], ((1,), (0,)))
        spread(part.astype(BF16), out_ref, 2 * n)


def sum_blocks(blocks_ref, size):
    total = blocks_ref[0, :size, :].astype(F32)
    for y in range(1, blocks_ref.shape[0]):
        total = total + blocks_ref[y, :size, :].astype(F32)
    return total


def sum_parts(blocks_ref, size):
    total = blocks_ref[0, size:, :].astype(F32)
    for y in range(1, blocks_ref.shape[0]):
        total = total + blocks_ref[y, size:, :].astype(F32)
    half = total.shape[0] // 2
    return total[:half] + total[half:]


def soft_parts(total, bias):
    value = SHARPNESS * (total + bias)
    small = jnp.exp(-jnp.abs(value))
    soft = jnp.maximum(value, 0.0) + jnp.log1p(small)
    return value, small, (soft / SHARPNESS).astype(BF16)


def act_kernel(blocks_ref, bias_ref, copies_hbm, one_ref, sems):
    size = copies_hbm.shape[1]
    share = size // bias_ref.shape[0]
    total = sum_blocks(blocks_ref, size)
    for k in range(bias_ref.shape[0]):
        lines = slice(k * share, (k + 1) * share)
        _, _, one_ref[lines, :] = soft_parts(total[lines], bias_ref[k : k + 1, :])
    give(one_ref, copies_hbm, sems)


def norms_of(blocks_ref, count):
    return jnp.sqrt(sum_parts(blocks_ref, blocks_ref.shape[1] - 2 * count) + 1e-06)


def unit_kernel(blocks_ref, dec_own, dec_other, unit_ref):
    width, latents = dec_own.shape
    norms = norms_of(blocks_ref, latents // LANES)
    for k in range(latents // LANES):
        lanes = pl.ds(k * LANES, LANES)
        norm = norms[k : k + 1]
        unit_ref[:width, lanes] = (dec_own[:, lanes].astype(F32) / norm).astype(BF16)
        unit_ref[width:, lanes] = (dec_other[:, lanes].astype(F32) / norm).astype(BF16)


def join_lanes(copies_ref, active_ref, share, k):
    for y in range(copies_ref.shape[0]):
        active_ref[y * share : (y + 1) * share, k * LANES : (k + 1) * LANES] = copies_ref[
            y, k * share : (k + 1) * share, :
        ]


def rebuild_kernel(copies_ref, unit_ref, out_ref, active_ref):
    count = unit_ref.shape[1] // LANES
    for k in range(count):
        join_lanes(copies_ref, active_ref, copies_ref.shape[1] // count, k)
    part = dot(active_ref[...], unit_ref[...], ((1,), (1,)))
    out_ref[...] = part.astype(BF16).reshape(out_ref.shape)


def keep_kernel(copies_ref, active_ref):
    count = active_ref.shape[1] // LANES
    for k in range(count):
        join_lanes(copies_ref, active_ref, copies_ref.shape[1] // count, k)


def error_kernel(blocks_ref, bias_ref, rows_ref, copies_ref):
    total = blocks_ref[0].astype(F32)
    for i in range(1, blocks_ref.shape[0]):
        total = total + blocks_ref[i].astype(F32)
    rebuilt = total + bias_ref[...]
    error = (2.0 / ROWS * (rebuilt - rows_ref[...].astype(F32))).astype(BF16)
    for i in range(copies_ref.shape[0]):
        copies_ref[i] = error


def raw_kernel(error_ref, unit_ref, out_ref):
    count = error_ref.shape[0] * error_ref.shape[1]
    error = error_ref[...].reshape(count, error_ref.shape[2])
    step = 2 * LANES
    for n in range(unit_ref.shape[1] // step):
        part = dot(error, unit_ref[:, n * step : (n + 1) * step], ((1,), (0,)))
        spread(part.astype(BF16), out_ref, 2 * n)


def grad_kernel(blocks_ref, pre_ref, bias_ref, copies_hbm, one_ref, sems):
    size = blocks_ref.shape[1]
    count = bias_ref.shape[0]
    share = size // count
    raw = sum_blocks(blocks_ref, size)
    pre = sum_blocks(pre_ref, size)
    row = lax.broadcasted_iota(jnp.int32, (count, LANES), 0)
    dots = jnp.zeros((count, LANES), F32)
    for k in range(count):
        lines = slice(k * share, (k + 1) * share)
        value, small, active = soft_parts(pre[lines], bias_ref[k : k + 1, :])
        gate = jnp.where(value >= 0.0, 1.0, small) / (1.0 + small)
        one_ref[lines, :] = ((raw[lines] + 1.0 / ROWS) * gate).astype(BF16)
        part = jnp.sum(active.astype(F32) * raw[lines], axis=0, keepdims=True)
        dots = jnp.where(row == k, part, dots)
    high = dots.astype(BF16).astype(F32)
    one_ref[size:] = jnp.concatenate([high, dots - high], axis=0).astype(BF16)
    give(one_ref, copies_hbm, sems)


def own_kernel(own_ref, centered_ref, blocks_ref, enc_ref, sums_ref, grad_ref):
    count = enc_ref.shape[1] // LANES
    size = own_ref.shape[1] - 2 * count
    share = size // count
    for k in range(count):
        cut = pl.ds(k * LANES, LANES)
        lines = pl.ds(k * share, share)
        total = jnp.zeros((share, LANES), F32)
        for y in range(own_ref.shape[0]):
            value = own_ref[y, lines, :]
            grad_ref[pl.ds(y * share, share), cut] = value
            total = total + value.astype(F32)
        sums_ref[k : k + 1, :] = jnp.sum(total, axis=0, keepdims=True)
    sums_ref[count : 2 * count] = sum_parts(own_ref, size)
    sums_ref[2 * count :] = 1.0 / norms_of(blocks_ref, count)
    enc_ref[...] = dot(centered_ref[...], grad_ref[...], ((1,), (0,)))


def last_kernel(
    its_ref, part_ref, sums_ref, centered_ref, product_ref, unit_ref,
    enc_out, bias_ref, dec_out,
    grad_ref, enc_ref, dec_ref, sems,
):
    count = enc_ref.shape[1] // LANES
    size = its_ref.shape[1] - 2 * count
    share = size // count
    dots = sums_ref[count : 2 * count] + sum_parts(its_ref, size)
    step = 2 * LANES
    copies = []
    for n in range(count // 2):
        lanes = pl.ds(n * step, step)
        for k in (2 * n, 2 * n + 1):
            cut = pl.ds(k * LANES, LANES)
            lines = pl.ds(k * share, share)
            ratio = sums_ref[2 * count + k : 2 * count + k + 1]
            dec_ref[:, cut] = (
                product_ref[:, cut] - unit_ref[:, cut].astype(F32) * dots[k : k + 1]
            ) * ratio
            total = jnp.zeros((share, LANES), F32)
            for y in range(its_ref.shape[0]):
                value = its_ref[y, lines, :]
                grad_ref[pl.ds(y * share, share), cut] = value
                total = total + value.astype(F32)
            bias_ref[k : k + 1, :] = sums_ref[k : k + 1, :] + jnp.sum(total, axis=0, keepdims=True)
        copies.append(pltpu.make_async_copy(dec_ref.at[:, lanes], dec_out.at[:, lanes], sems.at[2 * n]))
        copies[-1].start()
        enc_ref[:, lanes] = part_ref[:, lanes] + dot(
            centered_ref[...], grad_ref[:, lanes], ((1,), (0,))
        )
        copies.append(
            pltpu.make_async_copy(enc_ref.at[:, lanes], enc_out.at[:, lanes], sems.at[2 * n + 1])
        )
        copies[-1].start()
    for copy in copies:
        copy.wait()


def body(residual, picked, enc_weight, enc_bias, dec_weight, dec_bias):
    count_y = lax.axis_size("y")
    count_t = lax.axis_size(TENSOR)
    rows = ROWS // 2
    share = rows // count_y
    piece = rows // count_t
    width, latents = enc_weight.shape
    blocks_n = latents // LANES
    size = share * blocks_n
    extra = 2 * blocks_n
    wide = 2 * width
    matmul = 2 * rows * wide * latents
    moved = 3 << 20

    small = shape((piece, wide), BF16)
    own_rows, other_rows = call(
        pick_kernel,
        (small, small),
        [HBM] * 2,
        (1 << 20, 1 << 17),
        [
            pltpu.SMEM(picked.shape, jnp.int32),
            pltpu.VMEM(residual.shape[::-1], BF16),
            pltpu.SemaphoreType.DMA((2,)),
        ],
        limit=PICK,
    )(picked, residual.T)
    tensor_blocks = shape((count_t, piece, wide), BF16)
    local_rows, copies = call(
        join_kernel,
        (small, tensor_blocks),
        [VMEM] * 2,
        (1 << 12, 1 << 19),
        [pltpu.SemaphoreType.DMA((count_t,))],
        (VMEM, ANY),
    )(own_rows, swap(other_rows))
    sampled = exchange(copies, TENSOR)
    bias_all = jnp.concatenate([dec_bias[None], swap(dec_bias)[None]], axis=1)
    enc_other = swap(enc_weight)
    dec_own = dec_weight.T
    dec_other = swap(dec_own)
    squares = jnp.sum(jnp.square(dec_own.astype(F32)) + jnp.square(dec_other.astype(F32)), axis=0)
    centered = (sampled.reshape(rows, wide).astype(F32) - bias_all).astype(BF16)
    pre_blocks = call(
        pre_kernel,
        shape((count_y, size + extra, LANES), BF16),
        [VMEM] * 4,
        (matmul, moved),
        [pltpu.VMEM((wide, latents), BF16)],
    )(centered, enc_weight, enc_other, squares.reshape(blocks_n, LANES))
    blocks = exchange(pre_blocks, "y")
    enc_bias = enc_bias.reshape(blocks_n, LANES)
    copies = call(
        act_kernel,
        shape((count_y, size, LANES), BF16),
        [VMEM] * 2,
        (1 << 20, 1 << 20),
        [pltpu.VMEM((size, LANES), BF16), pltpu.SemaphoreType.DMA((count_y,))],
        ANY,
    )(blocks, enc_bias)
    unit = call(unit_kernel, shape((wide, latents), BF16), [VMEM] * 3, (1 << 20, moved))(
        blocks, dec_own, dec_other
    )
    copies = exchange(copies, "y")
    partial = call(
        rebuild_kernel,
        tensor_blocks,
        [VMEM] * 2,
        (matmul, moved),
        [pltpu.VMEM((rows, latents), BF16)],
    )(copies, unit)
    active = call(keep_kernel, shape((rows, latents), BF16), [VMEM], (1 << 20, 1 << 20))(copies)
    its_active = swap(active)
    turned = shape((width, rows), BF16)
    centered_own, centered_other = call(turn_kernel, (turned, turned), [VMEM], (1 << 20, 1 << 20))(
        centered
    )
    centered_its = swap(centered_other)
    errors = call(error_kernel, tensor_blocks, [VMEM] * 3, (1 << 20, 1 << 20))(
        exchange(partial, TENSOR), bias_all, local_rows
    )
    error = exchange(errors, TENSOR)
    raw_blocks = call(
        raw_kernel, shape((count_y, size, LANES), BF16), [VMEM] * 2, (matmul, moved)
    )(error, unit)
    err_grad = error.reshape(rows, wide)
    its_err = swap(err_grad[:, width:])
    product = dot(err_grad[:, :width], active, ((0,), (0,))) + dot(
        its_err, its_active, ((0,), (0,))
    )
    own = exchange(
        call(
            grad_kernel,
            shape((count_y, size + extra, LANES), BF16),
            [VMEM] * 3,
            (1 << 20, 1 << 20),
            [pltpu.VMEM((size + extra, LANES), BF16), pltpu.SemaphoreType.DMA((count_y,))],
            ANY,
        )(exchange(raw_blocks, "y"), blocks, enc_bias),
        "y",
    )
    its = swap(own)
    out = shape((width, latents), F32)
    enc_part, sums = call(
        own_kernel,
        (out, shape((3 * blocks_n, LANES), F32)),
        [VMEM] * 3,
        (40 * matmul, 20 * moved),
        [pltpu.VMEM((rows, latents), BF16)],
    )(own, centered_own, blocks)
    enc_grad, bias_grad, dec_grad = call(
        last_kernel,
        (out, shape((blocks_n, LANES), F32), out),
        [VMEM] * 6,
        (matmul, 2 * moved),
        [
            pltpu.VMEM((rows, latents), BF16),
            pltpu.VMEM((width, latents), F32),
            pltpu.VMEM((width, latents), F32),
            pltpu.SemaphoreType.DMA((blocks_n,)),
        ],
        (ANY, VMEM, ANY),
    )(its, enc_part, sums, centered_its, product, unit[:width])
    return (enc_grad, bias_grad.reshape(latents), dec_grad.T)


def solution(mesh):
    grid = Mesh(mesh.devices.reshape(8, 2, 4, 8), ("y", "core", "x", "z"))
    dp = ("y", "core")
    return jax.shard_map(
        body,
        mesh=grid,
        in_specs=(
            P(TENSOR, dp),
            P(TENSOR),
            P(dp, TENSOR),
            P(TENSOR),
            P(TENSOR, dp),
            P(dp),
        ),
        out_specs=(P(dp, TENSOR), P(TENSOR), P(TENSOR, dp)),
        check_vma=False,
    )
```

```python
import jax
import jax.numpy as jnp
from jax import lax
from jax.experimental import pallas as pl
from jax.experimental.pallas import tpu as pltpu
from jax.sharding import Mesh
from jax.sharding import PartitionSpec as P

ROWS = 512
LANES = 128
TENSOR = ("x", "z")
F32 = jnp.float32
BF16 = jnp.bfloat16
SHARPNESS = 8.0
VMEM = pl.BlockSpec(memory_space=pltpu.VMEM)
ANY = pl.BlockSpec(memory_space=pl.ANY)
HBM = pl.BlockSpec(memory_space=pltpu.HBM)


def exchange(blocks, axis):
    if axis == TENSOR:
        return lax.all_to_all(blocks, axis, 0, 0, tiled=False)
    count = lax.axis_size(axis)
    even = [2 * i for i in range(count)]
    odd = [2 * i + 1 for i in reversed(range(count))]
    return lax.all_to_all(
        blocks, (axis, "core"), 0, 0, tiled=False, axis_index_groups=[even, odd]
    )


def swap(block):
    return lax.ppermute(block, "core", [(0, 1), (1, 0)])


def dot(a, b, dims):
    return lax.dot_general(a, b, (dims, ((), ())), preferred_element_type=F32)


def call(kernel, outs, specs, cost, scratch=(), out_specs=None, limit=12):
    flops, moved = cost
    return pl.pallas_call(
        kernel,
        out_shape=outs,
        in_specs=specs,
        out_specs=jax.tree.map(lambda _: VMEM, outs) if out_specs is None else out_specs,
        scratch_shapes=list(scratch),
        compiler_params=pltpu.CompilerParams(vmem_limit_bytes=limit * 1024 * 1024),
        cost_estimate=pl.CostEstimate(flops=flops, bytes_accessed=moved, transcendentals=0),
    )


def shape(dims, kind):
    return jax.ShapeDtypeStruct(dims, kind)


def pick_kernel(picked_hbm, residual_hbm, own_ref, other_ref, picked, table, sems):
    width, tokens = table.shape
    piece = own_ref.shape[0]
    pairs = ((residual_hbm, table), (picked_hbm, picked))
    copies = [pltpu.make_async_copy(a, b, sems.at[i]) for i, (a, b) in enumerate(pairs)]
    for copy in copies:
        copy.start()
    for copy in copies:
        copy.wait()
    core = lax.axis_index("core")
    place = lax.axis_index("x") * lax.axis_size("z") + lax.axis_index("z")
    row = lax.broadcasted_iota(jnp.int32, (piece, tokens), 0)
    token = lax.broadcasted_iota(jnp.int32, (piece, tokens), 1) + place * tokens
    columns = table[...]
    zeros = jnp.zeros_like(columns)

    def pick(start, columns):
        wanted = jnp.zeros((piece, tokens), jnp.int32)
        for i in range(piece):
            wanted = jnp.where(row == i, picked[start + i], wanted)
        hot = jnp.where(wanted == token, 1.0, 0.0).astype(BF16)
        return dot(hot, columns, ((1,), (1,))).astype(BF16)

    own_ref[...] = pick(core * piece, jnp.concatenate([columns, zeros], axis=0))
    other_ref[...] = pick((1 - core) * piece, jnp.concatenate([zeros, columns], axis=0))


def join_kernel(own_ref, got_ref, rows_ref, copies_ref):
    rows = own_ref[...] + got_ref[...]
    rows_ref[...] = rows
    for i in range(copies_ref.shape[0]):
        copies_ref[i] = rows


def turn_kernel(value_ref, own_ref, other_ref):
    turned = value_ref[...].astype(F32).T
    width = own_ref.shape[0]
    own_ref[...] = turned[:width].astype(BF16)
    other_ref[...] = turned[width:].astype(BF16)


def spread(value, out_ref, first):
    share = value.shape[0] // out_ref.shape[0]
    for y in range(out_ref.shape[0]):
        for k in range(value.shape[1] // LANES):
            out_ref[y, pl.ds((first + k) * share, share), :] = value[
                y * share : (y + 1) * share, k * LANES : (k + 1) * LANES
            ]


def pre_kernel(centered_ref, enc_own, enc_other, squares_ref, out_ref, enc_ref):
    width, latents = enc_own.shape
    step = 2 * LANES
    squares = squares_ref[...]
    high = squares.astype(BF16).astype(F32)
    parts = jnp.concatenate([high, squares - high], axis=0).astype(BF16)
    for y in range(out_ref.shape[0]):
        out_ref[y, pl.ds(out_ref.shape[1] - parts.shape[0], parts.shape[0]), :] = parts
    for n in range(latents // step):
        lanes = pl.ds(n * step, step)
        enc_ref[:width, lanes] = enc_own[:, lanes]
        enc_ref[width:, lanes] = enc_other[:, lanes]
        part = dot(centered_ref[...], enc_ref[:, lanes], ((1,), (0,)))
        spread(part.astype(BF16), out_ref, 2 * n)


def sum_blocks(blocks_ref, size):
    total = blocks_ref[0, :size, :].astype(F32)
    for y in range(1, blocks_ref.shape[0]):
        total = total + blocks_ref[y, :size, :].astype(F32)
    return total


def sum_parts(blocks_ref, size):
    total = blocks_ref[0, size:, :].astype(F32)
    for y in range(1, blocks_ref.shape[0]):
        total = total + blocks_ref[y, size:, :].astype(F32)
    half = total.shape[0] // 2
    return total[:half] + total[half:]


def soft_parts(total, bias):
    value = SHARPNESS * (total + bias)
    small = jnp.exp(-jnp.abs(value))
    soft = jnp.maximum(value, 0.0) + jnp.log1p(small)
    return value, small, (soft / SHARPNESS).astype(BF16)


def act_kernel(blocks_ref, bias_ref, copies_ref):
    size = copies_ref.shape[1]
    share = size // bias_ref.shape[0]
    total = sum_blocks(blocks_ref, size)
    for k in range(bias_ref.shape[0]):
        lines = slice(k * share, (k + 1) * share)
        _, _, active = soft_parts(total[lines], bias_ref[k : k + 1, :])
        for y in range(copies_ref.shape[0]):
            copies_ref[y, lines, :] = active


def norms_of(blocks_ref, count):
    return jnp.sqrt(sum_parts(blocks_ref, blocks_ref.shape[1] - 2 * count) + 1e-06)


def unit_kernel(blocks_ref, dec_own, dec_other, unit_ref):
    width, latents = dec_own.shape
    norms = norms_of(blocks_ref, latents // LANES)
    for k in range(latents // LANES):
        lanes = pl.ds(k * LANES, LANES)
        norm = norms[k : k + 1]
        unit_ref[:width, lanes] = (dec_own[:, lanes].astype(F32) / norm).astype(BF16)
        unit_ref[width:, lanes] = (dec_other[:, lanes].astype(F32) / norm).astype(BF16)


def join_lanes(copies_ref, active_ref, share, k):
    for y in range(copies_ref.shape[0]):
        active_ref[y * share : (y + 1) * share, k * LANES : (k + 1) * LANES] = copies_ref[
            y, k * share : (k + 1) * share, :
        ]


def rebuild_kernel(copies_ref, unit_ref, out_ref, active_ref):
    count = unit_ref.shape[1] // LANES
    for k in range(count):
        join_lanes(copies_ref, active_ref, copies_ref.shape[1] // count, k)
    part = dot(active_ref[...], unit_ref[...], ((1,), (1,)))
    out_ref[...] = part.astype(BF16).reshape(out_ref.shape)


def keep_kernel(copies_ref, active_ref):
    count = active_ref.shape[1] // LANES
    for k in range(count):
        join_lanes(copies_ref, active_ref, copies_ref.shape[1] // count, k)


def error_kernel(blocks_ref, bias_ref, rows_ref, copies_ref):
    total = blocks_ref[0].astype(F32)
    for i in range(1, blocks_ref.shape[0]):
        total = total + blocks_ref[i].astype(F32)
    rebuilt = total + bias_ref[...]
    error = (2.0 / ROWS * (rebuilt - rows_ref[...].astype(F32))).astype(BF16)
    for i in range(copies_ref.shape[0]):
        copies_ref[i] = error


def raw_kernel(error_ref, unit_ref, out_ref):
    count = error_ref.shape[0] * error_ref.shape[1]
    error = error_ref[...].reshape(count, error_ref.shape[2])
    step = 2 * LANES
    for n in range(unit_ref.shape[1] // step):
        part = dot(error, unit_ref[:, n * step : (n + 1) * step], ((1,), (0,)))
        spread(part.astype(BF16), out_ref, 2 * n)


def grad_kernel(blocks_ref, pre_ref, bias_ref, copies_ref):
    size = blocks_ref.shape[1]
    count = bias_ref.shape[0]
    share = size // count
    raw = sum_blocks(blocks_ref, size)
    pre = sum_blocks(pre_ref, size)
    row = lax.broadcasted_iota(jnp.int32, (count, LANES), 0)
    dots = jnp.zeros((count, LANES), F32)
    for k in range(count):
        lines = slice(k * share, (k + 1) * share)
        value, small, active = soft_parts(pre[lines], bias_ref[k : k + 1, :])
        gate = jnp.where(value >= 0.0, 1.0, small) / (1.0 + small)
        grad = ((raw[lines] + 1.0 / ROWS) * gate).astype(BF16)
        for y in range(copies_ref.shape[0]):
            copies_ref[y, lines, :] = grad
        part = jnp.sum(active.astype(F32) * raw[lines], axis=0, keepdims=True)
        dots = jnp.where(row == k, part, dots)
    high = dots.astype(BF16).astype(F32)
    parts = jnp.concatenate([high, dots - high], axis=0).astype(BF16)
    for y in range(copies_ref.shape[0]):
        copies_ref[y, size:, :] = parts


def own_kernel(own_ref, centered_ref, blocks_ref, enc_ref, sums_ref, grad_ref):
    count = enc_ref.shape[1] // LANES
    size = own_ref.shape[1] - 2 * count
    share = size // count
    for k in range(count):
        cut = pl.ds(k * LANES, LANES)
        lines = pl.ds(k * share, share)
        total = jnp.zeros((share, LANES), F32)
        for y in range(own_ref.shape[0]):
            value = own_ref[y, lines, :]
            grad_ref[pl.ds(y * share, share), cut] = value
            total = total + value.astype(F32)
        sums_ref[k : k + 1, :] = jnp.sum(total, axis=0, keepdims=True)
    sums_ref[count : 2 * count] = sum_parts(own_ref, size)
    sums_ref[2 * count :] = 1.0 / norms_of(blocks_ref, count)
    enc_ref[...] = dot(centered_ref[...], grad_ref[...], ((1,), (0,)))


def last_kernel(
    its_ref, part_ref, sums_ref, centered_ref, product_ref, unit_ref,
    enc_out, bias_ref, dec_out,
    grad_ref, enc_ref, dec_ref, sems,
):
    count = enc_ref.shape[1] // LANES
    size = its_ref.shape[1] - 2 * count
    share = size // count
    dots = sums_ref[count : 2 * count] + sum_parts(its_ref, size)
    step = 2 * LANES
    copies = []
    for n in range(count // 2):
        lanes = pl.ds(n * step, step)
        for k in (2 * n, 2 * n + 1):
            cut = pl.ds(k * LANES, LANES)
            lines = pl.ds(k * share, share)
            ratio = sums_ref[2 * count + k : 2 * count + k + 1]
            dec_ref[:, cut] = (
                product_ref[:, cut] - unit_ref[:, cut].astype(F32) * dots[k : k + 1]
            ) * ratio
            total = jnp.zeros((share, LANES), F32)
            for y in range(its_ref.shape[0]):
                value = its_ref[y, lines, :]
                grad_ref[pl.ds(y * share, share), cut] = value
                total = total + value.astype(F32)
            bias_ref[k : k + 1, :] = sums_ref[k : k + 1, :] + jnp.sum(total, axis=0, keepdims=True)
        copies.append(pltpu.make_async_copy(dec_ref.at[:, lanes], dec_out.at[:, lanes], sems.at[2 * n]))
        copies[-1].start()
        enc_ref[:, lanes] = part_ref[:, lanes] + dot(
            centered_ref[...], grad_ref[:, lanes], ((1,), (0,))
        )
        copies.append(
            pltpu.make_async_copy(enc_ref.at[:, lanes], enc_out.at[:, lanes], sems.at[2 * n + 1])
        )
        copies[-1].start()
    for copy in copies:
        copy.wait()


def body(residual, picked, enc_weight, enc_bias, dec_weight, dec_bias):
    count_y = lax.axis_size("y")
    count_t = lax.axis_size(TENSOR)
    rows = ROWS // 2
    share = rows // count_y
    piece = rows // count_t
    width, latents = enc_weight.shape
    blocks_n = latents // LANES
    size = share * blocks_n
    extra = 2 * blocks_n
    wide = 2 * width
    matmul = 2 * rows * wide * latents
    moved = 3 << 20

    small = shape((piece, wide), BF16)
    own_rows, other_rows = call(
        pick_kernel,
        (small, small),
        [HBM] * 2,
        (1 << 20, 1 << 17),
        [
            pltpu.SMEM(picked.shape, jnp.int32),
            pltpu.VMEM(residual.shape[::-1], BF16),
            pltpu.SemaphoreType.DMA((2,)),
        ],
    )(picked, residual.T)
    tensor_blocks = shape((count_t, piece, wide), BF16)
    local_rows, copies = call(join_kernel, (small, tensor_blocks), [VMEM] * 2, (1 << 12, 1 << 19))(
        own_rows, swap(other_rows)
    )
    sampled = exchange(copies, TENSOR)
    bias_all = jnp.concatenate([dec_bias[None], swap(dec_bias)[None]], axis=1)
    enc_other = swap(enc_weight)
    dec_own = dec_weight.T
    dec_other = swap(dec_own)
    squares = jnp.sum(jnp.square(dec_own.astype(F32)) + jnp.square(dec_other.astype(F32)), axis=0)
    centered = (sampled.reshape(rows, wide).astype(F32) - bias_all).astype(BF16)
    pre_blocks = call(
        pre_kernel,
        shape((count_y, size + extra, LANES), BF16),
        [VMEM] * 4,
        (matmul, moved),
        [pltpu.VMEM((wide, latents), BF16)],
    )(centered, enc_weight, enc_other, squares.reshape(blocks_n, LANES))
    blocks = exchange(pre_blocks, "y")
    enc_bias = enc_bias.reshape(blocks_n, LANES)
    copies = call(
        act_kernel, shape((count_y, size, LANES), BF16), [VMEM] * 2, (1 << 20, 1 << 20)
    )(blocks, enc_bias)
    unit = call(unit_kernel, shape((wide, latents), BF16), [VMEM] * 3, (1 << 20, moved))(
        blocks, dec_own, dec_other
    )
    copies = exchange(copies, "y")
    partial = call(
        rebuild_kernel,
        tensor_blocks,
        [VMEM] * 2,
        (matmul, moved),
        [pltpu.VMEM((rows, latents), BF16)],
    )(copies, unit)
    active = call(keep_kernel, shape((rows, latents), BF16), [VMEM], (1 << 20, 1 << 20))(copies)
    its_active = swap(active)
    turned = shape((width, rows), BF16)
    centered_own, centered_other = call(turn_kernel, (turned, turned), [VMEM], (1 << 20, 1 << 20))(
        centered
    )
    centered_its = swap(centered_other)
    errors = call(error_kernel, tensor_blocks, [VMEM] * 3, (1 << 20, 1 << 20))(
        exchange(partial, TENSOR), bias_all, local_rows
    )
    error = exchange(errors, TENSOR)
    raw_blocks = call(
        raw_kernel, shape((count_y, size, LANES), BF16), [VMEM] * 2, (matmul, moved)
    )(error, unit)
    err_grad = error.reshape(rows, wide)
    its_err = swap(err_grad[:, width:])
    product = dot(err_grad[:, :width], active, ((0,), (0,))) + dot(
        its_err, its_active, ((0,), (0,))
    )
    own = exchange(
        call(
            grad_kernel,
            shape((count_y, size + extra, LANES), BF16),
            [VMEM] * 3,
            (1 << 20, 1 << 20),
        )(exchange(raw_blocks, "y"), blocks, enc_bias),
        "y",
    )
    its = swap(own)
    out = shape((width, latents), F32)
    enc_part, sums = call(
        own_kernel,
        (out, shape((3 * blocks_n, LANES), F32)),
        [VMEM] * 3,
        (40 * matmul, 20 * moved),
        [pltpu.VMEM((rows, latents), BF16)],
    )(own, centered_own, blocks)
    enc_grad, bias_grad, dec_grad = call(
        last_kernel,
        (out, shape((blocks_n, LANES), F32), out),
        [VMEM] * 6,
        (matmul, 2 * moved),
        [
            pltpu.VMEM((rows, latents), BF16),
            pltpu.VMEM((width, latents), F32),
            pltpu.VMEM((width, latents), F32),
            pltpu.SemaphoreType.DMA((blocks_n,)),
        ],
        (ANY, VMEM, ANY),
    )(its, enc_part, sums, centered_its, product, unit[:width])
    return (enc_grad, bias_grad.reshape(latents), dec_grad.T)


def solution(mesh):
    grid = Mesh(mesh.devices.reshape(8, 2, 4, 8), ("y", "core", "x", "z"))
    dp = ("y", "core")
    return jax.shard_map(
        body,
        mesh=grid,
        in_specs=(
            P(TENSOR, dp),
            P(TENSOR),
            P(dp, TENSOR),
            P(TENSOR),
            P(TENSOR, dp),
            P(dp),
        ),
        out_specs=(P(dp, TENSOR), P(TENSOR), P(TENSOR, dp)),
        check_vma=False,
    )
```

```python
import jax
import jax.numpy as jnp
from jax import lax
from jax.experimental import pallas as pl
from jax.experimental.pallas import tpu as pltpu
from jax.sharding import Mesh
from jax.sharding import PartitionSpec as P

ROWS = 512
LANES = 128
TENSOR = ("x", "z")
F32 = jnp.float32
BF16 = jnp.bfloat16
SHARPNESS = 8.0
VMEM = pl.BlockSpec(memory_space=pltpu.VMEM)
ANY = pl.BlockSpec(memory_space=pl.ANY)
HBM = pl.BlockSpec(memory_space=pltpu.HBM)


def exchange(blocks, axis):
    return lax.all_to_all(blocks, axis, 0, 0, tiled=False)


def swap(block):
    return lax.ppermute(block, "core", [(0, 1), (1, 0)])


def dot(a, b, dims):
    return lax.dot_general(a, b, (dims, ((), ())), preferred_element_type=F32)


def call(kernel, outs, specs, cost, scratch=(), out_specs=None, limit=12):
    flops, moved = cost
    return pl.pallas_call(
        kernel,
        out_shape=outs,
        in_specs=specs,
        out_specs=jax.tree.map(lambda _: VMEM, outs) if out_specs is None else out_specs,
        scratch_shapes=list(scratch),
        compiler_params=pltpu.CompilerParams(vmem_limit_bytes=limit * 1024 * 1024),
        cost_estimate=pl.CostEstimate(flops=flops, bytes_accessed=moved, transcendentals=0),
    )


def shape(dims, kind):
    return jax.ShapeDtypeStruct(dims, kind)


def pick_kernel(picked_hbm, residual_hbm, own_ref, other_ref, picked, table, sems):
    width, tokens = table.shape
    piece = own_ref.shape[0]
    pairs = ((residual_hbm, table), (picked_hbm, picked))
    copies = [pltpu.make_async_copy(a, b, sems.at[i]) for i, (a, b) in enumerate(pairs)]
    for copy in copies:
        copy.start()
    for copy in copies:
        copy.wait()
    core = lax.axis_index("core")
    place = lax.axis_index("x") * lax.axis_size("z") + lax.axis_index("z")
    row = lax.broadcasted_iota(jnp.int32, (piece, tokens), 0)
    token = lax.broadcasted_iota(jnp.int32, (piece, tokens), 1) + place * tokens
    columns = table[...]
    zeros = jnp.zeros_like(columns)

    def pick(start, columns):
        wanted = jnp.zeros((piece, tokens), jnp.int32)
        for i in range(piece):
            wanted = jnp.where(row == i, picked[start + i], wanted)
        hot = jnp.where(wanted == token, 1.0, 0.0).astype(BF16)
        return dot(hot, columns, ((1,), (1,))).astype(BF16)

    own_ref[...] = pick(core * piece, jnp.concatenate([columns, zeros], axis=0))
    other_ref[...] = pick((1 - core) * piece, jnp.concatenate([zeros, columns], axis=0))


def join_kernel(own_ref, got_ref, rows_ref, copies_ref):
    rows = own_ref[...] + got_ref[...]
    rows_ref[...] = rows
    for i in range(copies_ref.shape[0]):
        copies_ref[i] = rows


def turn_kernel(value_ref, own_ref, other_ref):
    turned = value_ref[...].astype(F32).T
    width = own_ref.shape[0]
    own_ref[...] = turned[:width].astype(BF16)
    other_ref[...] = turned[width:].astype(BF16)


def spread(value, out_ref, first):
    share = value.shape[0] // out_ref.shape[0]
    for y in range(out_ref.shape[0]):
        for k in range(value.shape[1] // LANES):
            out_ref[y, pl.ds((first + k) * share, share), :] = value[
                y * share : (y + 1) * share, k * LANES : (k + 1) * LANES
            ]


def pre_kernel(centered_ref, enc_own, enc_other, squares_ref, out_ref, enc_ref):
    width, latents = enc_own.shape
    step = 2 * LANES
    squares = squares_ref[...]
    high = squares.astype(BF16).astype(F32)
    parts = jnp.concatenate([high, squares - high], axis=0).astype(BF16)
    for y in range(out_ref.shape[0]):
        out_ref[y, pl.ds(out_ref.shape[1] - parts.shape[0], parts.shape[0]), :] = parts
    for n in range(latents // step):
        lanes = pl.ds(n * step, step)
        enc_ref[:width, lanes] = enc_own[:, lanes]
        enc_ref[width:, lanes] = enc_other[:, lanes]
        part = dot(centered_ref[...], enc_ref[:, lanes], ((1,), (0,)))
        spread(part.astype(BF16), out_ref, 2 * n)


def sum_blocks(blocks_ref, size):
    total = blocks_ref[0, :size, :].astype(F32)
    for y in range(1, blocks_ref.shape[0]):
        total = total + blocks_ref[y, :size, :].astype(F32)
    return total


def sum_parts(blocks_ref, size):
    total = blocks_ref[0, size:, :].astype(F32)
    for y in range(1, blocks_ref.shape[0]):
        total = total + blocks_ref[y, size:, :].astype(F32)
    half = total.shape[0] // 2
    return total[:half] + total[half:]


def soft_parts(total, bias):
    value = SHARPNESS * (total + bias)
    small = jnp.exp(-jnp.abs(value))
    soft = jnp.maximum(value, 0.0) + jnp.log1p(small)
    return value, small, (soft / SHARPNESS).astype(BF16)


def act_kernel(blocks_ref, bias_ref, copies_ref):
    size = copies_ref.shape[1]
    share = size // bias_ref.shape[0]
    total = sum_blocks(blocks_ref, size)
    for k in range(bias_ref.shape[0]):
        lines = slice(k * share, (k + 1) * share)
        _, _, active = soft_parts(total[lines], bias_ref[k : k + 1, :])
        for y in range(copies_ref.shape[0]):
            copies_ref[y, lines, :] = active


def norms_of(blocks_ref, count):
    return jnp.sqrt(sum_parts(blocks_ref, blocks_ref.shape[1] - 2 * count) + 1e-06)


def unit_kernel(blocks_ref, dec_own, dec_other, unit_ref):
    width, latents = dec_own.shape
    norms = norms_of(blocks_ref, latents // LANES)
    for k in range(latents // LANES):
        lanes = pl.ds(k * LANES, LANES)
        norm = norms[k : k + 1]
        unit_ref[:width, lanes] = (dec_own[:, lanes].astype(F32) / norm).astype(BF16)
        unit_ref[width:, lanes] = (dec_other[:, lanes].astype(F32) / norm).astype(BF16)


def join_lanes(copies_ref, active_ref, share, k):
    for y in range(copies_ref.shape[0]):
        active_ref[y * share : (y + 1) * share, k * LANES : (k + 1) * LANES] = copies_ref[
            y, k * share : (k + 1) * share, :
        ]


def rebuild_kernel(copies_ref, unit_ref, out_ref, active_ref):
    count = unit_ref.shape[1] // LANES
    for k in range(count):
        join_lanes(copies_ref, active_ref, copies_ref.shape[1] // count, k)
    part = dot(active_ref[...], unit_ref[...], ((1,), (1,)))
    out_ref[...] = part.astype(BF16).reshape(out_ref.shape)


def keep_kernel(copies_ref, active_ref):
    count = active_ref.shape[1] // LANES
    for k in range(count):
        join_lanes(copies_ref, active_ref, copies_ref.shape[1] // count, k)


def error_kernel(blocks_ref, bias_ref, rows_ref, copies_ref):
    total = blocks_ref[0].astype(F32)
    for i in range(1, blocks_ref.shape[0]):
        total = total + blocks_ref[i].astype(F32)
    rebuilt = total + bias_ref[...]
    error = (2.0 / ROWS * (rebuilt - rows_ref[...].astype(F32))).astype(BF16)
    for i in range(copies_ref.shape[0]):
        copies_ref[i] = error


def raw_kernel(error_ref, unit_ref, out_ref):
    count = error_ref.shape[0] * error_ref.shape[1]
    error = error_ref[...].reshape(count, error_ref.shape[2])
    step = 2 * LANES
    for n in range(unit_ref.shape[1] // step):
        part = dot(error, unit_ref[:, n * step : (n + 1) * step], ((1,), (0,)))
        spread(part.astype(BF16), out_ref, 2 * n)


def grad_kernel(blocks_ref, pre_ref, bias_ref, copies_ref):
    size = blocks_ref.shape[1]
    count = bias_ref.shape[0]
    share = size // count
    raw = sum_blocks(blocks_ref, size)
    pre = sum_blocks(pre_ref, size)
    row = lax.broadcasted_iota(jnp.int32, (count, LANES), 0)
    dots = jnp.zeros((count, LANES), F32)
    for k in range(count):
        lines = slice(k * share, (k + 1) * share)
        value, small, active = soft_parts(pre[lines], bias_ref[k : k + 1, :])
        gate = jnp.where(value >= 0.0, 1.0, small) / (1.0 + small)
        grad = ((raw[lines] + 1.0 / ROWS) * gate).astype(BF16)
        for y in range(copies_ref.shape[0]):
            copies_ref[y, lines, :] = grad
        part = jnp.sum(active.astype(F32) * raw[lines], axis=0, keepdims=True)
        dots = jnp.where(row == k, part, dots)
    high = dots.astype(BF16).astype(F32)
    parts = jnp.concatenate([high, dots - high], axis=0).astype(BF16)
    for y in range(copies_ref.shape[0]):
        copies_ref[y, size:, :] = parts


def own_kernel(own_ref, centered_ref, blocks_ref, enc_ref, sums_ref, grad_ref):
    count = enc_ref.shape[1] // LANES
    size = own_ref.shape[1] - 2 * count
    share = size // count
    for k in range(count):
        cut = pl.ds(k * LANES, LANES)
        lines = pl.ds(k * share, share)
        total = jnp.zeros((share, LANES), F32)
        for y in range(own_ref.shape[0]):
            value = own_ref[y, lines, :]
            grad_ref[pl.ds(y * share, share), cut] = value
            total = total + value.astype(F32)
        sums_ref[k : k + 1, :] = jnp.sum(total, axis=0, keepdims=True)
    sums_ref[count : 2 * count] = sum_parts(own_ref, size)
    sums_ref[2 * count :] = 1.0 / norms_of(blocks_ref, count)
    enc_ref[...] = dot(centered_ref[...], grad_ref[...], ((1,), (0,)))


def last_kernel(
    its_ref, part_ref, sums_ref, centered_ref, product_ref, unit_ref,
    enc_out, bias_out, dec_out,
    grad_ref, enc_ref, dec_ref, bias_ref, sems,
):
    count = enc_ref.shape[1] // LANES
    size = its_ref.shape[1] - 2 * count
    share = size // count
    dots = sums_ref[count : 2 * count] + sum_parts(its_ref, size)
    step = 2 * LANES
    pieces = count // 2
    copies = []

    def send(source, target, sem):
        copies.append(pltpu.make_async_copy(source, target, sems.at[sem]))
        copies[-1].start()

    for n in range(pieces):
        lanes = pl.ds(n * step, step)
        for k in (2 * n, 2 * n + 1):
            cut = pl.ds(k * LANES, LANES)
            ratio = sums_ref[2 * count + k : 2 * count + k + 1]
            dec_ref[:, cut] = (
                product_ref[:, cut] - unit_ref[:, cut].astype(F32) * dots[k : k + 1]
            ) * ratio
        send(dec_ref.at[:, lanes], dec_out.at[:, lanes], n)
    for k in range(count):
        lines = pl.ds(k * share, share)
        total = jnp.zeros((share, LANES), F32)
        for y in range(its_ref.shape[0]):
            value = its_ref[y, lines, :]
            grad_ref[pl.ds(y * share, share), pl.ds(k * LANES, LANES)] = value
            total = total + value.astype(F32)
        bias_ref[k : k + 1, :] = sums_ref[k : k + 1, :] + jnp.sum(total, axis=0, keepdims=True)
    send(bias_ref, bias_out, 2 * pieces)
    for n in range(pieces):
        lanes = pl.ds(n * step, step)
        enc_ref[:, lanes] = part_ref[:, lanes] + dot(
            centered_ref[...], grad_ref[:, lanes], ((1,), (0,))
        )
        send(enc_ref.at[:, lanes], enc_out.at[:, lanes], pieces + n)
    for copy in copies:
        copy.wait()


def body(residual, picked, enc_weight, enc_bias, dec_weight, dec_bias):
    count_y = lax.axis_size("y")
    count_t = lax.axis_size(TENSOR)
    rows = ROWS // 2
    share = rows // count_y
    piece = rows // count_t
    width, latents = enc_weight.shape
    blocks_n = latents // LANES
    size = share * blocks_n
    extra = 2 * blocks_n
    wide = 2 * width
    matmul = 2 * rows * wide * latents
    moved = 3 << 20

    small = shape((piece, wide), BF16)
    own_rows, other_rows = call(
        pick_kernel,
        (small, small),
        [HBM] * 2,
        (1 << 20, 1 << 17),
        [
            pltpu.SMEM(picked.shape, jnp.int32),
            pltpu.VMEM(residual.shape[::-1], BF16),
            pltpu.SemaphoreType.DMA((2,)),
        ],
    )(picked, residual.T)
    tensor_blocks = shape((count_t, piece, wide), BF16)
    local_rows, copies = call(join_kernel, (small, tensor_blocks), [VMEM] * 2, (1 << 12, 1 << 19))(
        own_rows, swap(other_rows)
    )
    sampled = exchange(copies, TENSOR)
    bias_all = jnp.concatenate([dec_bias[None], swap(dec_bias)[None]], axis=1)
    enc_other = swap(enc_weight)
    dec_own = dec_weight.T
    dec_other = swap(dec_own)
    squares = jnp.sum(jnp.square(dec_own.astype(F32)) + jnp.square(dec_other.astype(F32)), axis=0)
    centered = (sampled.reshape(rows, wide).astype(F32) - bias_all).astype(BF16)
    pre_blocks = call(
        pre_kernel,
        shape((count_y, size + extra, LANES), BF16),
        [VMEM] * 4,
        (matmul, moved),
        [pltpu.VMEM((wide, latents), BF16)],
    )(centered, enc_weight, enc_other, squares.reshape(blocks_n, LANES))
    blocks = exchange(pre_blocks, "y")
    enc_bias = enc_bias.reshape(blocks_n, LANES)
    copies = call(
        act_kernel, shape((count_y, size, LANES), BF16), [VMEM] * 2, (1 << 20, 1 << 20)
    )(blocks, enc_bias)
    unit = call(unit_kernel, shape((wide, latents), BF16), [VMEM] * 3, (1 << 20, moved))(
        blocks, dec_own, dec_other
    )
    copies = exchange(copies, "y")
    partial = call(
        rebuild_kernel,
        tensor_blocks,
        [VMEM] * 2,
        (matmul, moved),
        [pltpu.VMEM((rows, latents), BF16)],
    )(copies, unit)
    active = call(keep_kernel, shape((rows, latents), BF16), [VMEM], (1 << 20, 1 << 20))(copies)
    its_active = swap(active)
    turned = shape((width, rows), BF16)
    centered_own, centered_other = call(turn_kernel, (turned, turned), [VMEM], (1 << 20, 1 << 20))(
        centered
    )
    centered_its = swap(centered_other)
    errors = call(error_kernel, tensor_blocks, [VMEM] * 3, (1 << 20, 1 << 20))(
        exchange(partial, TENSOR), bias_all, local_rows
    )
    error = exchange(errors, TENSOR)
    raw_blocks = call(
        raw_kernel, shape((count_y, size, LANES), BF16), [VMEM] * 2, (matmul, moved)
    )(error, unit)
    err_grad = error.reshape(rows, wide)
    its_err = swap(err_grad[:, width:])
    product = dot(err_grad[:, :width], active, ((0,), (0,))) + dot(
        its_err, its_active, ((0,), (0,))
    )
    own = exchange(
        call(
            grad_kernel,
            shape((count_y, size + extra, LANES), BF16),
            [VMEM] * 3,
            (1 << 20, 1 << 20),
        )(exchange(raw_blocks, "y"), blocks, enc_bias),
        "y",
    )
    its = swap(own)
    out = shape((width, latents), F32)
    enc_part, sums = call(
        own_kernel,
        (out, shape((3 * blocks_n, LANES), F32)),
        [VMEM] * 3,
        (40 * matmul, 20 * moved),
        [pltpu.VMEM((rows, latents), BF16)],
    )(own, centered_own, blocks)
    enc_grad, bias_grad, dec_grad = call(
        last_kernel,
        (out, shape((blocks_n, LANES), F32), out),
        [VMEM] * 6,
        (matmul, 2 * moved),
        [
            pltpu.VMEM((rows, latents), BF16),
            pltpu.VMEM((width, latents), F32),
            pltpu.VMEM((width, latents), F32),
            pltpu.VMEM((blocks_n, LANES), F32),
            pltpu.SemaphoreType.DMA((blocks_n + 1,)),
        ],
        (ANY, ANY, ANY),
    )(its, enc_part, sums, centered_its, product, unit[:width])
    return (enc_grad, bias_grad.reshape(latents), dec_grad.T)


def solution(mesh):
    grid = Mesh(mesh.devices.reshape(8, 2, 4, 8), ("y", "core", "x", "z"))
    dp = ("y", "core")
    return jax.shard_map(
        body,
        mesh=grid,
        in_specs=(
            P(TENSOR, dp),
            P(TENSOR),
            P(dp, TENSOR),
            P(TENSOR),
            P(TENSOR, dp),
            P(dp),
        ),
        out_specs=(P(dp, TENSOR), P(TENSOR), P(TENSOR, dp)),
        check_vma=False,
    )
```

```python
import jax
import jax.numpy as jnp
from jax import lax
from jax.experimental import pallas as pl
from jax.experimental.pallas import tpu as pltpu
from jax.sharding import Mesh
from jax.sharding import PartitionSpec as P

ROWS = 512
LANES = 128
TENSOR = ("x", "z")
F32 = jnp.float32
BF16 = jnp.bfloat16
SHARPNESS = 8.0
VMEM = pl.BlockSpec(memory_space=pltpu.VMEM)
ANY = pl.BlockSpec(memory_space=pl.ANY)
HBM = pl.BlockSpec(memory_space=pltpu.HBM)


def exchange(blocks, axis):
    return lax.all_to_all(blocks, axis, 0, 0, tiled=False)


def swap(block):
    return lax.ppermute(block, "core", [(0, 1), (1, 0)])


def dot(a, b, dims):
    return lax.dot_general(a, b, (dims, ((), ())), preferred_element_type=F32)


def call(kernel, outs, specs, cost, scratch=(), out_specs=None, limit=12):
    flops, moved = cost
    return pl.pallas_call(
        kernel,
        out_shape=outs,
        in_specs=specs,
        out_specs=jax.tree.map(lambda _: VMEM, outs) if out_specs is None else out_specs,
        scratch_shapes=list(scratch),
        compiler_params=pltpu.CompilerParams(vmem_limit_bytes=limit * 1024 * 1024),
        cost_estimate=pl.CostEstimate(flops=flops, bytes_accessed=moved, transcendentals=0),
    )


def shape(dims, kind):
    return jax.ShapeDtypeStruct(dims, kind)


def pick_kernel(picked_hbm, residual_hbm, own_ref, other_ref, picked, table, sems):
    width, tokens = table.shape
    piece = own_ref.shape[0]
    pairs = ((residual_hbm, table), (picked_hbm, picked))
    copies = [pltpu.make_async_copy(a, b, sems.at[i]) for i, (a, b) in enumerate(pairs)]
    for copy in copies:
        copy.start()
    for copy in copies:
        copy.wait()
    core = lax.axis_index("core")
    place = lax.axis_index("x") * lax.axis_size("z") + lax.axis_index("z")
    row = lax.broadcasted_iota(jnp.int32, (piece, tokens), 0)
    token = lax.broadcasted_iota(jnp.int32, (piece, tokens), 1) + place * tokens
    columns = table[...]
    zeros = jnp.zeros_like(columns)

    def pick(start, columns):
        wanted = jnp.zeros((piece, tokens), jnp.int32)
        for i in range(piece):
            wanted = jnp.where(row == i, picked[start + i], wanted)
        hot = jnp.where(wanted == token, 1.0, 0.0).astype(BF16)
        return dot(hot, columns, ((1,), (1,))).astype(BF16)

    own_ref[...] = pick(core * piece, jnp.concatenate([columns, zeros], axis=0))
    other_ref[...] = pick((1 - core) * piece, jnp.concatenate([zeros, columns], axis=0))


def join_kernel(own_ref, got_ref, rows_ref, copies_ref):
    rows = own_ref[...] + got_ref[...]
    rows_ref[...] = rows
    for i in range(copies_ref.shape[0]):
        copies_ref[i] = rows


def turn_kernel(value_ref, own_ref, other_ref):
    turned = value_ref[...].astype(F32).T
    width = own_ref.shape[0]
    own_ref[...] = turned[:width].astype(BF16)
    other_ref[...] = turned[width:].astype(BF16)


def spread(value, out_ref, first):
    share = value.shape[0] // out_ref.shape[0]
    for y in range(out_ref.shape[0]):
        for k in range(value.shape[1] // LANES):
            out_ref[y, pl.ds((first + k) * share, share), :] = value[
                y * share : (y + 1) * share, k * LANES : (k + 1) * LANES
            ]


def pre_kernel(centered_ref, enc_own, enc_other, squares_ref, out_ref, enc_ref):
    width, latents = enc_own.shape
    step = 2 * LANES
    squares = squares_ref[...]
    high = squares.astype(BF16).astype(F32)
    parts = jnp.concatenate([high, squares - high], axis=0).astype(BF16)
    for y in range(out_ref.shape[0]):
        out_ref[y, pl.ds(out_ref.shape[1] - parts.shape[0], parts.shape[0]), :] = parts
    for n in range(latents // step):
        lanes = pl.ds(n * step, step)
        enc_ref[:width, lanes] = enc_own[:, lanes]
        enc_ref[width:, lanes] = enc_other[:, lanes]
        part = dot(centered_ref[...], enc_ref[:, lanes], ((1,), (0,)))
        spread(part.astype(BF16), out_ref, 2 * n)


def sum_blocks(blocks_ref, size):
    total = blocks_ref[0, :size, :].astype(F32)
    for y in range(1, blocks_ref.shape[0]):
        total = total + blocks_ref[y, :size, :].astype(F32)
    return total


def sum_parts(blocks_ref, size):
    total = blocks_ref[0, size:, :].astype(F32)
    for y in range(1, blocks_ref.shape[0]):
        total = total + blocks_ref[y, size:, :].astype(F32)
    half = total.shape[0] // 2
    return total[:half] + total[half:]


def soft_parts(total, bias):
    value = SHARPNESS * (total + bias)
    small = jnp.exp(-jnp.abs(value))
    soft = jnp.maximum(value, 0.0) + jnp.log1p(small)
    return value, small, (soft / SHARPNESS).astype(BF16)


def act_kernel(blocks_ref, bias_ref, copies_ref):
    size = copies_ref.shape[1]
    share = size // bias_ref.shape[0]
    total = sum_blocks(blocks_ref, size)
    for k in range(bias_ref.shape[0]):
        lines = slice(k * share, (k + 1) * share)
        _, _, active = soft_parts(total[lines], bias_ref[k : k + 1, :])
        for y in range(copies_ref.shape[0]):
            copies_ref[y, lines, :] = active


def norms_of(blocks_ref, count):
    return jnp.sqrt(sum_parts(blocks_ref, blocks_ref.shape[1] - 2 * count) + 1e-06)


def unit_kernel(blocks_ref, dec_own, dec_other, bias_ref, unit_ref, active_ref, gate_ref):
    width, latents = dec_own.shape
    size = active_ref.shape[0]
    share = size // bias_ref.shape[0]
    total = sum_blocks(blocks_ref, size)
    for k in range(bias_ref.shape[0]):
        lines = slice(k * share, (k + 1) * share)
        value, small, active = soft_parts(total[lines], bias_ref[k : k + 1, :])
        active_ref[lines, :] = active
        gate_ref[lines, :] = jnp.where(value >= 0.0, 1.0, small) / (1.0 + small)
    norms = norms_of(blocks_ref, latents // LANES)
    for k in range(latents // LANES):
        lanes = pl.ds(k * LANES, LANES)
        norm = norms[k : k + 1]
        unit_ref[:width, lanes] = (dec_own[:, lanes].astype(F32) / norm).astype(BF16)
        unit_ref[width:, lanes] = (dec_other[:, lanes].astype(F32) / norm).astype(BF16)


def join_lanes(copies_ref, active_ref, share, k):
    for y in range(copies_ref.shape[0]):
        active_ref[y * share : (y + 1) * share, k * LANES : (k + 1) * LANES] = copies_ref[
            y, k * share : (k + 1) * share, :
        ]


def rebuild_kernel(copies_ref, unit_ref, out_ref, active_ref):
    count = unit_ref.shape[1] // LANES
    for k in range(count):
        join_lanes(copies_ref, active_ref, copies_ref.shape[1] // count, k)
    part = dot(active_ref[...], unit_ref[...], ((1,), (1,)))
    out_ref[...] = part.astype(BF16).reshape(out_ref.shape)


def keep_kernel(copies_ref, active_ref):
    count = active_ref.shape[1] // LANES
    for k in range(count):
        join_lanes(copies_ref, active_ref, copies_ref.shape[1] // count, k)


def error_kernel(blocks_ref, bias_ref, rows_ref, copies_ref):
    total = blocks_ref[0].astype(F32)
    for i in range(1, blocks_ref.shape[0]):
        total = total + blocks_ref[i].astype(F32)
    rebuilt = total + bias_ref[...]
    error = (2.0 / ROWS * (rebuilt - rows_ref[...].astype(F32))).astype(BF16)
    for i in range(copies_ref.shape[0]):
        copies_ref[i] = error


def raw_kernel(error_ref, unit_ref, out_ref):
    count = error_ref.shape[0] * error_ref.shape[1]
    error = error_ref[...].reshape(count, error_ref.shape[2])
    step = 2 * LANES
    for n in range(unit_ref.shape[1] // step):
        part = dot(error, unit_ref[:, n * step : (n + 1) * step], ((1,), (0,)))
        spread(part.astype(BF16), out_ref, 2 * n)


def grad_kernel(blocks_ref, active_ref, gate_ref, copies_ref):
    size = blocks_ref.shape[1]
    count = (copies_ref.shape[1] - size) // 2
    share = size // count
    raw = sum_blocks(blocks_ref, size)
    row = lax.broadcasted_iota(jnp.int32, (count, LANES), 0)
    dots = jnp.zeros((count, LANES), F32)
    for k in range(count):
        lines = slice(k * share, (k + 1) * share)
        grad = ((raw[lines] + 1.0 / ROWS) * gate_ref[lines, :]).astype(BF16)
        for y in range(copies_ref.shape[0]):
            copies_ref[y, lines, :] = grad
        part = jnp.sum(active_ref[lines, :].astype(F32) * raw[lines], axis=0, keepdims=True)
        dots = jnp.where(row == k, part, dots)
    high = dots.astype(BF16).astype(F32)
    parts = jnp.concatenate([high, dots - high], axis=0).astype(BF16)
    for y in range(copies_ref.shape[0]):
        copies_ref[y, size:, :] = parts


def own_kernel(own_ref, centered_ref, blocks_ref, enc_ref, sums_ref, grad_ref):
    count = enc_ref.shape[1] // LANES
    size = own_ref.shape[1] - 2 * count
    share = size // count
    for k in range(count):
        cut = pl.ds(k * LANES, LANES)
        lines = pl.ds(k * share, share)
        total = jnp.zeros((share, LANES), F32)
        for y in range(own_ref.shape[0]):
            value = own_ref[y, lines, :]
            grad_ref[pl.ds(y * share, share), cut] = value
            total = total + value.astype(F32)
        sums_ref[k : k + 1, :] = jnp.sum(total, axis=0, keepdims=True)
    sums_ref[count : 2 * count] = sum_parts(own_ref, size)
    sums_ref[2 * count :] = 1.0 / norms_of(blocks_ref, count)
    enc_ref[...] = dot(centered_ref[...], grad_ref[...], ((1,), (0,)))


def last_kernel(
    its_ref, part_ref, sums_ref, centered_ref, product_ref, unit_ref,
    enc_out, bias_out, dec_out,
    grad_ref, enc_ref, dec_ref, bias_ref, sems,
):
    count = enc_ref.shape[1] // LANES
    size = its_ref.shape[1] - 2 * count
    share = size // count
    dots = sums_ref[count : 2 * count] + sum_parts(its_ref, size)
    step = 2 * LANES
    pieces = count // 2
    copies = []

    def send(source, target, sem):
        copies.append(pltpu.make_async_copy(source, target, sems.at[sem]))
        copies[-1].start()

    for n in range(pieces):
        lanes = pl.ds(n * step, step)
        for k in (2 * n, 2 * n + 1):
            cut = pl.ds(k * LANES, LANES)
            ratio = sums_ref[2 * count + k : 2 * count + k + 1]
            dec_ref[:, cut] = (
                product_ref[:, cut] - unit_ref[:, cut].astype(F32) * dots[k : k + 1]
            ) * ratio
        send(dec_ref.at[:, lanes], dec_out.at[:, lanes], n)
    for k in range(count):
        lines = pl.ds(k * share, share)
        total = jnp.zeros((share, LANES), F32)
        for y in range(its_ref.shape[0]):
            value = its_ref[y, lines, :]
            grad_ref[pl.ds(y * share, share), pl.ds(k * LANES, LANES)] = value
            total = total + value.astype(F32)
        bias_ref[k : k + 1, :] = sums_ref[k : k + 1, :] + jnp.sum(total, axis=0, keepdims=True)
    send(bias_ref, bias_out, 2 * pieces)
    for n in range(pieces):
        lanes = pl.ds(n * step, step)
        enc_ref[:, lanes] = part_ref[:, lanes] + dot(
            centered_ref[...], grad_ref[:, lanes], ((1,), (0,))
        )
        send(enc_ref.at[:, lanes], enc_out.at[:, lanes], pieces + n)
    for copy in copies:
        copy.wait()


def body(residual, picked, enc_weight, enc_bias, dec_weight, dec_bias):
    count_y = lax.axis_size("y")
    count_t = lax.axis_size(TENSOR)
    rows = ROWS // 2
    share = rows // count_y
    piece = rows // count_t
    width, latents = enc_weight.shape
    blocks_n = latents // LANES
    size = share * blocks_n
    extra = 2 * blocks_n
    wide = 2 * width
    matmul = 2 * rows * wide * latents
    moved = 3 << 20

    small = shape((piece, wide), BF16)
    own_rows, other_rows = call(
        pick_kernel,
        (small, small),
        [HBM] * 2,
        (1 << 20, 1 << 17),
        [
            pltpu.SMEM(picked.shape, jnp.int32),
            pltpu.VMEM(residual.shape[::-1], BF16),
            pltpu.SemaphoreType.DMA((2,)),
        ],
    )(picked, residual.T)
    tensor_blocks = shape((count_t, piece, wide), BF16)
    local_rows, copies = call(join_kernel, (small, tensor_blocks), [VMEM] * 2, (1 << 12, 1 << 19))(
        own_rows, swap(other_rows)
    )
    sampled = exchange(copies, TENSOR)
    bias_all = jnp.concatenate([dec_bias[None], swap(dec_bias)[None]], axis=1)
    enc_other = swap(enc_weight)
    dec_own = dec_weight.T
    dec_other = swap(dec_own)
    squares = jnp.sum(jnp.square(dec_own.astype(F32)) + jnp.square(dec_other.astype(F32)), axis=0)
    centered = (sampled.reshape(rows, wide).astype(F32) - bias_all).astype(BF16)
    pre_blocks = call(
        pre_kernel,
        shape((count_y, size + extra, LANES), BF16),
        [VMEM] * 4,
        (matmul, moved),
        [pltpu.VMEM((wide, latents), BF16)],
    )(centered, enc_weight, enc_other, squares.reshape(blocks_n, LANES))
    blocks = exchange(pre_blocks, "y")
    enc_bias = enc_bias.reshape(blocks_n, LANES)
    copies = call(
        act_kernel, shape((count_y, size, LANES), BF16), [VMEM] * 2, (1 << 20, 1 << 20)
    )(blocks, enc_bias)
    unit, active_share, gate = call(
        unit_kernel,
        (
            shape((wide, latents), BF16),
            shape((size, LANES), BF16),
            shape((size, LANES), F32),
        ),
        [VMEM] * 4,
        (1 << 20, moved),
    )(blocks, dec_own, dec_other, enc_bias)
    copies = exchange(copies, "y")
    partial = call(
        rebuild_kernel,
        tensor_blocks,
        [VMEM] * 2,
        (matmul, moved),
        [pltpu.VMEM((rows, latents), BF16)],
    )(copies, unit)
    active = call(keep_kernel, shape((rows, latents), BF16), [VMEM], (1 << 20, 1 << 20))(copies)
    its_active = swap(active)
    turned = shape((width, rows), BF16)
    centered_own, centered_other = call(turn_kernel, (turned, turned), [VMEM], (1 << 20, 1 << 20))(
        centered
    )
    centered_its = swap(centered_other)
    errors = call(error_kernel, tensor_blocks, [VMEM] * 3, (1 << 20, 1 << 20))(
        exchange(partial, TENSOR), bias_all, local_rows
    )
    error = exchange(errors, TENSOR)
    raw_blocks = call(
        raw_kernel, shape((count_y, size, LANES), BF16), [VMEM] * 2, (matmul, moved)
    )(error, unit)
    err_grad = error.reshape(rows, wide)
    its_err = swap(err_grad[:, width:])
    product = dot(err_grad[:, :width], active, ((0,), (0,))) + dot(
        its_err, its_active, ((0,), (0,))
    )
    own = exchange(
        call(
            grad_kernel,
            shape((count_y, size + extra, LANES), BF16),
            [VMEM] * 3,
            (1 << 20, 1 << 20),
        )(exchange(raw_blocks, "y"), active_share, gate),
        "y",
    )
    its = swap(own)
    out = shape((width, latents), F32)
    enc_part, sums = call(
        own_kernel,
        (out, shape((3 * blocks_n, LANES), F32)),
        [VMEM] * 3,
        (40 * matmul, 20 * moved),
        [pltpu.VMEM((rows, latents), BF16)],
    )(own, centered_own, blocks)
    enc_grad, bias_grad, dec_grad = call(
        last_kernel,
        (out, shape((blocks_n, LANES), F32), out),
        [VMEM] * 6,
        (matmul, 2 * moved),
        [
            pltpu.VMEM((rows, latents), BF16),
            pltpu.VMEM((width, latents), F32),
            pltpu.VMEM((width, latents), F32),
            pltpu.VMEM((blocks_n, LANES), F32),
            pltpu.SemaphoreType.DMA((blocks_n + 1,)),
        ],
        (ANY, ANY, ANY),
    )(its, enc_part, sums, centered_its, product, unit[:width])
    return (enc_grad, bias_grad.reshape(latents), dec_grad.T)


def solution(mesh):
    grid = Mesh(mesh.devices.reshape(8, 2, 4, 8), ("y", "core", "x", "z"))
    dp = ("y", "core")
    return jax.shard_map(
        body,
        mesh=grid,
        in_specs=(
            P(TENSOR, dp),
            P(TENSOR),
            P(dp, TENSOR),
            P(TENSOR),
            P(TENSOR, dp),
            P(dp),
        ),
        out_specs=(P(dp, TENSOR), P(TENSOR), P(TENSOR, dp)),
        check_vma=False,
    )
```

```python
import jax
import jax.numpy as jnp
from jax import lax
from jax.experimental import pallas as pl
from jax.experimental.pallas import tpu as pltpu
from jax.sharding import Mesh
from jax.sharding import PartitionSpec as P

ROWS = 512
LANES = 128
TENSOR = ("x", "z")
F32 = jnp.float32
BF16 = jnp.bfloat16
SHARPNESS = 8.0
VMEM = pl.BlockSpec(memory_space=pltpu.VMEM)
ANY = pl.BlockSpec(memory_space=pl.ANY)
HBM = pl.BlockSpec(memory_space=pltpu.HBM)


def exchange(blocks, axis):
    return lax.all_to_all(blocks, axis, 0, 0, tiled=False)


def swap(block):
    return lax.ppermute(block, "core", [(0, 1), (1, 0)])


def dot(a, b, dims):
    return lax.dot_general(a, b, (dims, ((), ())), preferred_element_type=F32)


def call(kernel, outs, specs, cost, scratch=(), out_specs=None, limit=12):
    flops, moved = cost
    return pl.pallas_call(
        kernel,
        out_shape=outs,
        in_specs=specs,
        out_specs=jax.tree.map(lambda _: VMEM, outs) if out_specs is None else out_specs,
        scratch_shapes=list(scratch),
        compiler_params=pltpu.CompilerParams(vmem_limit_bytes=limit * 1024 * 1024),
        cost_estimate=pl.CostEstimate(flops=flops, bytes_accessed=moved, transcendentals=0),
    )


def shape(dims, kind):
    return jax.ShapeDtypeStruct(dims, kind)


def pick_kernel(picked, table, own_ref, other_ref):
    width, tokens = table.shape
    piece = own_ref.shape[0]
    core = lax.axis_index("core")
    place = lax.axis_index("x") * lax.axis_size("z") + lax.axis_index("z")
    row = lax.broadcasted_iota(jnp.int32, (piece, tokens), 0)
    token = lax.broadcasted_iota(jnp.int32, (piece, tokens), 1) + place * tokens
    columns = table[...]
    zeros = jnp.zeros_like(columns)

    def pick(start, columns):
        wanted = jnp.zeros((piece, tokens), jnp.int32)
        for i in range(piece):
            wanted = jnp.where(row == i, picked[start + i], wanted)
        hot = jnp.where(wanted == token, 1.0, 0.0).astype(BF16)
        return dot(hot, columns, ((1,), (1,))).astype(BF16)

    own_ref[...] = pick(core * piece, jnp.concatenate([columns, zeros], axis=0))
    other_ref[...] = pick((1 - core) * piece, jnp.concatenate([zeros, columns], axis=0))


def join_kernel(own_ref, got_ref, rows_ref, copies_ref):
    rows = own_ref[...] + got_ref[...]
    rows_ref[...] = rows
    for i in range(copies_ref.shape[0]):
        copies_ref[i] = rows


def turn_kernel(value_ref, own_ref, other_ref):
    turned = value_ref[...].astype(F32).T
    width = own_ref.shape[0]
    own_ref[...] = turned[:width].astype(BF16)
    other_ref[...] = turned[width:].astype(BF16)


def spread(value, out_ref, first):
    share = value.shape[0] // out_ref.shape[0]
    for y in range(out_ref.shape[0]):
        for k in range(value.shape[1] // LANES):
            out_ref[y, pl.ds((first + k) * share, share), :] = value[
                y * share : (y + 1) * share, k * LANES : (k + 1) * LANES
            ]


def pre_kernel(centered_ref, enc_own, enc_other, squares_ref, out_ref, enc_ref):
    width, latents = enc_own.shape
    step = 2 * LANES
    squares = squares_ref[...]
    high = squares.astype(BF16).astype(F32)
    parts = jnp.concatenate([high, squares - high], axis=0).astype(BF16)
    for y in range(out_ref.shape[0]):
        out_ref[y, pl.ds(out_ref.shape[1] - parts.shape[0], parts.shape[0]), :] = parts
    for n in range(latents // step):
        lanes = pl.ds(n * step, step)
        enc_ref[:width, lanes] = enc_own[:, lanes]
        enc_ref[width:, lanes] = enc_other[:, lanes]
        part = dot(centered_ref[...], enc_ref[:, lanes], ((1,), (0,)))
        spread(part.astype(BF16), out_ref, 2 * n)


def sum_blocks(blocks_ref, size):
    total = blocks_ref[0, :size, :].astype(F32)
    for y in range(1, blocks_ref.shape[0]):
        total = total + blocks_ref[y, :size, :].astype(F32)
    return total


def sum_parts(blocks_ref, size):
    total = blocks_ref[0, size:, :].astype(F32)
    for y in range(1, blocks_ref.shape[0]):
        total = total + blocks_ref[y, size:, :].astype(F32)
    half = total.shape[0] // 2
    return total[:half] + total[half:]


def soft_parts(total, bias):
    value = SHARPNESS * (total + bias)
    small = jnp.exp(-jnp.abs(value))
    soft = jnp.maximum(value, 0.0) + jnp.log1p(small)
    return value, small, (soft / SHARPNESS).astype(BF16)


def act_kernel(blocks_ref, bias_ref, copies_ref):
    size = copies_ref.shape[1]
    share = size // bias_ref.shape[0]
    total = sum_blocks(blocks_ref, size)
    for k in range(bias_ref.shape[0]):
        lines = slice(k * share, (k + 1) * share)
        _, _, active = soft_parts(total[lines], bias_ref[k : k + 1, :])
        for y in range(copies_ref.shape[0]):
            copies_ref[y, lines, :] = active


def norms_of(blocks_ref, count):
    return jnp.sqrt(sum_parts(blocks_ref, blocks_ref.shape[1] - 2 * count) + 1e-06)


def unit_kernel(blocks_ref, dec_own, dec_other, unit_ref):
    width, latents = dec_own.shape
    norms = norms_of(blocks_ref, latents // LANES)
    for k in range(latents // LANES):
        lanes = pl.ds(k * LANES, LANES)
        norm = norms[k : k + 1]
        unit_ref[:width, lanes] = (dec_own[:, lanes].astype(F32) / norm).astype(BF16)
        unit_ref[width:, lanes] = (dec_other[:, lanes].astype(F32) / norm).astype(BF16)


def join_lanes(copies_ref, active_ref, share, k):
    for y in range(copies_ref.shape[0]):
        active_ref[y * share : (y + 1) * share, k * LANES : (k + 1) * LANES] = copies_ref[
            y, k * share : (k + 1) * share, :
        ]


def rebuild_kernel(copies_ref, unit_ref, out_ref, active_ref):
    count = unit_ref.shape[1] // LANES
    for k in range(count):
        join_lanes(copies_ref, active_ref, copies_ref.shape[1] // count, k)
    part = dot(active_ref[...], unit_ref[...], ((1,), (1,)))
    out_ref[...] = part.astype(BF16).reshape(out_ref.shape)


def keep_kernel(copies_ref, active_ref):
    count = active_ref.shape[1] // LANES
    for k in range(count):
        join_lanes(copies_ref, active_ref, copies_ref.shape[1] // count, k)


def error_kernel(blocks_ref, bias_ref, rows_ref, copies_ref):
    total = blocks_ref[0].astype(F32)
    for i in range(1, blocks_ref.shape[0]):
        total = total + blocks_ref[i].astype(F32)
    rebuilt = total + bias_ref[...]
    error = (2.0 / ROWS * (rebuilt - rows_ref[...].astype(F32))).astype(BF16)
    for i in range(copies_ref.shape[0]):
        copies_ref[i] = error


def raw_kernel(error_ref, unit_ref, out_ref):
    count = error_ref.shape[0] * error_ref.shape[1]
    error = error_ref[...].reshape(count, error_ref.shape[2])
    step = 2 * LANES
    for n in range(unit_ref.shape[1] // step):
        part = dot(error, unit_ref[:, n * step : (n + 1) * step], ((1,), (0,)))
        spread(part.astype(BF16), out_ref, 2 * n)


def grad_kernel(blocks_ref, pre_ref, bias_ref, copies_ref):
    size = blocks_ref.shape[1]
    count = bias_ref.shape[0]
    share = size // count
    raw = sum_blocks(blocks_ref, size)
    pre = sum_blocks(pre_ref, size)
    row = lax.broadcasted_iota(jnp.int32, (count, LANES), 0)
    dots = jnp.zeros((count, LANES), F32)
    for k in range(count):
        lines = slice(k * share, (k + 1) * share)
        value, small, active = soft_parts(pre[lines], bias_ref[k : k + 1, :])
        gate = jnp.where(value >= 0.0, 1.0, small) / (1.0 + small)
        grad = ((raw[lines] + 1.0 / ROWS) * gate).astype(BF16)
        for y in range(copies_ref.shape[0]):
            copies_ref[y, lines, :] = grad
        part = jnp.sum(active.astype(F32) * raw[lines], axis=0, keepdims=True)
        dots = jnp.where(row == k, part, dots)
    high = dots.astype(BF16).astype(F32)
    parts = jnp.concatenate([high, dots - high], axis=0).astype(BF16)
    for y in range(copies_ref.shape[0]):
        copies_ref[y, size:, :] = parts


def own_kernel(own_ref, centered_ref, blocks_ref, enc_ref, sums_ref, grad_ref):
    count = enc_ref.shape[1] // LANES
    size = own_ref.shape[1] - 2 * count
    share = size // count
    for k in range(count):
        cut = pl.ds(k * LANES, LANES)
        lines = pl.ds(k * share, share)
        total = jnp.zeros((share, LANES), F32)
        for y in range(own_ref.shape[0]):
            value = own_ref[y, lines, :]
            grad_ref[pl.ds(y * share, share), cut] = value
            total = total + value.astype(F32)
        sums_ref[k : k + 1, :] = jnp.sum(total, axis=0, keepdims=True)
    sums_ref[count : 2 * count] = sum_parts(own_ref, size)
    sums_ref[2 * count :] = 1.0 / norms_of(blocks_ref, count)
    enc_ref[...] = dot(centered_ref[...], grad_ref[...], ((1,), (0,)))


def last_kernel(
    its_ref, part_ref, sums_ref, centered_ref, product_ref, unit_ref,
    enc_out, bias_out, dec_out,
    grad_ref, enc_ref, dec_ref, bias_ref, sems,
):
    count = enc_ref.shape[1] // LANES
    size = its_ref.shape[1] - 2 * count
    share = size // count
    dots = sums_ref[count : 2 * count] + sum_parts(its_ref, size)
    step = 2 * LANES
    pieces = count // 2
    copies = []

    def send(source, target, sem):
        copies.append(pltpu.make_async_copy(source, target, sems.at[sem]))
        copies[-1].start()

    for n in range(pieces):
        lanes = pl.ds(n * step, step)
        for k in (2 * n, 2 * n + 1):
            cut = pl.ds(k * LANES, LANES)
            ratio = sums_ref[2 * count + k : 2 * count + k + 1]
            dec_ref[:, cut] = (
                product_ref[:, cut] - unit_ref[:, cut].astype(F32) * dots[k : k + 1]
            ) * ratio
        send(dec_ref.at[:, lanes], dec_out.at[:, lanes], n)
    for k in range(count):
        lines = pl.ds(k * share, share)
        total = jnp.zeros((share, LANES), F32)
        for y in range(its_ref.shape[0]):
            value = its_ref[y, lines, :]
            grad_ref[pl.ds(y * share, share), pl.ds(k * LANES, LANES)] = value
            total = total + value.astype(F32)
        bias_ref[k : k + 1, :] = sums_ref[k : k + 1, :] + jnp.sum(total, axis=0, keepdims=True)
    send(bias_ref, bias_out, 2 * pieces)
    for n in range(pieces):
        lanes = pl.ds(n * step, step)
        enc_ref[:, lanes] = part_ref[:, lanes] + dot(
            centered_ref[...], grad_ref[:, lanes], ((1,), (0,))
        )
        send(enc_ref.at[:, lanes], enc_out.at[:, lanes], pieces + n)
    for copy in copies:
        copy.wait()


def body(residual, picked, enc_weight, enc_bias, dec_weight, dec_bias):
    count_y = lax.axis_size("y")
    count_t = lax.axis_size(TENSOR)
    rows = ROWS // 2
    share = rows // count_y
    piece = rows // count_t
    width, latents = enc_weight.shape
    blocks_n = latents // LANES
    size = share * blocks_n
    extra = 2 * blocks_n
    wide = 2 * width
    matmul = 2 * rows * wide * latents
    moved = 3 << 20

    small = shape((piece, wide), BF16)
    own_rows, other_rows = call(
        pick_kernel,
        (small, small),
        [pl.BlockSpec(memory_space=pltpu.SMEM), VMEM],
        (1 << 20, 1 << 17),
    )(picked, residual.T)
    tensor_blocks = shape((count_t, piece, wide), BF16)
    local_rows, copies = call(join_kernel, (small, tensor_blocks), [VMEM] * 2, (1 << 12, 1 << 19))(
        own_rows, swap(other_rows)
    )
    sampled = exchange(copies, TENSOR)
    bias_all = jnp.concatenate([dec_bias[None], swap(dec_bias)[None]], axis=1)
    enc_other = swap(enc_weight)
    dec_own = dec_weight.T
    dec_other = swap(dec_own)
    squares = jnp.sum(jnp.square(dec_own.astype(F32)) + jnp.square(dec_other.astype(F32)), axis=0)
    centered = (sampled.reshape(rows, wide).astype(F32) - bias_all).astype(BF16)
    pre_blocks = call(
        pre_kernel,
        shape((count_y, size + extra, LANES), BF16),
        [VMEM] * 4,
        (matmul, moved),
        [pltpu.VMEM((wide, latents), BF16)],
    )(centered, enc_weight, enc_other, squares.reshape(blocks_n, LANES))
    blocks = exchange(pre_blocks, "y")
    enc_bias = enc_bias.reshape(blocks_n, LANES)
    copies = call(
        act_kernel, shape((count_y, size, LANES), BF16), [VMEM] * 2, (1 << 20, 1 << 20)
    )(blocks, enc_bias)
    unit = call(unit_kernel, shape((wide, latents), BF16), [VMEM] * 3, (1 << 20, moved))(
        blocks, dec_own, dec_other
    )
    copies = exchange(copies, "y")
    partial = call(
        rebuild_kernel,
        tensor_blocks,
        [VMEM] * 2,
        (matmul, moved),
        [pltpu.VMEM((rows, latents), BF16)],
    )(copies, unit)
    active = call(keep_kernel, shape((rows, latents), BF16), [VMEM], (1 << 20, 1 << 20))(copies)
    its_active = swap(active)
    turned = shape((width, rows), BF16)
    centered_own, centered_other = call(turn_kernel, (turned, turned), [VMEM], (1 << 20, 1 << 20))(
        centered
    )
    centered_its = swap(centered_other)
    errors = call(error_kernel, tensor_blocks, [VMEM] * 3, (1 << 20, 1 << 20))(
        exchange(partial, TENSOR), bias_all, local_rows
    )
    error = exchange(errors, TENSOR)
    raw_blocks = call(
        raw_kernel, shape((count_y, size, LANES), BF16), [VMEM] * 2, (matmul, moved)
    )(error, unit)
    err_grad = error.reshape(rows, wide)
    its_err = swap(err_grad[:, width:])
    product = dot(err_grad[:, :width], active, ((0,), (0,))) + dot(
        its_err, its_active, ((0,), (0,))
    )
    own = exchange(
        call(
            grad_kernel,
            shape((count_y, size + extra, LANES), BF16),
            [VMEM] * 3,
            (1 << 20, 1 << 20),
        )(exchange(raw_blocks, "y"), blocks, enc_bias),
        "y",
    )
    its = swap(own)
    out = shape((width, latents), F32)
    enc_part, sums = call(
        own_kernel,
        (out, shape((3 * blocks_n, LANES), F32)),
        [VMEM] * 3,
        (40 * matmul, 20 * moved),
        [pltpu.VMEM((rows, latents), BF16)],
    )(own, centered_own, blocks)
    enc_grad, bias_grad, dec_grad = call(
        last_kernel,
        (out, shape((blocks_n, LANES), F32), out),
        [VMEM] * 6,
        (matmul, 2 * moved),
        [
            pltpu.VMEM((rows, latents), BF16),
            pltpu.VMEM((width, latents), F32),
            pltpu.VMEM((width, latents), F32),
            pltpu.VMEM((blocks_n, LANES), F32),
            pltpu.SemaphoreType.DMA((blocks_n + 1,)),
        ],
        (ANY, ANY, ANY),
    )(its, enc_part, sums, centered_its, product, unit[:width])
    return (enc_grad, bias_grad.reshape(latents), dec_grad.T)


def solution(mesh):
    grid = Mesh(mesh.devices.reshape(8, 2, 4, 8), ("y", "core", "x", "z"))
    dp = ("y", "core")
    return jax.shard_map(
        body,
        mesh=grid,
        in_specs=(
            P(TENSOR, dp),
            P(TENSOR),
            P(dp, TENSOR),
            P(TENSOR),
            P(TENSOR, dp),
            P(dp),
        ),
        out_specs=(P(dp, TENSOR), P(TENSOR), P(TENSOR, dp)),
        check_vma=False,
    )
```

```python
import jax
import jax.numpy as jnp
from jax import lax
from jax.experimental import pallas as pl
from jax.experimental.pallas import tpu as pltpu
from jax.sharding import Mesh
from jax.sharding import PartitionSpec as P

ROWS = 512
LANES = 128
TENSOR = ("x", "z")
F32 = jnp.float32
BF16 = jnp.bfloat16
SHARPNESS = 8.0
VMEM = pl.BlockSpec(memory_space=pltpu.VMEM)
ANY = pl.BlockSpec(memory_space=pl.ANY)
HBM = pl.BlockSpec(memory_space=pltpu.HBM)


def exchange(blocks, axis):
    return lax.all_to_all(blocks, axis, 0, 0, tiled=False)


def swap(block):
    return lax.ppermute(block, "core", [(0, 1), (1, 0)])


def dot(a, b, dims):
    return lax.dot_general(a, b, (dims, ((), ())), preferred_element_type=F32)


def call(kernel, outs, specs, cost, scratch=(), out_specs=None, limit=12):
    flops, moved = cost
    return pl.pallas_call(
        kernel,
        out_shape=outs,
        in_specs=specs,
        out_specs=jax.tree.map(lambda _: VMEM, outs) if out_specs is None else out_specs,
        scratch_shapes=list(scratch),
        compiler_params=pltpu.CompilerParams(vmem_limit_bytes=limit * 1024 * 1024),
        cost_estimate=pl.CostEstimate(flops=flops, bytes_accessed=moved, transcendentals=0),
    )


def shape(dims, kind):
    return jax.ShapeDtypeStruct(dims, kind)


def pick_kernel(picked_hbm, residual_hbm, own_ref, other_ref, picked, table, sems):
    width, tokens = table.shape
    piece = own_ref.shape[0]
    pairs = ((residual_hbm, table), (picked_hbm, picked))
    copies = [pltpu.make_async_copy(a, b, sems.at[i]) for i, (a, b) in enumerate(pairs)]
    for copy in copies:
        copy.start()
    for copy in copies:
        copy.wait()
    core = lax.axis_index("core")
    place = lax.axis_index("x") * lax.axis_size("z") + lax.axis_index("z")
    row = lax.broadcasted_iota(jnp.int32, (piece, tokens), 0)
    token = lax.broadcasted_iota(jnp.int32, (piece, tokens), 1) + place * tokens
    columns = table[...]
    zeros = jnp.zeros_like(columns)

    def pick(start, columns):
        wanted = jnp.zeros((piece, tokens), jnp.int32)
        for i in range(piece):
            wanted = jnp.where(row == i, picked[start + i], wanted)
        hot = jnp.where(wanted == token, 1.0, 0.0).astype(BF16)
        return dot(hot, columns, ((1,), (1,))).astype(BF16)

    own_ref[...] = pick(core * piece, jnp.concatenate([columns, zeros], axis=0))
    other_ref[...] = pick((1 - core) * piece, jnp.concatenate([zeros, columns], axis=0))


def join_kernel(own_ref, got_ref, rows_ref, copies_ref):
    rows = own_ref[...] + got_ref[...]
    rows_ref[...] = rows
    for i in range(copies_ref.shape[0]):
        copies_ref[i] = rows


def turn_kernel(value_ref, own_ref, other_ref):
    turned = value_ref[...].astype(F32).T
    width = own_ref.shape[0]
    own_ref[...] = turned[:width].astype(BF16)
    other_ref[...] = turned[width:].astype(BF16)


def spread(value, out_ref, first):
    share = value.shape[0] // out_ref.shape[0]
    for y in range(out_ref.shape[0]):
        for k in range(value.shape[1] // LANES):
            out_ref[y, pl.ds((first + k) * share, share), :] = value[
                y * share : (y + 1) * share, k * LANES : (k + 1) * LANES
            ]


def pre_kernel(centered_ref, enc_own, enc_other, squares_ref, out_ref):
    width, latents = enc_own.shape
    step = 2 * LANES
    squares = squares_ref[...]
    high = squares.astype(BF16).astype(F32)
    parts = jnp.concatenate([high, squares - high], axis=0).astype(BF16)
    for y in range(out_ref.shape[0]):
        out_ref[y, pl.ds(out_ref.shape[1] - parts.shape[0], parts.shape[0]), :] = parts
    for n in range(latents // step):
        lanes = pl.ds(n * step, step)
        part = dot(centered_ref[:, :width], enc_own[:, lanes], ((1,), (0,))) + dot(
            centered_ref[:, width:], enc_other[:, lanes], ((1,), (0,))
        )
        spread(part.astype(BF16), out_ref, 2 * n)


def sum_blocks(blocks_ref, size):
    total = blocks_ref[0, :size, :].astype(F32)
    for y in range(1, blocks_ref.shape[0]):
        total = total + blocks_ref[y, :size, :].astype(F32)
    return total


def sum_parts(blocks_ref, size):
    total = blocks_ref[0, size:, :].astype(F32)
    for y in range(1, blocks_ref.shape[0]):
        total = total + blocks_ref[y, size:, :].astype(F32)
    half = total.shape[0] // 2
    return total[:half] + total[half:]


def soft_parts(total, bias):
    value = SHARPNESS * (total + bias)
    small = jnp.exp(-jnp.abs(value))
    soft = jnp.maximum(value, 0.0) + jnp.log1p(small)
    return value, small, (soft / SHARPNESS).astype(BF16)


def act_kernel(blocks_ref, bias_ref, copies_ref):
    size = copies_ref.shape[1]
    share = size // bias_ref.shape[0]
    total = sum_blocks(blocks_ref, size)
    for k in range(bias_ref.shape[0]):
        lines = slice(k * share, (k + 1) * share)
        _, _, active = soft_parts(total[lines], bias_ref[k : k + 1, :])
        for y in range(copies_ref.shape[0]):
            copies_ref[y, lines, :] = active


def norms_of(blocks_ref, count):
    return jnp.sqrt(sum_parts(blocks_ref, blocks_ref.shape[1] - 2 * count) + 1e-06)


def unit_kernel(blocks_ref, dec_own, dec_other, unit_ref):
    width, latents = dec_own.shape
    norms = norms_of(blocks_ref, latents // LANES)
    for k in range(latents // LANES):
        lanes = pl.ds(k * LANES, LANES)
        norm = norms[k : k + 1]
        unit_ref[:width, lanes] = (dec_own[:, lanes].astype(F32) / norm).astype(BF16)
        unit_ref[width:, lanes] = (dec_other[:, lanes].astype(F32) / norm).astype(BF16)


def join_lanes(copies_ref, active_ref, share, k):
    for y in range(copies_ref.shape[0]):
        active_ref[y * share : (y + 1) * share, k * LANES : (k + 1) * LANES] = copies_ref[
            y, k * share : (k + 1) * share, :
        ]


def rebuild_kernel(copies_ref, unit_ref, out_ref, active_ref):
    count = unit_ref.shape[1] // LANES
    for k in range(count):
        join_lanes(copies_ref, active_ref, copies_ref.shape[1] // count, k)
    part = dot(active_ref[...], unit_ref[...], ((1,), (1,)))
    out_ref[...] = part.astype(BF16).reshape(out_ref.shape)


def keep_kernel(copies_ref, active_ref):
    count = active_ref.shape[1] // LANES
    for k in range(count):
        join_lanes(copies_ref, active_ref, copies_ref.shape[1] // count, k)


def error_kernel(blocks_ref, bias_ref, rows_ref, copies_ref):
    total = blocks_ref[0].astype(F32)
    for i in range(1, blocks_ref.shape[0]):
        total = total + blocks_ref[i].astype(F32)
    rebuilt = total + bias_ref[...]
    error = (2.0 / ROWS * (rebuilt - rows_ref[...].astype(F32))).astype(BF16)
    for i in range(copies_ref.shape[0]):
        copies_ref[i] = error


def raw_kernel(error_ref, unit_ref, out_ref):
    count = error_ref.shape[0] * error_ref.shape[1]
    error = error_ref[...].reshape(count, error_ref.shape[2])
    step = 2 * LANES
    for n in range(unit_ref.shape[1] // step):
        part = dot(error, unit_ref[:, n * step : (n + 1) * step], ((1,), (0,)))
        spread(part.astype(BF16), out_ref, 2 * n)


def grad_kernel(blocks_ref, pre_ref, bias_ref, copies_ref):
    size = blocks_ref.shape[1]
    count = bias_ref.shape[0]
    share = size // count
    raw = sum_blocks(blocks_ref, size)
    pre = sum_blocks(pre_ref, size)
    row = lax.broadcasted_iota(jnp.int32, (count, LANES), 0)
    dots = jnp.zeros((count, LANES), F32)
    for k in range(count):
        lines = slice(k * share, (k + 1) * share)
        value, small, active = soft_parts(pre[lines], bias_ref[k : k + 1, :])
        gate = jnp.where(value >= 0.0, 1.0, small) / (1.0 + small)
        grad = ((raw[lines] + 1.0 / ROWS) * gate).astype(BF16)
        for y in range(copies_ref.shape[0]):
            copies_ref[y, lines, :] = grad
        part = jnp.sum(active.astype(F32) * raw[lines], axis=0, keepdims=True)
        dots = jnp.where(row == k, part, dots)
    high = dots.astype(BF16).astype(F32)
    parts = jnp.concatenate([high, dots - high], axis=0).astype(BF16)
    for y in range(copies_ref.shape[0]):
        copies_ref[y, size:, :] = parts


def own_kernel(own_ref, centered_ref, blocks_ref, enc_ref, sums_ref, grad_ref):
    count = enc_ref.shape[1] // LANES
    size = own_ref.shape[1] - 2 * count
    share = size // count
    for k in range(count):
        cut = pl.ds(k * LANES, LANES)
        lines = pl.ds(k * share, share)
        total = jnp.zeros((share, LANES), F32)
        for y in range(own_ref.shape[0]):
            value = own_ref[y, lines, :]
            grad_ref[pl.ds(y * share, share), cut] = value
            total = total + value.astype(F32)
        sums_ref[k : k + 1, :] = jnp.sum(total, axis=0, keepdims=True)
    sums_ref[count : 2 * count] = sum_parts(own_ref, size)
    sums_ref[2 * count :] = 1.0 / norms_of(blocks_ref, count)
    enc_ref[...] = dot(centered_ref[...], grad_ref[...], ((1,), (0,)))


def last_kernel(
    its_ref, part_ref, sums_ref, centered_ref, product_ref, unit_ref,
    enc_out, bias_out, dec_out,
    grad_ref, enc_ref, dec_ref, bias_ref, sems,
):
    count = enc_ref.shape[1] // LANES
    size = its_ref.shape[1] - 2 * count
    share = size // count
    dots = sums_ref[count : 2 * count] + sum_parts(its_ref, size)
    step = 2 * LANES
    pieces = count // 2
    copies = []

    def send(source, target, sem):
        copies.append(pltpu.make_async_copy(source, target, sems.at[sem]))
        copies[-1].start()

    for n in range(pieces):
        lanes = pl.ds(n * step, step)
        for k in (2 * n, 2 * n + 1):
            cut = pl.ds(k * LANES, LANES)
            ratio = sums_ref[2 * count + k : 2 * count + k + 1]
            dec_ref[:, cut] = (
                product_ref[:, cut] - unit_ref[:, cut].astype(F32) * dots[k : k + 1]
            ) * ratio
        send(dec_ref.at[:, lanes], dec_out.at[:, lanes], n)
    for k in range(count):
        lines = pl.ds(k * share, share)
        total = jnp.zeros((share, LANES), F32)
        for y in range(its_ref.shape[0]):
            value = its_ref[y, lines, :]
            grad_ref[pl.ds(y * share, share), pl.ds(k * LANES, LANES)] = value
            total = total + value.astype(F32)
        bias_ref[k : k + 1, :] = sums_ref[k : k + 1, :] + jnp.sum(total, axis=0, keepdims=True)
    send(bias_ref, bias_out, 2 * pieces)
    for n in range(pieces):
        lanes = pl.ds(n * step, step)
        enc_ref[:, lanes] = part_ref[:, lanes] + dot(
            centered_ref[...], grad_ref[:, lanes], ((1,), (0,))
        )
        send(enc_ref.at[:, lanes], enc_out.at[:, lanes], pieces + n)
    for copy in copies:
        copy.wait()


def body(residual, picked, enc_weight, enc_bias, dec_weight, dec_bias):
    count_y = lax.axis_size("y")
    count_t = lax.axis_size(TENSOR)
    rows = ROWS // 2
    share = rows // count_y
    piece = rows // count_t
    width, latents = enc_weight.shape
    blocks_n = latents // LANES
    size = share * blocks_n
    extra = 2 * blocks_n
    wide = 2 * width
    matmul = 2 * rows * wide * latents
    moved = 3 << 20

    small = shape((piece, wide), BF16)
    own_rows, other_rows = call(
        pick_kernel,
        (small, small),
        [HBM] * 2,
        (1 << 20, 1 << 17),
        [
            pltpu.SMEM(picked.shape, jnp.int32),
            pltpu.VMEM(residual.shape[::-1], BF16),
            pltpu.SemaphoreType.DMA((2,)),
        ],
    )(picked, residual.T)
    tensor_blocks = shape((count_t, piece, wide), BF16)
    local_rows, copies = call(join_kernel, (small, tensor_blocks), [VMEM] * 2, (1 << 12, 1 << 19))(
        own_rows, swap(other_rows)
    )
    sampled = exchange(copies, TENSOR)
    bias_all = jnp.concatenate([dec_bias[None], swap(dec_bias)[None]], axis=1)
    enc_other = swap(enc_weight)
    dec_own = dec_weight.T
    dec_other = swap(dec_own)
    squares = jnp.sum(jnp.square(dec_own.astype(F32)) + jnp.square(dec_other.astype(F32)), axis=0)
    centered = (sampled.reshape(rows, wide).astype(F32) - bias_all).astype(BF16)
    pre_blocks = call(
        pre_kernel,
        shape((count_y, size + extra, LANES), BF16),
        [VMEM] * 4,
        (matmul, moved),
    )(centered, enc_weight, enc_other, squares.reshape(blocks_n, LANES))
    blocks = exchange(pre_blocks, "y")
    enc_bias = enc_bias.reshape(blocks_n, LANES)
    copies = call(
        act_kernel, shape((count_y, size, LANES), BF16), [VMEM] * 2, (1 << 20, 1 << 20)
    )(blocks, enc_bias)
    unit = call(unit_kernel, shape((wide, latents), BF16), [VMEM] * 3, (1 << 20, moved))(
        blocks, dec_own, dec_other
    )
    copies = exchange(copies, "y")
    partial = call(
        rebuild_kernel,
        tensor_blocks,
        [VMEM] * 2,
        (matmul, moved),
        [pltpu.VMEM((rows, latents), BF16)],
    )(copies, unit)
    active = call(keep_kernel, shape((rows, latents), BF16), [VMEM], (1 << 20, 1 << 20))(copies)
    its_active = swap(active)
    turned = shape((width, rows), BF16)
    centered_own, centered_other = call(turn_kernel, (turned, turned), [VMEM], (1 << 20, 1 << 20))(
        centered
    )
    centered_its = swap(centered_other)
    errors = call(error_kernel, tensor_blocks, [VMEM] * 3, (1 << 20, 1 << 20))(
        exchange(partial, TENSOR), bias_all, local_rows
    )
    error = exchange(errors, TENSOR)
    raw_blocks = call(
        raw_kernel, shape((count_y, size, LANES), BF16), [VMEM] * 2, (matmul, moved)
    )(error, unit)
    err_grad = error.reshape(rows, wide)
    its_err = swap(err_grad[:, width:])
    product = dot(err_grad[:, :width], active, ((0,), (0,))) + dot(
        its_err, its_active, ((0,), (0,))
    )
    own = exchange(
        call(
            grad_kernel,
            shape((count_y, size + extra, LANES), BF16),
            [VMEM] * 3,
            (1 << 20, 1 << 20),
        )(exchange(raw_blocks, "y"), blocks, enc_bias),
        "y",
    )
    its = swap(own)
    out = shape((width, latents), F32)
    enc_part, sums = call(
        own_kernel,
        (out, shape((3 * blocks_n, LANES), F32)),
        [VMEM] * 3,
        (40 * matmul, 20 * moved),
        [pltpu.VMEM((rows, latents), BF16)],
    )(own, centered_own, blocks)
    enc_grad, bias_grad, dec_grad = call(
        last_kernel,
        (out, shape((blocks_n, LANES), F32), out),
        [VMEM] * 6,
        (matmul, 2 * moved),
        [
            pltpu.VMEM((rows, latents), BF16),
            pltpu.VMEM((width, latents), F32),
            pltpu.VMEM((width, latents), F32),
            pltpu.VMEM((blocks_n, LANES), F32),
            pltpu.SemaphoreType.DMA((blocks_n + 1,)),
        ],
        (ANY, ANY, ANY),
    )(its, enc_part, sums, centered_its, product, unit[:width])
    return (enc_grad, bias_grad.reshape(latents), dec_grad.T)


def solution(mesh):
    grid = Mesh(mesh.devices.reshape(8, 2, 4, 8), ("y", "core", "x", "z"))
    dp = ("y", "core")
    return jax.shard_map(
        body,
        mesh=grid,
        in_specs=(
            P(TENSOR, dp),
            P(TENSOR),
            P(dp, TENSOR),
            P(TENSOR),
            P(TENSOR, dp),
            P(dp),
        ),
        out_specs=(P(dp, TENSOR), P(TENSOR), P(TENSOR, dp)),
        check_vma=False,
    )
```
